128 devices in a mesh: gx: 8 (over y, core), yz: 16 (over x, z).
Axes of the slice: x: 4, y: 4, z: 4, core: 2. Of those that a mesh axis runs over, the one named last changes fastest.
Arguments:
- positions: float32 [8, 16, 64, 3, 256], P('gx', 'yz'), may hold values from 0 to 1
- masses: float32 [8, 16, 64, 256], P('gx', 'yz'), may hold values from 0.002 to 0.008
- smoothing: float32 [8, 16, 64, 256], P('gx', 'yz'), may hold values from 0.35 to 0.6
- counts: int32 [8, 16, 64], P('gx', 'yz'), may hold values from 32 to 256
- pair_local: int32 [8, 16, 128], P('gx', 'yz'), may hold values from 0 to 63
- pair_side: int32 [8, 16, 128], P('gx', 'yz'), may hold values from 0 to 3
- pair_remote: int32 [8, 16, 128], P('gx', 'yz'), may hold values from 0 to 63
Outputs:
- density: float32 [8, 16, 64, 256], P('gx', 'yz')
- accel: float32 [8, 16, 64, 3, 256], P('gx', 'yz')
The draws below stay inside these ranges and needn't reach their ends.
Inputs may be any that keep to these rules, and one draw needn't show every extreme that they name: `counts`: the number of real particles of a cell; the slots from it up to 256 are padding. `pair_side`: 0 and 1 are the lower and upper neighbour along gx, 2 and 3 along yz, with wrap.
All inputs are finite; a program needn't handle non-finite values.
Results may differ from the reference program's by a relative error of at most 0.000076.
Values sent between devices are 32-bit elements; how exact they have to be, the bound alone decides.
A program may use at most 64 MiB of HBM per device.

```python
import math
import jax
import jax.numpy as jnp
from jax import lax

SLOTS = 256
CELLS_DEV = 64
PAIRS_DEV = 128
N_GX = 8
N_YZ = 16


def place_ends(array, rng, least, largest):
    dims = array.shape
    index_at = [jax.random.randint(jax.random.fold_in(rng, axis), (), 0, dims[axis]) for axis in range(len(dims))]
    array = array.at[tuple(index_at)].set(least)
    longest = dims.index(max(dims))
    index_at[longest] = (index_at[longest] + 1) % dims[longest]
    return array.at[tuple(index_at)].set(largest)


def block_scale(key, shape, shards, low, largest):
    def one(dim, blocks):
        heights = jax.random.uniform(jax.random.fold_in(jax.random.fold_in(key, 6), dim), (blocks,), jnp.float32, low / len(shards), largest / len(shards))
        return jnp.repeat(jnp.exp(heights), shape[dim] // blocks).reshape((-1,) + (1,) * (len(shape) - dim - 1))

    loudness = one(*shards[0])
    for cut in shards[1:]:
        loudness = loudness * one(*cut)
    return loudness


def setup_inputs(seed: int = 0) -> dict:
    key_list = jax.random.split(jax.random.key(seed), 8)
    return {
        "positions": jnp.clip(1.0 * jax.random.uniform(key_list[0], (N_GX, N_YZ, CELLS_DEV, 3, SLOTS), jnp.float32) ** block_scale(key_list[0], (N_GX, N_YZ, CELLS_DEV, 3, SLOTS), ((0, 8), (1, 16)), -0.2, 0.2), 0.0, 1.0),
        "masses": jnp.clip(jnp.exp(math.log(0.008) - 1.3862944 * jax.random.uniform(key_list[1], (N_GX, N_YZ, CELLS_DEV, SLOTS), jnp.float32) ** block_scale(key_list[1], (N_GX, N_YZ, CELLS_DEV, SLOTS), ((0, 8), (1, 16)), -0.2, 0.2)), 0.002, 0.008),
        "smoothing": jnp.clip(jnp.exp(math.log(0.6) - 0.5389966 * jax.random.uniform(key_list[2], (N_GX, N_YZ, CELLS_DEV, SLOTS), jnp.float32) ** block_scale(key_list[2], (N_GX, N_YZ, CELLS_DEV, SLOTS), ((0, 8), (1, 16)), -0.2, 0.2)), 0.35, 0.6),
        "counts": place_ends(jax.random.randint(key_list[3], (N_GX, N_YZ, CELLS_DEV), 32, SLOTS + 1), jax.random.fold_in(key_list[3], 1), 32, SLOTS).astype(jnp.int32),
        "pair_local": place_ends(jax.random.randint(key_list[4], (N_GX, N_YZ, PAIRS_DEV), 0, CELLS_DEV), jax.random.fold_in(key_list[4], 1), 0, CELLS_DEV - 1).astype(jnp.int32),
        "pair_side": place_ends(jax.random.randint(key_list[5], (N_GX, N_YZ, PAIRS_DEV), 0, 4), jax.random.fold_in(key_list[5], 1), 0, 3).astype(jnp.int32),
        "pair_remote": place_ends(jax.random.randint(key_list[6], (N_GX, N_YZ, PAIRS_DEV), 0, CELLS_DEV), jax.random.fold_in(key_list[6], 1), 0, CELLS_DEV - 1).astype(jnp.int32),
    }


kernel_scale = 21.0 / (16.0 * math.pi)

def kernel_parts(cell_first, cell_second):
    offset = cell_first[0:3, :, None] - cell_second[0:3, None, :]
    distance = jnp.sqrt(lax.optimization_barrier(jnp.sum(offset * offset, axis=0)))
    support = 0.5 * (cell_first[4][:, None] + cell_second[4][None, :])
    scaled = distance / support
    falloff = jnp.maximum(1.0 - 0.5 * scaled, 0.0)
    return (offset, support, scaled, falloff)

def density_tile(cell_first, cell_second):
    offset, support, scaled, falloff = kernel_parts(cell_first, cell_second)
    squared = falloff * falloff
    weight = kernel_scale / (support * support * support) * squared * squared * (1.0 + 2.0 * scaled)
    toward_first = lax.optimization_barrier(jnp.sum(weight * cell_second[3][None, :], axis=1))
    toward_second = lax.optimization_barrier(jnp.sum(weight * cell_first[3][:, None], axis=0))
    return (toward_first, toward_second)

def force_tile(cell_first, cell_second, coef_first, coef_second):
    offset, support, scaled, falloff = kernel_parts(cell_first, cell_second)
    power_five = support * support * support * support * support
    gradient = -5.0 * kernel_scale * falloff * falloff * falloff / power_five
    gradient = gradient * (coef_first[:, None] + coef_second[None, :])
    pairwise = gradient[None] * offset
    toward_first = -lax.optimization_barrier(jnp.sum(pairwise * cell_second[3][None, None, :], axis=2))
    toward_second = lax.optimization_barrier(jnp.sum(pairwise * cell_first[3][None, :, None], axis=1))
    return (toward_first, toward_second)

def blocked(evaluate, operands):
    total_rows = operands[0].shape[0]
    stride = 16 if total_rows % 16 == 0 else 8 if total_rows % 8 == 0 else 4
    shaped = tuple((member.reshape((total_rows // stride, stride) + member.shape[1:]) for member in operands))

    def run_block(bundle):
        return jax.vmap(evaluate)(*bundle)
    result = lax.map(run_block, shaped)
    return jax.tree.map(lambda member: member.reshape((total_rows,) + member.shape[2:]), result)

def density_self(cell_data):
    return density_tile(cell_data, cell_data)[0]

def force_self(cell_data, coef_data):
    return force_tile(cell_data, cell_data, coef_data, coef_data)[0]

def reference(positions, masses, smoothing, counts, pair_local, pair_side, pair_remote):
    slot_ids = jnp.arange(SLOTS, dtype=jnp.int32)
    occupied = (slot_ids[None, None, None, :] < counts[:, :, :, None]).astype(jnp.float32)
    loaded = masses * occupied
    all_cells = jnp.concatenate([positions, loaded[:, :, :, None, :], smoothing[:, :, :, None, :]], axis=3)
    row_x = jnp.broadcast_to(jnp.arange(N_GX, dtype=jnp.int32)[:, None, None], pair_side.shape)
    row_y = jnp.broadcast_to(jnp.arange(N_YZ, dtype=jnp.int32)[None, :, None], pair_side.shape)
    other_x = (row_x + jnp.where(pair_side == 0, -1, 0) + jnp.where(pair_side == 1, 1, 0)) % N_GX
    other_y = (row_y + jnp.where(pair_side == 2, -1, 0) + jnp.where(pair_side == 3, 1, 0)) % N_YZ
    first_cells = all_cells[row_x, row_y, pair_local].reshape(-1, 5, SLOTS)
    second_cells = all_cells[other_x, other_y, pair_remote].reshape(-1, 5, SLOTS)
    flat_cells = all_cells.reshape(-1, 5, SLOTS)
    pair_shape = pair_side.shape + (SLOTS,)
    self_part = blocked(density_self, (flat_cells,)).reshape(occupied.shape)
    near_first, near_second = blocked(density_tile, (first_cells, second_cells))
    density_sum = self_part.at[row_x, row_y, pair_local].add(near_first.reshape(pair_shape))
    density_sum = density_sum.at[other_x, other_y, pair_remote].add(near_second.reshape(pair_shape))
    safe_density = jnp.where(occupied > 0, density_sum, 1.0)
    pressure_coef = jnp.power(safe_density, -1.0 / 3.0) * occupied
    first_coef = pressure_coef[row_x, row_y, pair_local].reshape(-1, SLOTS)
    second_coef = pressure_coef[other_x, other_y, pair_remote].reshape(-1, SLOTS)
    vector_shape = pair_side.shape + (3, SLOTS)
    self_force = blocked(force_self, (flat_cells, pressure_coef.reshape(-1, SLOTS))).reshape(positions.shape)
    force_first, force_second = blocked(force_tile, (first_cells, second_cells, first_coef, second_coef))
    accel_sum = self_force.at[row_x, row_y, pair_local].add(force_first.reshape(vector_shape))
    accel_sum = accel_sum.at[other_x, other_y, pair_remote].add(force_second.reshape(vector_shape))
    return (density_sum * occupied, accel_sum * occupied[:, :, :, None, :])
```

```python
import math

import jax
import jax.numpy as jnp
from jax import lax
from jax.experimental import pallas as pl
from jax.experimental.pallas import tpu as pltpu
from jax.sharding import PartitionSpec as P

f32, bf16, i32 = jnp.float32, jnp.bfloat16, jnp.int32
HB = 128
CELLS = 64
PAIRS = 128
OWN = 2 * CELLS
ALL = 10 * CELLS
FEAT = 48
U = 8
U2 = 16
FRONT = 2 * U
ITEMS = 4 * PAIRS + 3 * CELLS
LIST = FRONT + ITEMS + 4 * U
DENSITY_SCALE = 21.0 * 8.0 / (16.0 * math.pi)
FORCE_SCALE = 105.0 * 32.0 / (16.0 * math.pi)
SMEM = pl.BlockSpec(memory_space=pltpu.SMEM)
VMEM = pl.BlockSpec(memory_space=pltpu.VMEM)
HBM = pl.BlockSpec(memory_space=pl.ANY)


def nn(a, b):
    return lax.dot_general(a, b, (((1,), (0,)), ((), ())), preferred_element_type=f32)


def nt(a, b):
    return lax.dot_general(a, b, (((1,), (1,)), ((), ())), preferred_element_type=f32)


def pieces(t):
    one = t.astype(bf16).astype(f32)
    rest = t - one
    two = rest.astype(bf16).astype(f32)
    return one, two, rest - two


def cell_tile(planes, cell, half):
    tile = planes[pl.ds(half * 5 * CELLS + cell, 5, stride=CELLS), :]
    return jnp.concatenate([tile, jnp.zeros((3, HB), f32)], axis=0)


def row_masks():
    row = lax.broadcasted_iota(i32, (8, HB), 0)
    return row, [(row == k).astype(f32) for k in range(8)]


def lane_features(tile, row, at):
    x = jnp.where(row < 3, tile - 0.5, 0.0)
    norm = jnp.sum(x * x, axis=0, keepdims=True)
    h = tile[4:5, :]
    dist = x + at[3] + at[4] * norm
    supp = at[5] + at[6] * h
    d1, d2, d3 = pieces(dist)
    s1, s2, s3 = pieces(supp)
    d12 = jnp.concatenate([d1, d2], axis=0).astype(bf16)
    d31 = jnp.concatenate([d3, d1], axis=0).astype(bf16)
    s12 = jnp.concatenate([s1, s2], axis=0).astype(bf16)
    s31 = jnp.concatenate([s3, s1], axis=0).astype(bf16)
    left = jnp.concatenate([d12, d12, d31], axis=0)
    right = jnp.concatenate([s12, s12, s31], axis=0)
    return jnp.concatenate([left, right], axis=1)


def row_features(tile, row, at):
    x = jnp.where(row < 3, tile - 0.5, 0.0)
    norm = jnp.sum(x * x, axis=0, keepdims=True)
    h = tile[4:5, :]
    form = -2.0 * x + at[3] * norm + at[4] + at[5] * h + at[6]
    p1, p2, p3 = pieces(form)
    natural = jnp.concatenate([p1, p1, p2, p2, p1, p3, jnp.zeros((HB - FEAT, HB), f32)], axis=0)
    return natural.T.astype(bf16)


def two_pieces(tile):
    one = tile.astype(bf16).astype(f32)
    return jnp.concatenate([one, tile - one], axis=0).astype(bf16)


def fold(o):
    o = o[:, :HB] + o[:, HB:]
    return o[:8] + o[8:]


def partner_sums(va, vb, hi, lo):
    to_lane = fold(nn(va, jnp.concatenate([hi, lo], axis=1)))
    to_row = fold(nt(vb, jnp.concatenate([hi, lo], axis=0)))
    return to_row, to_lane


def split(g):
    hi = g.astype(bf16)
    return hi, (g - hi.astype(f32)).astype(bf16)


def density_kernel(
    counts, near_counts, local, side, remote,
    own, near0, near1, near2, near3,
    dens, dens0, dens1, dens2, dens3, gbuf, src, dst, cells, info,
    flags, rowf, lanef, mass, accr, accl, dist, his, los, gs, sem,
):
    nears = (near0, near1, near2, near3)
    row, at = row_masks()

    def dummy(i):
        src[i] = 0
        dst[i] = OWN + ALL * 1024

    lax.fori_loop(0, FRONT, lambda i, c: (dummy(i), c)[1], 0)
    lax.fori_loop(0, 4 * CELLS, lambda i, c: (flags.__setitem__(i, 0), c)[1], 0)

    def put(pos, a, b, da):
        src[pos] = a + b * 1024
        dst[pos] = da + b * 1024

    def pair_items(k, carry):
        pos, seen = carry
        a = local[k]
        b = side[k] * CELLS + remote[k]
        two_a = (counts[a] > HB).astype(i32)
        two_b = (near_counts[b] > HB).astype(i32)
        a0, b0 = 2 * a, 2 * (b + CELLS)
        put(pos, a0, b0, a0)
        pos = pos + 1
        put(pos, a0, b0 + 1, a0)
        pos = pos + two_b
        put(pos, a0 + 1, b0, a0 + 1)
        pos = pos + two_a
        put(pos, a0 + 1, b0 + 1, a0 + 1)
        pos = pos + two_a * two_b
        cells[seen] = b
        seen = seen + 1 - flags[b]
        flags[b] = 1
        return pos, seen

    def self_items(a, pos):
        two = (counts[a] > HB).astype(i32)
        a0 = 2 * a
        put(pos, a0, a0, OWN)
        pos = pos + 1
        put(pos, a0, a0 + 1, a0)
        pos = pos + two
        put(pos, a0 + 1, a0 + 1, OWN)
        return pos + two

    pos = lax.fori_loop(0, CELLS, self_items, FRONT)
    pos, seen = lax.fori_loop(0, PAIRS, pair_items, (pos, 0))
    lax.fori_loop(pos, pos + 4 * U, lambda i, c: (dummy(i), c)[1], 0)
    info[0] = pos
    info[1] = seen

    accr[...] = jnp.zeros_like(accr)
    accl[...] = jnp.zeros_like(accl)
    his[...] = jnp.zeros_like(his)
    los[...] = jnp.zeros_like(los)
    dist[...] = jnp.ones_like(dist)

    def build(tile, block):
        lanef[block] = lane_features(tile, row, at)
        mass[block] = two_pieces(at[0] * tile[3:4, :])

    def own_cell(c, carry):
        for half in range(2):
            tile = cell_tile(own, c, half)
            build(tile, 2 * c + half)
            rowf[2 * c + half] = row_features(tile, row, at)[:, :FEAT]
        return carry

    lax.fori_loop(0, CELLS, own_cell, 0)

    def near_cell(k, carry):
        b = cells[k]
        which = b // CELLS
        c = b % CELLS
        for s in range(4):

            @pl.when(which == s)
            def _():
                for half in range(2):
                    build(cell_tile(nears[s], c, half), 2 * (b + CELLS) + half)

        return carry

    lax.fori_loop(0, seen, near_cell, 0)

    def save(slot, batch):
        return pltpu.make_async_copy(gs.at[slot], gbuf.at[pl.ds(batch * U, U)], sem.at[slot])

    save(0, LIST // U - 2).start()
    save(1, LIST // U - 1).start()

    def step(i, carry):
        slot = lax.rem(i, 2)
        save(slot, i).wait()
        for u in range(U):
            s = src[i * U + u]
            d = dst[i * U + u]
            to_row, to_lane = partner_sums(mass[s % 1024], mass[s // 1024], his[u], los[u])
            r0 = pl.multiple_of((d % 1024) * 8, 8)
            l0 = pl.multiple_of((d // 1024) * 8, 8)
            accr[pl.ds(r0, 8), :] += to_row
            accl[pl.ds(l0, 8), :] += to_lane
        for u in range(U):
            for c in range(0, HB, 32):
                r2 = jnp.maximum(dist[u, c : c + 32, :HB], 1e-12)
                h2 = dist[u, c : c + 32, HB:]
                r = r2 * lax.rsqrt(r2)
                q = 1.0 / h2
                q2 = q * q
                y = jnp.maximum(q - r * q2, 0.0)
                y2 = y * y
                hi, lo = split((y2 * y2) * (h2 + 4.0 * r))
                his[u, c : c + 32, :] = hi
                los[u, c : c + 32, :] = lo
                gs[slot, u, c : c + 32, :] = (y2 * y) * q2
        save(slot, i + 1).start()
        for u in range(U):
            s = src[(i + 2) * U + u]
            dist[u] = nn(rowf[s % 1024], lanef[s // 1024])
        return carry

    batches = (pos - FRONT + U - 1) // U
    lax.fori_loop(0, batches + 2, step, 0)
    for slot in range(2):
        save(slot, 0).wait()

    for g, out in enumerate((dens, dens0, dens1, dens2, dens3)):
        for half in range(2):
            for c in range(0, CELLS, 8):
                first = (2 * (g * CELLS + c) + half) * 8
                total = accl[pl.ds(first, 8, stride=16), :]
                if g == 0:
                    total = total + accr[pl.ds(first, 8, stride=16), :]
                out[half * CELLS + c : half * CELLS + c + 8, :] = total * DENSITY_SCALE


def force_kernel(
    src, dst, cells, info,
    own, near0, near1, near2, near3, coef, coef0, coef1, coef2, coef3, gbuf,
    acc, acc0, acc1, acc2, acc3,
    vmat, accr, accl, gs, sem,
):
    nears = (near0, near1, near2, near3)
    coefs = (coef0, coef1, coef2, coef3)
    row, at = row_masks()
    pos = info[0]
    seen = info[1]
    batches = (pos - FRONT + U2 - 1) // U2

    def load(slot, batch):
        return pltpu.make_async_copy(gbuf.at[pl.ds(FRONT + batch * U2, U2)], gs.at[slot], sem.at[slot])

    load(0, 0).start()

    accr[...] = jnp.zeros_like(accr)
    accl[...] = jnp.zeros_like(accl)

    def build(planes, coef_plane, c, block):
        for half in range(2):
            tile = cell_tile(planes, c, half)
            cc = coef_plane[pl.ds(half * CELLS + c, 1), :]
            m = tile[3:4, :]
            mc = m * cc
            x = tile[0:3, :] - 0.5
            stack = jnp.concatenate([m, mc, m * x, mc * x], axis=0)
            vmat[block + half] = two_pieces(stack)

    def own_cell(c, carry):
        build(own, coef, c, 2 * c)
        return carry

    lax.fori_loop(0, CELLS, own_cell, 0)

    def near_cell(k, carry):
        b = cells[k]
        which = b // CELLS
        c = b % CELLS
        for s in range(4):

            @pl.when(which == s)
            def _():
                build(nears[s], coefs[s], c, 2 * (b + CELLS))

        return carry

    lax.fori_loop(0, seen, near_cell, 0)

    def step(i, carry):
        slot = lax.rem(i, 2)

        @pl.when(i + 1 < batches)
        def _():
            load(1 - slot, i + 1).start()

        load(slot, i).wait()
        for u in range(U2):
            s = src[FRONT + i * U2 + u]
            d = dst[FRONT + i * U2 + u]
            hi, lo = split(gs[slot, u])
            to_row, to_lane = partner_sums(vmat[s % 1024], vmat[s // 1024], hi, lo)
            r0 = pl.multiple_of((d % 1024) * 8, 8)
            l0 = pl.multiple_of((d // 1024) * 8, 8)
            accr[pl.ds(r0, 8), :] += to_row
            accl[pl.ds(l0, 8), :] += to_lane
        return carry

    lax.fori_loop(0, batches, step, 0)

    planes = (own,) + nears
    for g, (out, cf) in enumerate(zip((acc, acc0, acc1, acc2, acc3), (coef,) + coefs)):
        for half in range(2):
            for c in range(0, CELLS, 8):
                first = (2 * (g * CELLS + c) + half) * 8

                def total(k):
                    t = accl[pl.ds(first + k, 8, stride=16), :]
                    if g == 0:
                        t = t + accr[pl.ds(first + k, 8, stride=16), :]
                    return t

                cc = cf[half * CELLS + c : half * CELLS + c + 8, :]
                plain = cc * total(0) + total(1)
                for k in range(3):
                    at_x = half * 5 * CELLS + k * CELLS + c
                    x = planes[g][at_x : at_x + 8, :] - 0.5
                    moment = cc * total(2 + k) + total(5 + k)
                    at_o = half * 3 * CELLS + k * CELLS + c
                    out[at_o : at_o + 8, :] = (x * plain - moment) * FORCE_SCALE


def call_density(counts, near_counts, local, side, remote, own, nears):
    plane = jax.ShapeDtypeStruct((2 * CELLS, HB), f32)
    lists = jax.ShapeDtypeStruct((LIST,), i32)
    return pl.pallas_call(
        density_kernel,
        out_shape=[plane] * 5
        + [
            jax.ShapeDtypeStruct((LIST, HB, HB), f32),
            lists,
            lists,
            jax.ShapeDtypeStruct((4 * CELLS,), i32),
            jax.ShapeDtypeStruct((8,), i32),
        ],
        in_specs=[SMEM] * 5 + [VMEM] * 5,
        out_specs=[VMEM] * 5 + [HBM] + [SMEM] * 4,
        scratch_shapes=[
            pltpu.SMEM((4 * CELLS,), i32),
            pltpu.VMEM((OWN, HB, FEAT), bf16),
            pltpu.VMEM((ALL, FEAT, 2 * HB), bf16),
            pltpu.VMEM((ALL, 16, HB), bf16),
            pltpu.VMEM(((OWN + 1) * 8, HB), f32),
            pltpu.VMEM(((ALL + 1) * 8, HB), f32),
            pltpu.VMEM((U, HB, 2 * HB), f32),
            pltpu.VMEM((U, HB, HB), bf16),
            pltpu.VMEM((U, HB, HB), bf16),
            pltpu.VMEM((2, U, HB, HB), f32),
            pltpu.SemaphoreType.DMA((2,)),
        ],
        compiler_params=pltpu.CompilerParams(vmem_limit_bytes=48 << 20),
        name="density",
    )(counts, near_counts, local, side, remote, own, *nears)


def call_force(src, dst, cells, info, own, nears, coef, near_coefs, gbuf):
    plane = jax.ShapeDtypeStruct((6 * CELLS, HB), f32)
    return pl.pallas_call(
        force_kernel,
        out_shape=[plane] * 5,
        in_specs=[SMEM] * 4 + [VMEM] * 10 + [HBM],
        out_specs=[VMEM] * 5,
        scratch_shapes=[
            pltpu.VMEM((ALL, 16, HB), bf16),
            pltpu.VMEM(((OWN + 1) * 8, HB), f32),
            pltpu.VMEM(((ALL + 1) * 8, HB), f32),
            pltpu.VMEM((2, U2, HB, HB), f32),
            pltpu.SemaphoreType.DMA((2,)),
        ],
        compiler_params=pltpu.CompilerParams(vmem_limit_bytes=48 << 20),
        name="force",
    )(src, dst, cells, info, own, *nears, coef, *near_coefs, gbuf)


def from_behind(block, axis, distance):
    size = lax.axis_size(axis)
    return lax.ppermute(block, axis, [((i - distance) % size, i) for i in range(size)])


ROUTES = (("gx", 1), ("gx", -1), ("yz", 1), ("yz", -1))


def halo(block):
    return [from_behind(block, axis, distance) for axis, distance in ROUTES]


def send_back(blocks):
    back = [from_behind(b, axis, -distance) for b, (axis, distance) in zip(blocks, ROUTES)]
    return back[0] + back[1] + back[2] + back[3]


def body(positions, masses, smoothing, counts, pair_local, pair_side, pair_remote):
    n = counts[0, 0]
    slots = lax.broadcasted_iota(i32, (CELLS, 2 * HB), 1)
    occupied = (slots < n[:, None]).astype(f32)

    def halves(x):
        return jnp.stack([x[:, :HB], x[:, HB:]])

    fields = [positions[0, 0, :, k, :] for k in range(3)]
    fields += [masses[0, 0] * occupied, smoothing[0, 0]]
    own = jnp.stack([halves(x) for x in fields], axis=1).reshape(10 * CELLS, HB)
    occ = halves(occupied).reshape(2 * CELLS, HB)
    nears = halo(own)
    near_counts = jnp.concatenate(halo(n))
    local, side, remote = pair_local[0, 0], pair_side[0, 0], pair_remote[0, 0]
    *dens, gbuf, src, dst, cells, info = call_density(n, near_counts, local, side, remote, own, nears)
    rho = dens[0] + send_back(dens[1:])
    coef = jnp.power(jnp.where(occ > 0, rho, 1.0), -1.0 / 3.0) * occ
    acc = call_force(src, dst, cells, info, own, nears, coef, halo(coef), gbuf)
    total = (acc[0] + send_back(acc[1:])).reshape(2, 3, CELLS, HB) * occ.reshape(2, 1, CELLS, HB)
    rho = (rho * occ).reshape(2, CELLS, HB)
    density = jnp.concatenate([rho[0], rho[1]], axis=-1)
    accel = jnp.concatenate([total[0], total[1]], axis=-1).transpose(1, 0, 2)
    return density[None, None], accel[None, None]


def solution(mesh):
    in_specs = (
        P("gx", "yz", None, None, None),
        P("gx", "yz", None, None),
        P("gx", "yz", None, None),
        P("gx", "yz", None),
        P("gx", "yz", None),
        P("gx", "yz", None),
        P("gx", "yz", None),
    )
    out_specs = (P("gx", "yz", None, None), P("gx", "yz", None, None, None))
    return jax.shard_map(body, mesh=mesh, in_specs=in_specs, out_specs=out_specs, check_vma=False)
```

```python
import math

import jax
import jax.numpy as jnp
from jax import lax
from jax.experimental import pallas as pl
from jax.experimental.pallas import tpu as pltpu
from jax.sharding import PartitionSpec as P

f32, bf16, i32 = jnp.float32, jnp.bfloat16, jnp.int32
HB = 128
CELLS = 64
PAIRS = 128
OWN = 2 * CELLS
ALL = 10 * CELLS
READ = 2 * (CELLS + PAIRS)
FEAT = 48
U = 16
PARTS = 4
UNROLL = 4
PLANE = 2 * CELLS
FRONT = 2 * U
ITEMS = 4 * PAIRS + 3 * CELLS
LIST = FRONT + ITEMS + 4 * U
DENSITY_SCALE = 21.0 * 8.0 / (16.0 * math.pi)
FORCE_SCALE = 105.0 * 32.0 / (16.0 * math.pi)
SMEM = pl.BlockSpec(memory_space=pltpu.SMEM)
VMEM = pl.BlockSpec(memory_space=pltpu.VMEM)
HBM = pl.BlockSpec(memory_space=pl.ANY)
MESH = pl.DeviceIdType.MESH


def nn(a, b):
    return lax.dot_general(a, b, (((1,), (0,)), ((), ())), preferred_element_type=f32)


def nt(a, b):
    return lax.dot_general(a, b, (((1,), (1,)), ((), ())), preferred_element_type=f32)


def pieces(t):
    one = t.astype(bf16).astype(f32)
    rest = t - one
    two = rest.astype(bf16).astype(f32)
    return one, two, rest - two


def cell_tile(planes, base, cell, half):
    tile = planes[pl.ds(base + half * 5 * CELLS + cell, 5, stride=CELLS), :]
    return jnp.concatenate([tile, jnp.zeros((3, HB), f32)], axis=0)


def row_masks():
    row = lax.broadcasted_iota(i32, (8, HB), 0)
    return row, [(row == k).astype(f32) for k in range(8)]


def lane_features(tile, row, at):
    x = jnp.where(row < 3, tile - 0.5, 0.0)
    norm = jnp.sum(x * x, axis=0, keepdims=True)
    h = tile[4:5, :]
    dist = x + at[3] + at[4] * norm
    supp = at[5] + at[6] * h
    d1, d2, d3 = pieces(dist)
    s1, s2, s3 = pieces(supp)
    d12 = jnp.concatenate([d1, d2], axis=0).astype(bf16)
    d31 = jnp.concatenate([d3, d1], axis=0).astype(bf16)
    s12 = jnp.concatenate([s1, s2], axis=0).astype(bf16)
    s31 = jnp.concatenate([s3, s1], axis=0).astype(bf16)
    left = jnp.concatenate([d12, d12, d31], axis=0)
    right = jnp.concatenate([s12, s12, s31], axis=0)
    return jnp.concatenate([left, right], axis=1)


def row_features(tile, row, at):
    x = jnp.where(row < 3, tile - 0.5, 0.0)
    norm = jnp.sum(x * x, axis=0, keepdims=True)
    h = tile[4:5, :]
    form = -2.0 * x + at[3] * norm + at[4] + at[5] * h + at[6]
    p1, p2, p3 = pieces(form)
    natural = jnp.concatenate([p1, p1, p2, p2, p1, p3, jnp.zeros((HB - FEAT, HB), f32)], axis=0)
    return natural.T.astype(bf16)


def two_pieces(tile):
    one = tile.astype(bf16).astype(f32)
    return jnp.concatenate([one, tile - one], axis=0).astype(bf16)


def fold(o):
    o = o[:, :HB] + o[:, HB:]
    return o[:8] + o[8:]


def partner_sums(va, vb, hi, lo):
    to_lane = fold(nn(va, jnp.concatenate([hi, lo], axis=1)))
    to_row = fold(nt(vb, jnp.concatenate([hi, lo], axis=0)))
    return to_row, to_lane


def split(g):
    hi = g.astype(bf16)
    return hi, (g - hi.astype(f32)).astype(bf16)


def batch_copies(buffer, gs, sem, slot, batch, out):
    part = U // PARTS
    copies = []
    for k in range(PARTS):
        here = gs.at[slot, pl.ds(k * part, part)]
        there = buffer.at[pl.ds(batch * U + k * part, part)]
        pair = (here, there) if out else (there, here)
        copies.append(pltpu.make_async_copy(*pair, sem.at[slot, k]))
    return copies


def density_kernel(
    counts, near_counts, local, side, remote, own, near,
    dens, near_dens, gbuf, src, dst, info,
    rowf, lanef, mass, accr, accl, dist, his, los, gs, sem,
):
    row, at = row_masks()

    def dummy(i, carry):
        src[i] = 0
        dst[i] = OWN + ALL * 1024
        return carry

    lax.fori_loop(0, FRONT, dummy, 0)

    def put(pos, a, b, da, db):
        src[pos] = a + b * 1024
        dst[pos] = da + db * 1024

    def pair_items(step, pos):
        for j in range(UNROLL):
            k = step * UNROLL + j
            a = local[k]
            two_a = (counts[a] > HB).astype(i32)
            two_b = (near_counts[side[k] * HB + remote[k]] > HB).astype(i32)
            a0, b0 = 2 * a, OWN + 2 * k
            d0 = 2 * (side[k] * CELLS + remote[k] + CELLS)
            put(pos, a0, b0, a0, d0)
            pos = pos + 1
            put(pos, a0, b0 + 1, a0, d0 + 1)
            pos = pos + two_b
            put(pos, a0 + 1, b0, a0 + 1, d0)
            pos = pos + two_a
            put(pos, a0 + 1, b0 + 1, a0 + 1, d0 + 1)
            pos = pos + two_a * two_b
        return pos

    def self_items(step, pos):
        for j in range(UNROLL):
            a = step * UNROLL + j
            two = (counts[a] > HB).astype(i32)
            a0 = 2 * a
            put(pos, a0, a0, OWN, a0)
            pos = pos + 1
            put(pos, a0, a0 + 1, a0, a0 + 1)
            pos = pos + two
            put(pos, a0 + 1, a0 + 1, OWN, a0 + 1)
            pos = pos + two
        return pos

    pos = lax.fori_loop(0, CELLS // UNROLL, self_items, FRONT)
    pos = lax.fori_loop(0, PAIRS // UNROLL, pair_items, pos)
    lax.fori_loop(pos, pos + 4 * U, dummy, 0)
    info[0] = pos

    accr[...] = jnp.zeros_like(accr)
    accl[...] = jnp.zeros_like(accl)
    his[...] = jnp.zeros_like(his)
    los[...] = jnp.zeros_like(los)
    dist[...] = jnp.ones_like(dist)

    def build(tile, block):
        lanef[block] = lane_features(tile, row, at)
        mass[block] = two_pieces(at[0] * tile[3:4, :])

    def own_cells(step, carry):
        for j in range(UNROLL):
            c = step * UNROLL + j
            for half in range(2):
                tile = cell_tile(own, 0, c, half)
                build(tile, 2 * c + half)
                rowf[2 * c + half] = row_features(tile, row, at)[:, :FEAT]
        return carry

    lax.fori_loop(0, CELLS // UNROLL, own_cells, 0)

    def near_cells(step, carry):
        for j in range(UNROLL):
            k = step * UNROLL + j
            for half in range(2):
                tile = cell_tile(near, side[k] * 10 * CELLS, remote[k], half)
                build(tile, OWN + 2 * k + half)
        return carry

    lax.fori_loop(0, PAIRS // UNROLL, near_cells, 0)

    def save(slot, batch):
        return batch_copies(gbuf, gs, sem, slot, batch, True)

    for slot in range(2):
        for copy in save(slot, LIST // U - 2 + slot):
            copy.start()

    def step(i, carry):
        slot = lax.rem(i, 2)
        for copy in save(slot, i):
            copy.wait()
        for u in range(U):
            s = src[i * U + u]
            d = dst[i * U + u]
            to_row, to_lane = partner_sums(mass[s % 1024], mass[s // 1024], his[u], los[u])
            r0 = pl.multiple_of((d % 1024) * 8, 8)
            l0 = pl.multiple_of((d // 1024) * 8, 8)
            accr[pl.ds(r0, 8), :] += to_row
            accl[pl.ds(l0, 8), :] += to_lane
        for u in range(U):
            for c in range(0, HB, 32):
                r2 = jnp.maximum(dist[u, c : c + 32, :HB], 1e-12)
                h2 = dist[u, c : c + 32, HB:]
                r = r2 * lax.rsqrt(r2)
                q = 1.0 / h2
                q2 = q * q
                y = jnp.maximum(q - r * q2, 0.0)
                y2 = y * y
                hi, lo = split((y2 * y2) * (h2 + 4.0 * r))
                his[u, c : c + 32, :] = hi
                los[u, c : c + 32, :] = lo
                gs[slot, u, c : c + 32, :] = (y2 * y) * q2
        for copy in save(slot, i + 1):
            copy.start()
        for u in range(U):
            s = src[(i + 2) * U + u]
            dist[u] = nn(rowf[s % 1024], lanef[s // 1024])
        return carry

    batches = (pos - FRONT + U - 1) // U
    lax.fori_loop(0, batches + 2, step, 0)
    for slot in range(2):
        for copy in save(slot, 0):
            copy.wait()

    for half in range(2):
        for c in range(0, CELLS, 8):
            for g in range(5):
                first = (2 * (g * CELLS + c) + half) * 8
                total = accl[pl.ds(first, 8, stride=16), :]
                if g == 0:
                    total = total + accr[pl.ds(first, 8, stride=16), :]
                    dens[half * CELLS + c : half * CELLS + c + 8, :] = total * DENSITY_SCALE
                else:
                    to = (g - 1) * PLANE + half * CELLS + c
                    near_dens[to : to + 8, :] = total * DENSITY_SCALE


def force_kernel(
    src, dst, info, side, remote, own, near, coef, near_coef, gbuf,
    acc, near_acc,
    vmat, accr, accl, gs, sem,
):
    batches = (info[0] - FRONT + U - 1) // U

    def load(slot, batch):
        return batch_copies(gbuf, gs, sem, slot, FRONT // U + batch, False)

    for copy in load(0, 0):
        copy.start()

    accr[...] = jnp.zeros_like(accr)
    accl[...] = jnp.zeros_like(accl)

    def build(planes, base, coef_planes, coef_base, c, block):
        for half in range(2):
            tile = cell_tile(planes, base, c, half)
            cc = coef_planes[pl.ds(coef_base + half * CELLS + c, 1), :]
            m = tile[3:4, :]
            mc = m * cc
            x = tile[0:3, :] - 0.5
            stack = jnp.concatenate([m, mc, m * x, mc * x], axis=0)
            vmat[block + half] = two_pieces(stack)

    def own_cells(step, carry):
        for j in range(UNROLL):
            c = step * UNROLL + j
            build(own, 0, coef, 0, c, 2 * c)
        return carry

    lax.fori_loop(0, CELLS // UNROLL, own_cells, 0)

    def near_cells(step, carry):
        for j in range(UNROLL):
            k = step * UNROLL + j
            build(near, side[k] * 10 * CELLS, near_coef, side[k] * PLANE, remote[k], OWN + 2 * k)
        return carry

    lax.fori_loop(0, PAIRS // UNROLL, near_cells, 0)

    def step(i, carry):
        slot = lax.rem(i, 2)

        @pl.when(i + 1 < batches)
        def _():
            for copy in load(1 - slot, i + 1):
                copy.start()

        for copy in load(slot, i):
            copy.wait()
        for u in range(U):
            s = src[FRONT + i * U + u]
            d = dst[FRONT + i * U + u]
            hi, lo = split(gs[slot, u])
            to_row, to_lane = partner_sums(vmat[s % 1024], vmat[s // 1024], hi, lo)
            r0 = pl.multiple_of((d % 1024) * 8, 8)
            l0 = pl.multiple_of((d // 1024) * 8, 8)
            accr[pl.ds(r0, 8), :] += to_row
            accl[pl.ds(l0, 8), :] += to_lane
        return carry

    lax.fori_loop(0, batches, step, 0)

    for g in range(5):
        planes, base = (own, 0) if g == 0 else (near, (g - 1) * 10 * CELLS)
        cf, cf_base = (coef, 0) if g == 0 else (near_coef, (g - 1) * PLANE)
        out, out_base = (acc, 0) if g == 0 else (near_acc, (g - 1) * 3 * PLANE)
        for half in range(2):
            for c in range(0, CELLS, 8):
                first = (2 * (g * CELLS + c) + half) * 8

                def total(k):
                    t = accl[pl.ds(first + k, 8, stride=16), :]
                    if g == 0:
                        t = t + accr[pl.ds(first + k, 8, stride=16), :]
                    return t

                at_c = cf_base + half * CELLS + c
                cc = cf[at_c : at_c + 8, :]
                plain = cc * total(0) + total(1)
                for k in range(3):
                    at_x = base + half * 5 * CELLS + k * CELLS + c
                    x = planes[at_x : at_x + 8, :] - 0.5
                    moment = cc * total(2 + k) + total(5 + k)
                    at_o = out_base + half * 3 * CELLS + k * CELLS + c
                    out[at_o : at_o + 8, :] = (x * plain - moment) * FORCE_SCALE


def call_density(counts, near_counts, local, side, remote, own, near):
    lists = jax.ShapeDtypeStruct((LIST,), i32)
    return pl.pallas_call(
        density_kernel,
        out_shape=[
            jax.ShapeDtypeStruct((PLANE, HB), f32),
            jax.ShapeDtypeStruct((4 * PLANE, HB), f32),
            jax.ShapeDtypeStruct((LIST, HB, HB), f32),
            lists,
            lists,
            jax.ShapeDtypeStruct((8,), i32),
        ],
        in_specs=[SMEM] * 5 + [VMEM] * 2,
        out_specs=[VMEM] * 2 + [HBM] + [SMEM] * 3,
        scratch_shapes=[
            pltpu.VMEM((OWN, HB, FEAT), bf16),
            pltpu.VMEM((READ, FEAT, 2 * HB), bf16),
            pltpu.VMEM((READ, 16, HB), bf16),
            pltpu.VMEM(((OWN + 1) * 8, HB), f32),
            pltpu.VMEM(((ALL + 1) * 8, HB), f32),
            pltpu.VMEM((U, HB, 2 * HB), f32),
            pltpu.VMEM((U, HB, HB), bf16),
            pltpu.VMEM((U, HB, HB), bf16),
            pltpu.VMEM((2, U, HB, HB), f32),
            pltpu.SemaphoreType.DMA((2, PARTS)),
        ],
        compiler_params=pltpu.CompilerParams(vmem_limit_bytes=48 << 20),
        name="density",
    )(counts, near_counts, local, side, remote, own, near)


def call_force(src, dst, info, side, remote, own, near, coef, near_coef, gbuf):
    return pl.pallas_call(
        force_kernel,
        out_shape=[
            jax.ShapeDtypeStruct((3 * PLANE, HB), f32),
            jax.ShapeDtypeStruct((12 * PLANE, HB), f32),
        ],
        in_specs=[SMEM] * 5 + [VMEM] * 4 + [HBM],
        out_specs=[VMEM] * 2,
        scratch_shapes=[
            pltpu.VMEM((READ, 16, HB), bf16),
            pltpu.VMEM(((OWN + 1) * 8, HB), f32),
            pltpu.VMEM(((ALL + 1) * 8, HB), f32),
            pltpu.VMEM((2, U, HB, HB), f32),
            pltpu.SemaphoreType.DMA((2, PARTS)),
        ],
        compiler_params=pltpu.CompilerParams(vmem_limit_bytes=48 << 20),
        name="force",
    )(src, dst, info, side, remote, own, near, coef, near_coef, gbuf)


def neighbours():
    i, j = lax.axis_index("gx"), lax.axis_index("yz")
    nx, ny = lax.axis_size("gx"), lax.axis_size("yz")
    return (
        (lax.rem(i + nx - 1, nx), j),
        (lax.rem(i + 1, nx), j),
        (i, lax.rem(j + ny - 1, ny)),
        (i, lax.rem(j + 1, ny)),
    )


def greet(devices):
    barrier = pltpu.get_barrier_semaphore()
    for device in devices:
        pl.semaphore_signal(barrier, inc=1, device_id=device, device_id_type=MESH)
    pl.semaphore_wait(barrier, 4)


def exchange(devices, source, target, send, recv):
    copies = []
    for s in (2, 3, 0, 1):
        copy = pltpu.make_async_remote_copy(
            src_ref=source(s),
            dst_ref=target(s ^ 1),
            send_sem=send.at[s],
            recv_sem=recv.at[s ^ 1],
            device_id=devices[s],
            device_id_type=MESH,
        )
        copy.start()
        copies.append(copy)
    return copies


def rows(ref, s, n):
    return ref.at[pl.ds(s * n, n), :]


def halo_kernel(own, count, near, near_count, send, recv):
    devices = neighbours()
    greet(devices)
    copies = exchange(devices, lambda s: own, lambda s: rows(near, s, 5 * PLANE), send.at[0], recv.at[0])
    copies += exchange(devices, lambda s: count, lambda s: near_count.at[s], send.at[1], recv.at[1])
    for copy in copies:
        copy.wait()


def settle_kernel(dens, near_dens, occ, rho_out, coef, near_coef, back, send, recv):
    devices = neighbours()
    greet(devices)
    copies = exchange(
        devices, lambda s: rows(near_dens, s, PLANE), lambda s: rows(back, s, PLANE), send.at[0], recv.at[0]
    )
    for copy in copies:
        copy.wait()
    rho = dens[...]
    for s in range(4):
        rho = rho + back[s * PLANE : (s + 1) * PLANE, :]
    mask = occ[...]
    rho_out[...] = rho * mask
    coef[...] = jnp.exp(jnp.log(jnp.where(mask > 0, rho, 1.0)) * (-1.0 / 3.0)) * mask
    copies = exchange(devices, lambda s: coef, lambda s: rows(near_coef, s, PLANE), send.at[1], recv.at[1])
    for copy in copies:
        copy.wait()


def finish_kernel(acc, near_acc, occ, out, back, send, recv):
    devices = neighbours()
    greet(devices)
    size = 3 * PLANE
    copies = exchange(
        devices, lambda s: rows(near_acc, s, size), lambda s: rows(back, s, size), send.at[0], recv.at[0]
    )
    for copy in copies:
        copy.wait()
    for half in range(2):
        mask = occ[half * CELLS : (half + 1) * CELLS, :]
        for k in range(3):
            at = (half * 3 + k) * CELLS
            total = acc[at : at + CELLS, :]
            for s in range(4):
                total = total + back[s * size + at : s * size + at + CELLS, :]
            out[at : at + CELLS, :] = total * mask


def remote_call(kernel, name, ident, operands, in_specs, out_shape, out_specs, scratch, phases):
    return pl.pallas_call(
        kernel,
        out_shape=out_shape,
        in_specs=in_specs,
        out_specs=out_specs,
        scratch_shapes=scratch + [pltpu.SemaphoreType.DMA((phases, 4))] * 2,
        compiler_params=pltpu.CompilerParams(collective_id=ident, has_side_effects=True),
        name=name,
    )(*operands)


def planes_of(n):
    return jax.ShapeDtypeStruct((n * PLANE, HB), f32)


def body(positions, masses, smoothing, counts, pair_local, pair_side, pair_remote):
    n = counts[0, 0]
    slots = lax.broadcasted_iota(i32, (CELLS, 2 * HB), 1)
    occupied = (slots < n[:, None]).astype(f32)

    def halves(x):
        return jnp.stack([x[:, :HB], x[:, HB:]])

    fields = [positions[0, 0, :, k, :] for k in range(3)]
    fields += [masses[0, 0] * occupied, smoothing[0, 0]]
    own = jnp.stack([halves(x) for x in fields], axis=1).reshape(5 * PLANE, HB)
    occ = halves(occupied).reshape(PLANE, HB)
    count = jnp.pad(n, (0, HB - CELLS)).reshape(1, HB)
    near, near_count = remote_call(
        halo_kernel, "halo", 0, (own, count), [HBM] * 2,
        [planes_of(20), jax.ShapeDtypeStruct((4, 1, HB), i32)], [HBM] * 2, [], 2,
    )
    local, side, remote = pair_local[0, 0], pair_side[0, 0], pair_remote[0, 0]
    dens, near_dens, gbuf, src, dst, info = call_density(
        n, near_count.reshape(4 * HB), local, side, remote, own, near
    )
    rho, coef, near_coef = remote_call(
        settle_kernel, "settle", 1, (dens, near_dens, occ), [VMEM] * 3,
        [planes_of(1), planes_of(1), planes_of(4)], [VMEM, VMEM, HBM], [pltpu.VMEM((4 * PLANE, HB), f32)], 2,
    )
    acc, near_acc = call_force(src, dst, info, side, remote, own, near, coef, near_coef, gbuf)
    total = remote_call(
        finish_kernel, "finish", 2, (acc, near_acc, occ), [VMEM] * 3,
        planes_of(3), VMEM, [pltpu.VMEM((12 * PLANE, HB), f32)], 1,
    )
    total = total.reshape(2, 3, CELLS, HB)
    rho = rho.reshape(2, CELLS, HB)
    density = jnp.concatenate([rho[0], rho[1]], axis=-1)
    accel = jnp.concatenate([total[0], total[1]], axis=-1).transpose(1, 0, 2)
    return density[None, None], accel[None, None]


def solution(mesh):
    in_specs = (
        P("gx", "yz", None, None, None),
        P("gx", "yz", None, None),
        P("gx", "yz", None, None),
        P("gx", "yz", None),
        P("gx", "yz", None),
        P("gx", "yz", None),
        P("gx", "yz", None),
    )
    out_specs = (P("gx", "yz", None, None), P("gx", "yz", None, None, None))
    return jax.shard_map(body, mesh=mesh, in_specs=in_specs, out_specs=out_specs, check_vma=False)
```

```python
import math

import jax
import jax.numpy as jnp
from jax import lax
from jax.experimental import pallas as pl
from jax.experimental.pallas import tpu as pltpu
from jax.sharding import PartitionSpec as P

f32, bf16, i32 = jnp.float32, jnp.bfloat16, jnp.int32
HB = 128
CELLS = 64
PAIRS = 128
OWN = 2 * CELLS
ALL = 10 * CELLS
READ = 2 * (CELLS + PAIRS)
FEAT = 48
U = 16
PARTS = 4
UNROLL = 4
PLANE = 2 * CELLS
PLANES = 25 * PLANE
FRONT = U
ITEMS = 4 * PAIRS + 3 * CELLS
LIST = FRONT + ITEMS + 4 * U
DENSITY_SCALE = 21.0 * 8.0 / (16.0 * math.pi)
FORCE_SCALE = 105.0 * 32.0 / (16.0 * math.pi)
SMEM = pl.BlockSpec(memory_space=pltpu.SMEM)
VMEM = pl.BlockSpec(memory_space=pltpu.VMEM)
HBM = pl.BlockSpec(memory_space=pl.ANY)
MESH = pl.DeviceIdType.MESH


def nn(a, b):
    return lax.dot_general(a, b, (((1,), (0,)), ((), ())), preferred_element_type=f32)


def nt(a, b):
    return lax.dot_general(a, b, (((1,), (1,)), ((), ())), preferred_element_type=f32)


def pieces(t):
    one = t.astype(bf16).astype(f32)
    rest = t - one
    two = rest.astype(bf16).astype(f32)
    return one, two, rest - two


def cell_tile(planes, base, cell, half):
    return planes[pl.ds(base + half * 5 * CELLS + cell, 5, stride=CELLS), :]


def masked(mass, count, half):
    slot = lax.broadcasted_iota(i32, mass.shape, 1) + half * HB
    return jnp.where(slot < count, mass, 0.0)


def masked_tile(planes, base, cell, half, count):
    tile = cell_tile(planes, base, cell, half)
    mass = masked(tile[3:4, :], count, half)
    return jnp.concatenate([tile[0:3, :], mass, tile[4:5, :], jnp.zeros((3, HB), f32)], axis=0)


def row_masks():
    row = lax.broadcasted_iota(i32, (8, HB), 0)
    return row, [(row == k).astype(f32) for k in range(8)]


def lane_features(tile, row, at):
    x = jnp.where(row < 3, tile - 0.5, 0.0)
    norm = jnp.sum(x * x, axis=0, keepdims=True)
    h = tile[4:5, :]
    dist = x + at[3] + at[4] * norm
    supp = at[5] + at[6] * h
    d1, d2, d3 = pieces(dist)
    s1, s2, s3 = pieces(supp)
    d12 = jnp.concatenate([d1, d2], axis=0).astype(bf16)
    d31 = jnp.concatenate([d3, d1], axis=0).astype(bf16)
    s12 = jnp.concatenate([s1, s2], axis=0).astype(bf16)
    s31 = jnp.concatenate([s3, s1], axis=0).astype(bf16)
    left = jnp.concatenate([d12, d12, d31], axis=0)
    right = jnp.concatenate([s12, s12, s31], axis=0)
    return jnp.concatenate([left, right], axis=1)


def row_features(tile, row, at):
    x = jnp.where(row < 3, tile - 0.5, 0.0)
    norm = jnp.sum(x * x, axis=0, keepdims=True)
    h = tile[4:5, :]
    form = -2.0 * x + at[3] * norm + at[4] + at[5] * h + at[6]
    p1, p2, p3 = pieces(form)
    rest = jnp.zeros((HB - FEAT - 8, HB), f32)
    turned = jnp.concatenate([p1, p1, p2, p2, p1, p3, tile, rest], axis=0).T
    return turned[:, :FEAT].astype(bf16), jnp.broadcast_to(turned[:, FEAT + 3 : FEAT + 4], (HB, HB))


def two_pieces(tile):
    one = tile.astype(bf16).astype(f32)
    return jnp.concatenate([one, tile - one], axis=0).astype(bf16)


def fold(o):
    o = o[:, :HB] + o[:, HB:]
    return o[:8] + o[8:]


def partner_sums(va, vb, hi, lo):
    to_lane = fold(nn(va, jnp.concatenate([hi, lo], axis=1)))
    to_row = fold(nt(vb, jnp.concatenate([hi, lo], axis=0)))
    return to_row, to_lane


def split(g):
    hi = g.astype(bf16)
    return hi, (g - hi.astype(f32)).astype(bf16)


def batch_copies(buffer, gs, sem, slot, batch, out):
    part = U // PARTS
    copies = []
    for k in range(PARTS):
        here = gs.at[slot, pl.ds(k * part, part)]
        there = buffer.at[pl.ds(batch * U + k * part, part)]
        pair = (here, there) if out else (there, here)
        copies.append(pltpu.make_async_copy(*pair, sem.at[slot, k]))
    return copies


def density_kernel(
    counts_hbm, near_counts_hbm, local_hbm, side_hbm, remote_hbm, planes_hbm,
    dens_hbm, gbuf, items_hbm,
    counts, near_counts, local, side, remote, items, planes, dens,
    rowf, lanef, massc, massr, accr, accl, dist, gs, sem, in_sem,
):
    sources = (counts_hbm, near_counts_hbm, local_hbm, side_hbm, remote_hbm, planes_hbm)
    targets = (counts, near_counts, local, side, remote, planes)
    inputs = [pltpu.make_async_copy(x, y, in_sem.at[k]) for k, (x, y) in enumerate(zip(sources, targets))]
    for copy in inputs:
        copy.start()
    for copy in inputs[:5]:
        copy.wait()
    row, at = row_masks()

    def dummy(i, carry):
        items[i] = 0
        items[LIST + i] = OWN + ALL * 1024
        return carry

    lax.fori_loop(0, FRONT, dummy, 0)

    def put(pos, a, b, da, db):
        items[pos] = a + b * 1024
        items[LIST + pos] = da + db * 1024

    def pair_items(step, pos):
        for j in range(UNROLL):
            k = step * UNROLL + j
            a = local[k]
            two_a = (counts[0, a] > HB).astype(i32)
            two_b = (near_counts[side[k], 0, remote[k]] > HB).astype(i32)
            a0, b0 = 2 * a, OWN + 2 * k
            d0 = 2 * (side[k] * CELLS + remote[k] + CELLS)
            put(pos, a0, b0, a0, d0)
            pos = pos + 1
            put(pos, a0, b0 + 1, a0, d0 + 1)
            pos = pos + two_b
            put(pos, a0 + 1, b0, a0 + 1, d0)
            pos = pos + two_a
            put(pos, a0 + 1, b0 + 1, a0 + 1, d0 + 1)
            pos = pos + two_a * two_b
        return pos

    def self_items(step, pos):
        for j in range(UNROLL):
            a = step * UNROLL + j
            two = (counts[0, a] > HB).astype(i32)
            a0 = 2 * a
            put(pos, a0, a0, OWN, a0)
            pos = pos + 1
            put(pos, a0, a0 + 1, a0, a0 + 1)
            pos = pos + two
            put(pos, a0 + 1, a0 + 1, OWN, a0 + 1)
            pos = pos + two
        return pos

    pos = lax.fori_loop(0, CELLS // UNROLL, self_items, FRONT)
    pos = lax.fori_loop(0, PAIRS // UNROLL, pair_items, pos)
    lax.fori_loop(pos, pos + 4 * U, dummy, 0)
    items[2 * LIST] = pos
    listed = pltpu.make_async_copy(items, items_hbm, in_sem.at[0])
    listed.start()

    accr[...] = jnp.zeros_like(accr)
    accl[...] = jnp.zeros_like(accl)
    dist[...] = jnp.ones_like(dist)
    inputs[5].wait()

    def build(tile, block):
        lanef[block] = lane_features(tile, row, at)
        massr[pl.ds(block, 1), :] = tile[3:4, :]

    def own_cells(step, carry):
        for j in range(2):
            c = step * 2 + j
            for half in range(2):
                tile = masked_tile(planes, 0, c, half, counts[0, c])
                build(tile, 2 * c + half)
                rowf[2 * c + half], massc[2 * c + half] = row_features(tile, row, at)
                occ = masked(jnp.ones((1, HB), f32), counts[0, c], half)
                dens[pl.ds(5 * PLANE + half * CELLS + c, 1), :] = occ
        return carry

    lax.fori_loop(0, CELLS // 2, own_cells, 0)

    def near_cells(step, carry):
        for j in range(UNROLL):
            k = step * UNROLL + j
            for half in range(2):
                count = near_counts[side[k], 0, remote[k]]
                tile = masked_tile(planes, (side[k] + 1) * 5 * PLANE, remote[k], half, count)
                build(tile, OWN + 2 * k + half)
        return carry

    lax.fori_loop(0, PAIRS // UNROLL, near_cells, 0)

    def save(slot, batch):
        return batch_copies(gbuf, gs, sem, slot, batch, True)

    for slot in range(2):
        for copy in save(slot, LIST // U - 2 + slot):
            copy.start()

    def step(i, carry):
        slot = lax.rem(i, 2)
        for copy in save(slot, i):
            copy.wait()
        for u in range(U):
            s = items[i * U + u]
            d = items[LIST + i * U + u]
            a, ra = s % 1024, d % 1024
            mq = massr[pl.ds(s // 1024, 1), :]
            down = jnp.zeros((8, HB), f32)
            for c in range(0, HB, 32):
                r2 = jnp.maximum(dist[u, c : c + 32, :HB], 1e-12)
                h2 = dist[u, c : c + 32, HB:]
                r = r2 * lax.rsqrt(r2)
                q = 1.0 / h2
                q2 = q * q
                y = jnp.maximum(q - r * q2, 0.0)
                y2 = y * y
                gs[slot, u, c : c + 32, :] = (y2 * y) * q2
                w = (y2 * y2) * (h2 + 4.0 * r)
                accr[ra, c : c + 32, :] += w * mq
                wm = w * massc[a, c : c + 32, :]
                down = down + ((wm[:8] + wm[8:16]) + (wm[16:24] + wm[24:]))
            l0 = pl.multiple_of((d // 1024) * 8, 8)
            accl[pl.ds(l0, 8), :] += down
        for copy in save(slot, i):
            copy.start()
        for u in range(U):
            s = items[(i + 1) * U + u]
            dist[u] = nn(rowf[s % 1024], lanef[s // 1024])
        return carry

    batches = (pos - FRONT + U - 1) // U
    lax.fori_loop(0, batches + 1, step, 0)

    row16 = lax.broadcasted_iota(i32, (16, HB), 0)
    for half in range(2):

        def own_sums(c8, carry):
            first = (2 * c8 * 8 + half) * 8
            total = jnp.zeros((16, 2 * HB), f32)
            for j in range(8):
                hi, lo = split(accr[2 * (c8 * 8 + j) + half])
                pick = (row16 == j).astype(bf16)
                total = total + nt(pick, jnp.concatenate([hi, lo], axis=0))
            rows8 = total[:8, :HB] + total[:8, HB:]
            for k in range(8):
                rows8 = rows8 + accl[pl.ds(first + k, 8, stride=16), :]
            to = pl.multiple_of(half * CELLS + c8 * 8, 8)
            dens[pl.ds(to, 8), :] = rows8 * DENSITY_SCALE
            return carry

        lax.fori_loop(0, CELLS // 8, own_sums, 0)

        def near_sums(c8, carry):
            for g in range(1, 5):
                first = (2 * (g * CELLS + c8 * 8) + half) * 8
                rows8 = accl[pl.ds(first, 8, stride=16), :]
                for k in range(1, 8):
                    rows8 = rows8 + accl[pl.ds(first + k, 8, stride=16), :]
                to = pl.multiple_of(g * PLANE + half * CELLS + c8 * 8, 8)
                dens[pl.ds(to, 8), :] = rows8 * DENSITY_SCALE
            return carry

        lax.fori_loop(0, CELLS // 8, near_sums, 0)

    out = pltpu.make_async_copy(dens, dens_hbm, in_sem.at[1])
    out.start()
    listed.wait()
    for slot in range(2):
        for copy in save(slot, 0):
            copy.wait()
    out.wait()


def force_kernel(
    items_hbm, counts_hbm, near_counts_hbm, side_hbm, remote_hbm, planes_hbm, coef_hbm, gbuf,
    acc_hbm,
    items, counts, near_counts, side, remote, planes, coef, acc,
    vmat, accr, accl, gs, sem, in_sem,
):
    sources = (items_hbm, counts_hbm, near_counts_hbm, side_hbm, remote_hbm, planes_hbm, coef_hbm)
    targets = (items, counts, near_counts, side, remote, planes, coef)
    inputs = [pltpu.make_async_copy(x, y, in_sem.at[k]) for k, (x, y) in enumerate(zip(sources, targets))]
    for copy in inputs:
        copy.start()

    def load(slot, batch):
        return batch_copies(gbuf, gs, sem, slot, FRONT // U + batch, False)

    for copy in load(0, 0):
        copy.start()
    for copy in inputs:
        copy.wait()
    batches = (items[2 * LIST] - FRONT + U - 1) // U

    accr[...] = jnp.zeros_like(accr)
    accl[...] = jnp.zeros_like(accl)

    def build(group, c, count, block):
        for half in range(2):
            tile = cell_tile(planes, group * 5 * PLANE, c, half)
            cc = coef[pl.ds(group * PLANE + half * CELLS + c, 1), :]
            m = masked(tile[3:4, :], count, half)
            mc = m * cc
            x = tile[0:3, :] - 0.5
            stack = jnp.concatenate([m, mc, m * x, mc * x], axis=0)
            vmat[block + half] = two_pieces(stack)

    def own_cells(step, carry):
        for j in range(UNROLL):
            c = step * UNROLL + j
            build(0, c, counts[0, c], 2 * c)
        return carry

    lax.fori_loop(0, CELLS // UNROLL, own_cells, 0)

    def near_cells(step, carry):
        for j in range(UNROLL):
            k = step * UNROLL + j
            build(side[k] + 1, remote[k], near_counts[side[k], 0, remote[k]], OWN + 2 * k)
        return carry

    lax.fori_loop(0, PAIRS // UNROLL, near_cells, 0)

    def step(i, carry):
        slot = lax.rem(i, 2)

        @pl.when(i + 1 < batches)
        def _():
            for copy in load(1 - slot, i + 1):
                copy.start()

        for copy in load(slot, i):
            copy.wait()
        for u in range(U):
            s = items[FRONT + i * U + u]
            d = items[LIST + FRONT + i * U + u]
            hi, lo = split(gs[slot, u])
            to_row, to_lane = partner_sums(vmat[s % 1024], vmat[s // 1024], hi, lo)
            r0 = pl.multiple_of((d % 1024) * 8, 8)
            l0 = pl.multiple_of((d // 1024) * 8, 8)
            accr[pl.ds(r0, 8), :] += to_row
            accl[pl.ds(l0, 8), :] += to_lane
        return carry

    lax.fori_loop(0, batches, step, 0)

    for half in range(2):

        def sums(c8, carry):
            for g in range(5):
                first = (2 * (g * CELLS + c8 * 8) + half) * 8

                def total(k):
                    t = accl[pl.ds(first + k, 8, stride=16), :]
                    if g == 0:
                        t = t + accr[pl.ds(first + k, 8, stride=16), :]
                    return t

                cc = coef[pl.ds(pl.multiple_of(g * PLANE + half * CELLS + c8 * 8, 8), 8), :]
                plain = cc * total(0) + total(1)
                for k in range(3):
                    at_x = pl.multiple_of(((g * 2 + half) * 5 + k) * CELLS + c8 * 8, 8)
                    x = planes[pl.ds(at_x, 8), :] - 0.5
                    moment = cc * total(2 + k) + total(5 + k)
                    at_o = pl.multiple_of(((g * 2 + half) * 3 + k) * CELLS + c8 * 8, 8)
                    acc[pl.ds(at_o, 8), :] = (x * plain - moment) * FORCE_SCALE
            return carry

        lax.fori_loop(0, CELLS // 8, sums, 0)

    out = pltpu.make_async_copy(acc, acc_hbm, in_sem.at[0])
    out.start()
    out.wait()


def planes_of(n):
    return jax.ShapeDtypeStruct((n * PLANE, HB), f32)


def call_density(counts, near_counts, local, side, remote, planes):
    return pl.pallas_call(
        density_kernel,
        out_shape=[
            planes_of(6),
            jax.ShapeDtypeStruct((LIST, HB, HB), f32),
            jax.ShapeDtypeStruct((2 * LIST + 8,), i32),
        ],
        in_specs=[HBM] * 6,
        out_specs=[HBM] * 3,
        scratch_shapes=[
            pltpu.SMEM((1, CELLS), i32),
            pltpu.SMEM((4, 1, CELLS), i32),
            pltpu.SMEM((PAIRS,), i32),
            pltpu.SMEM((PAIRS,), i32),
            pltpu.SMEM((PAIRS,), i32),
            pltpu.SMEM((2 * LIST + 8,), i32),
            pltpu.VMEM((PLANES, HB), f32),
            pltpu.VMEM((6 * PLANE, HB), f32),
            pltpu.VMEM((OWN, HB, FEAT), bf16),
            pltpu.VMEM((READ, FEAT, 2 * HB), bf16),
            pltpu.VMEM((OWN, HB, HB), f32),
            pltpu.VMEM((READ, HB), f32),
            pltpu.VMEM((OWN + 1, HB, HB), f32),
            pltpu.VMEM(((ALL + 1) * 8, HB), f32),
            pltpu.VMEM((U, HB, 2 * HB), f32),
            pltpu.VMEM((2, U, HB, HB), f32),
            pltpu.SemaphoreType.DMA((2, PARTS)),
            pltpu.SemaphoreType.DMA((6,)),
        ],
        compiler_params=pltpu.CompilerParams(vmem_limit_bytes=60 << 20),
        name="density",
    )(counts, near_counts, local, side, remote, planes)


def call_force(items, counts, near_counts, side, remote, planes, coef, gbuf):
    return pl.pallas_call(
        force_kernel,
        out_shape=planes_of(15),
        in_specs=[HBM] * 8,
        out_specs=HBM,
        scratch_shapes=[
            pltpu.SMEM((2 * LIST + 8,), i32),
            pltpu.SMEM((1, CELLS), i32),
            pltpu.SMEM((4, 1, CELLS), i32),
            pltpu.SMEM((PAIRS,), i32),
            pltpu.SMEM((PAIRS,), i32),
            pltpu.VMEM((PLANES, HB), f32),
            pltpu.VMEM((5 * PLANE, HB), f32),
            pltpu.VMEM((15 * PLANE, HB), f32),
            pltpu.VMEM((READ, 16, HB), bf16),
            pltpu.VMEM(((OWN + 1) * 8, HB), f32),
            pltpu.VMEM(((ALL + 1) * 8, HB), f32),
            pltpu.VMEM((2, U, HB, HB), f32),
            pltpu.SemaphoreType.DMA((2, PARTS)),
            pltpu.SemaphoreType.DMA((7,)),
        ],
        compiler_params=pltpu.CompilerParams(vmem_limit_bytes=60 << 20),
        name="force",
    )(items, counts, near_counts, side, remote, planes, coef, gbuf)


def neighbours():
    i, j = lax.axis_index("gx"), lax.axis_index("yz")
    nx, ny = lax.axis_size("gx"), lax.axis_size("yz")
    return (
        (lax.rem(i + nx - 1, nx), j),
        (lax.rem(i + 1, nx), j),
        (i, lax.rem(j + ny - 1, ny)),
        (i, lax.rem(j + 1, ny)),
    )


def greet(devices):
    barrier = pltpu.get_barrier_semaphore()
    for device in devices:
        pl.semaphore_signal(barrier, inc=1, device_id=device, device_id_type=MESH)
    pl.semaphore_wait(barrier, 4)


def exchange(devices, source, target, send, recv):
    copies = []
    for s in (2, 3, 0, 1):
        copy = pltpu.make_async_remote_copy(
            src_ref=source(s),
            dst_ref=target(s ^ 1),
            send_sem=send.at[s],
            recv_sem=recv.at[s ^ 1],
            device_id=devices[s],
            device_id_type=MESH,
        )
        copy.start()
        copies.append(copy)
    return copies


def rows(ref, s, n):
    return ref.at[pl.ds(s * n, n), :]


def halo_kernel(
    positions, masses, smoothing, count,
    planes, near_count,
    pos, mass, smooth, own, in_sem, send, recv,
):
    devices = neighbours()
    sources, targets = (positions, masses, smoothing), (pos, mass, smooth)
    inputs = [pltpu.make_async_copy(x, y, in_sem.at[k]) for k, (x, y) in enumerate(zip(sources, targets))]
    for copy in inputs:
        copy.start()
    greet(devices)
    copies = exchange(devices, lambda s: count, lambda s: near_count.at[s], send.at[1], recv.at[1])
    for copy in inputs:
        copy.wait()
    for half in range(2):
        lanes = slice(half * HB, (half + 1) * HB)
        base = half * 5 * CELLS
        for k in range(3):
            own[base + k * CELLS : base + (k + 1) * CELLS, :] = pos[k, :, lanes]
        own[base + 3 * CELLS : base + 4 * CELLS, :] = mass[:, lanes]
        own[base + 4 * CELLS : base + 5 * CELLS, :] = smooth[:, lanes]
    copies += exchange(
        devices, lambda s: own, lambda s: rows(planes, s + 1, 5 * PLANE), send.at[0], recv.at[0]
    )
    keep = pltpu.make_async_copy(own, rows(planes, 0, 5 * PLANE), in_sem.at[3])
    keep.start()
    for copy in copies:
        copy.wait()
    keep.wait()


def settle_kernel(dens, rho_out, coef, mine, occ, cf, back, in_sem, send, recv):
    devices = neighbours()
    inputs = [
        pltpu.make_async_copy(rows(dens, 0, PLANE), mine, in_sem.at[0]),
        pltpu.make_async_copy(rows(dens, 5, PLANE), occ, in_sem.at[1]),
    ]
    for copy in inputs:
        copy.start()
    greet(devices)
    copies = exchange(
        devices, lambda s: rows(dens, s + 1, PLANE), lambda s: rows(back, s, PLANE), send.at[0], recv.at[0]
    )
    for copy in inputs + copies:
        copy.wait()
    rho = mine[...]
    for s in range(4):
        rho = rho + back[s * PLANE : (s + 1) * PLANE, :]
    mask = occ[...]
    cf[...] = jnp.exp(jnp.log(jnp.where(mask > 0, rho, 1.0)) * (-1.0 / 3.0)) * mask
    copies = exchange(devices, lambda s: cf, lambda s: rows(coef, s + 1, PLANE), send.at[1], recv.at[1])
    keep = pltpu.make_async_copy(cf, rows(coef, 0, PLANE), in_sem.at[0])
    keep.start()
    rho = rho * mask
    for half in range(2):
        rho_out[:, half * HB : (half + 1) * HB] = rho[half * CELLS : (half + 1) * CELLS]
    for copy in copies:
        copy.wait()
    keep.wait()


def finish_kernel(acc, dens, out, mine, occ, back, in_sem, send, recv):
    devices = neighbours()
    size = 3 * PLANE
    inputs = [
        pltpu.make_async_copy(rows(acc, 0, size), mine, in_sem.at[0]),
        pltpu.make_async_copy(rows(dens, 5, PLANE), occ, in_sem.at[1]),
    ]
    for copy in inputs:
        copy.start()
    greet(devices)
    copies = exchange(
        devices, lambda s: rows(acc, s + 1, size), lambda s: rows(back, s, size), send.at[0], recv.at[0]
    )
    for copy in inputs + copies:
        copy.wait()
    for half in range(2):
        mask = occ[half * CELLS : (half + 1) * CELLS, :]
        for k in range(3):
            at = (half * 3 + k) * CELLS
            total = mine[at : at + CELLS, :]
            for s in range(4):
                total = total + back[s * size + at : s * size + at + CELLS, :]
            out[k, :, half * HB : (half + 1) * HB] = total * mask


def remote_call(kernel, name, ident, operands, out_shape, out_specs, scratch, copies, phases):
    return pl.pallas_call(
        kernel,
        out_shape=out_shape,
        in_specs=[HBM] * len(operands),
        out_specs=out_specs,
        scratch_shapes=[pltpu.VMEM(shape, f32) for shape in scratch]
        + [pltpu.SemaphoreType.DMA((copies,))]
        + [pltpu.SemaphoreType.DMA((phases, 4))] * 2,
        compiler_params=pltpu.CompilerParams(collective_id=ident, has_side_effects=True, vmem_limit_bytes=60 << 20),
        name=name,
    )(*operands)


def body(positions, masses, smoothing, counts, pair_local, pair_side, pair_remote):
    count = counts.reshape(1, CELLS)
    local, side, remote = (x.reshape(PAIRS) for x in (pair_local, pair_side, pair_remote))
    slots = 2 * HB
    planes, near_count = remote_call(
        halo_kernel, "halo", 0, (positions[0, 0].transpose(1, 0, 2), masses[0, 0], smoothing[0, 0], count),
        [planes_of(25), jax.ShapeDtypeStruct((4, 1, CELLS), i32)], [HBM] * 2,
        [(3, CELLS, slots), (CELLS, slots), (CELLS, slots), (5 * PLANE, HB)], 4, 2,
    )
    dens, gbuf, items = call_density(count, near_count, local, side, remote, planes)
    rho, coef = remote_call(
        settle_kernel, "settle", 1, (dens,),
        [jax.ShapeDtypeStruct((CELLS, slots), f32), planes_of(5)], [VMEM, HBM],
        [(PLANE, HB), (PLANE, HB), (PLANE, HB), (4 * PLANE, HB)], 2, 2,
    )
    acc = call_force(items, count, near_count, side, remote, planes, coef, gbuf)
    accel = remote_call(
        finish_kernel, "finish", 2, (acc, dens),
        jax.ShapeDtypeStruct((3, CELLS, slots), f32), VMEM,
        [(3 * PLANE, HB), (PLANE, HB), (12 * PLANE, HB)], 2, 1,
    )
    return rho[None, None], accel.transpose(1, 0, 2)[None, None]


def solution(mesh):
    in_specs = (
        P("gx", "yz", None, None, None),
        P("gx", "yz", None, None),
        P("gx", "yz", None, None),
        P("gx", "yz", None),
        P("gx", "yz", None),
        P("gx", "yz", None),
        P("gx", "yz", None),
    )
    out_specs = (P("gx", "yz", None, None), P("gx", "yz", None, None, None))
    return jax.shard_map(body, mesh=mesh, in_specs=in_specs, out_specs=out_specs, check_vma=False)
```

```python
import math

import jax
import jax.numpy as jnp
from jax import lax
from jax.experimental import pallas as pl
from jax.experimental.pallas import tpu as pltpu
from jax.sharding import PartitionSpec as P

f32, bf16, i32 = jnp.float32, jnp.bfloat16, jnp.int32
HB = 128
CELLS = 64
PAIRS = 128
OWN = 2 * CELLS
ALL = 10 * CELLS
READ = 2 * (CELLS + PAIRS)
FEAT = 48
U = 16
PARTS = 4
SLOTS = 4
UNROLL = 4
PLANE = 2 * CELLS
PLANES = 25 * PLANE
FRONT = U
ITEMS = 4 * PAIRS + 3 * CELLS
LIST = FRONT + ITEMS + (SLOTS + 3) * U
DENSITY_SCALE = 21.0 * 8.0 / (16.0 * math.pi)
FORCE_SCALE = 105.0 * 32.0 / (16.0 * math.pi)
SMEM = pl.BlockSpec(memory_space=pltpu.SMEM)
VMEM = pl.BlockSpec(memory_space=pltpu.VMEM)
HBM = pl.BlockSpec(memory_space=pl.ANY)
MESH = pl.DeviceIdType.MESH


def nn(a, b):
    return lax.dot_general(a, b, (((1,), (0,)), ((), ())), preferred_element_type=f32)


def nt(a, b):
    return lax.dot_general(a, b, (((1,), (1,)), ((), ())), preferred_element_type=f32)


def pieces(t):
    one = t.astype(bf16).astype(f32)
    rest = t - one
    two = rest.astype(bf16).astype(f32)
    return one, two, rest - two


def cell_tile(planes, base, cell, half):
    return planes[pl.ds(base + half * 5 * CELLS + cell, 5, stride=CELLS), :]


def masked(mass, count, half):
    slot = lax.broadcasted_iota(i32, mass.shape, 1) + half * HB
    return jnp.where(slot < count, mass, 0.0)


def masked_tile(planes, base, cell, half, count):
    tile = cell_tile(planes, base, cell, half)
    mass = masked(tile[3:4, :], count, half)
    return jnp.concatenate([tile[0:3, :], mass, tile[4:5, :], jnp.zeros((3, HB), f32)], axis=0)


def row_masks():
    row = lax.broadcasted_iota(i32, (8, HB), 0)
    return row, [(row == k).astype(f32) for k in range(8)]


def lane_features(tile, row, at):
    x = jnp.where(row < 3, tile - 0.5, 0.0)
    norm = jnp.sum(x * x, axis=0, keepdims=True)
    h = tile[4:5, :]
    dist = x + at[3] + at[4] * norm
    supp = at[5] + at[6] * h
    d1, d2, d3 = pieces(dist)
    s1, s2, s3 = pieces(supp)
    d12 = jnp.concatenate([d1, d2], axis=0).astype(bf16)
    d31 = jnp.concatenate([d3, d1], axis=0).astype(bf16)
    s12 = jnp.concatenate([s1, s2], axis=0).astype(bf16)
    s31 = jnp.concatenate([s3, s1], axis=0).astype(bf16)
    left = jnp.concatenate([d12, d12, d31], axis=0)
    right = jnp.concatenate([s12, s12, s31], axis=0)
    return jnp.concatenate([left, right], axis=1)


def row_features(tile, row, at):
    x = jnp.where(row < 3, tile - 0.5, 0.0)
    norm = jnp.sum(x * x, axis=0, keepdims=True)
    h = tile[4:5, :]
    form = -2.0 * x + at[3] * norm + at[4] + at[5] * h + at[6]
    p1, p2, p3 = pieces(form)
    rest = jnp.zeros((HB - FEAT - 8, HB), f32)
    m1, m2, m3 = pieces(at[0] * tile[3:4, :])
    masses = m1 + pltpu.roll(m2, 1, 0) + pltpu.roll(m3, 2, 0)
    rest = jnp.zeros((64 - FEAT - 8, HB), f32)
    turned = jnp.concatenate([p1, p1, p2, p2, p1, p3, masses, rest], axis=0).T.astype(bf16)
    k = lax.broadcasted_iota(i32, (64, HB), 0)
    pick = ((k >= FEAT) & (k < FEAT + 3)).astype(f32).astype(bf16)
    return turned[:, :FEAT], nn(turned, pick)


def two_pieces(tile):
    one = tile.astype(bf16).astype(f32)
    return jnp.concatenate([one, tile - one], axis=0).astype(bf16)


def fold(o):
    o = o[:, :HB] + o[:, HB:]
    return o[:8] + o[8:]


def partner_sums(va, vb, hi, lo):
    to_lane = fold(nn(va, jnp.concatenate([hi, lo], axis=1)))
    to_row = fold(nt(vb, jnp.concatenate([hi, lo], axis=0)))
    return to_row, to_lane


def split(g):
    hi = g.astype(bf16)
    return hi, (g - hi.astype(f32)).astype(bf16)


def batch_copies(buffer, gs, sem, slot, batch, out):
    part = U // PARTS
    copies = []
    for k in range(PARTS):
        here = gs.at[slot, pl.ds(k * part, part)]
        there = buffer.at[pl.ds(batch * U + k * part, part)]
        pair = (here, there) if out else (there, here)
        copies.append(pltpu.make_async_copy(*pair, sem.at[slot, k]))
    return copies


def density_kernel(
    counts_hbm, near_counts_hbm, local_hbm, side_hbm, remote_hbm, planes_hbm,
    dens_hbm, gbuf, items_hbm,
    counts, near_counts, local, side, remote, items, planes, dens,
    rowf, lanef, massc, massr, accr, accl, dist, gs, sem, in_sem,
):
    sources = (counts_hbm, near_counts_hbm, local_hbm, side_hbm, remote_hbm, planes_hbm)
    targets = (counts, near_counts, local, side, remote, planes)
    inputs = [pltpu.make_async_copy(x, y, in_sem.at[k]) for k, (x, y) in enumerate(zip(sources, targets))]
    for copy in inputs:
        copy.start()
    for copy in inputs[:5]:
        copy.wait()
    row, at = row_masks()

    def dummy(i, carry):
        items[i] = 0
        items[LIST + i] = OWN + ALL * 1024
        return carry

    lax.fori_loop(0, FRONT, dummy, 0)

    def put(pos, a, b, da, db):
        items[pos] = a + b * 1024
        items[LIST + pos] = da + db * 1024

    def pair_items(step, pos):
        for j in range(UNROLL):
            k = step * UNROLL + j
            a = local[k]
            two_a = (counts[0, a] > HB).astype(i32)
            two_b = (near_counts[side[k], 0, remote[k]] > HB).astype(i32)
            a0, b0 = 2 * a, OWN + 2 * k
            d0 = 2 * (side[k] * CELLS + remote[k] + CELLS)
            put(pos, a0, b0, a0, d0)
            pos = pos + 1
            put(pos, a0, b0 + 1, a0, d0 + 1)
            pos = pos + two_b
            put(pos, a0 + 1, b0, a0 + 1, d0)
            pos = pos + two_a
            put(pos, a0 + 1, b0 + 1, a0 + 1, d0 + 1)
            pos = pos + two_a * two_b
        return pos

    def self_items(step, pos):
        for j in range(UNROLL):
            a = step * UNROLL + j
            two = (counts[0, a] > HB).astype(i32)
            a0 = 2 * a
            put(pos, a0, a0, OWN, a0)
            pos = pos + 1
            put(pos, a0, a0 + 1, a0, a0 + 1)
            pos = pos + two
            put(pos, a0 + 1, a0 + 1, OWN, a0 + 1)
            pos = pos + two
        return pos

    pos = lax.fori_loop(0, CELLS // UNROLL, self_items, FRONT)
    pos = lax.fori_loop(0, PAIRS // UNROLL, pair_items, pos)
    lax.fori_loop(pos, pos + 4 * U, dummy, 0)
    items[2 * LIST] = pos
    listed = pltpu.make_async_copy(items, items_hbm, in_sem.at[0])
    listed.start()

    accr[...] = jnp.zeros_like(accr)
    accl[...] = jnp.zeros_like(accl)
    dist[...] = jnp.ones_like(dist)
    inputs[5].wait()

    def build(tile, block):
        lanef[block] = lane_features(tile, row, at)
        massr[pl.ds(block, 1), :] = tile[3:4, :]

    def own_cells(step, carry):
        for j in range(4):
            c = step * 4 + j
            for half in range(2):
                tile = masked_tile(planes, 0, c, half, counts[0, c])
                build(tile, 2 * c + half)
                rowf[2 * c + half], massc[2 * c + half] = row_features(tile, row, at)
                occ = masked(jnp.ones((1, HB), f32), counts[0, c], half)
                dens[pl.ds(5 * PLANE + half * CELLS + c, 1), :] = occ
        return carry

    lax.fori_loop(0, CELLS // 4, own_cells, 0)

    def near_cells(step, carry):
        for j in range(UNROLL):
            k = step * UNROLL + j
            for half in range(2):
                count = near_counts[side[k], 0, remote[k]]
                tile = masked_tile(planes, (side[k] + 1) * 5 * PLANE, remote[k], half, count)
                build(tile, OWN + 2 * k + half)
        return carry

    lax.fori_loop(0, PAIRS // UNROLL, near_cells, 0)

    def save(slot, batch):
        return batch_copies(gbuf, gs, sem, slot, batch, True)

    for slot in range(SLOTS):
        for copy in save(slot, LIST // U - SLOTS + slot):
            copy.start()

    def step(i, carry):
        slot = lax.rem(i, SLOTS)
        for copy in save(slot, i):
            copy.wait()
        for u in range(U):
            s = items[i * U + u]
            d = items[LIST + i * U + u]
            a, ra = s % 1024, d % 1024
            mq = massr[pl.ds(s // 1024, 1), :]
            down = jnp.zeros((8, HB), f32)
            for c in range(0, HB, 32):
                r2 = jnp.maximum(dist[u, c : c + 32, :HB], 1e-12)
                h2 = dist[u, c : c + 32, HB:]
                r = r2 * lax.rsqrt(r2)
                q = 1.0 / h2
                q2 = q * q
                y = jnp.maximum(q - r * q2, 0.0)
                y2 = y * y
                gs[slot, u, c : c + 32, :] = (y2 * y) * q2
                w = (y2 * y2) * (h2 + 4.0 * r)
                accr[ra, c : c + 32, :] += w * mq
                wm = w * massc[a, c : c + 32, :]
                down = down + ((wm[:8] + wm[8:16]) + (wm[16:24] + wm[24:]))
            l0 = pl.multiple_of((d // 1024) * 8, 8)
            accl[pl.ds(l0, 8), :] += down
        for copy in save(slot, i):
            copy.start()
        for u in range(U):
            s = items[(i + 1) * U + u]
            dist[u] = nn(rowf[s % 1024], lanef[s // 1024])
        return carry

    batches = (pos - FRONT + U - 1) // U
    lax.fori_loop(0, batches + 1, step, 0)

    row16 = lax.broadcasted_iota(i32, (16, HB), 0)
    for half in range(2):

        def own_sums(c8, carry):
            first = (2 * c8 * 8 + half) * 8
            total = jnp.zeros((16, 2 * HB), f32)
            for j in range(8):
                hi, lo = split(accr[2 * (c8 * 8 + j) + half])
                pick = (row16 == j).astype(bf16)
                total = total + nt(pick, jnp.concatenate([hi, lo], axis=0))
            rows8 = total[:8, :HB] + total[:8, HB:]
            for k in range(8):
                rows8 = rows8 + accl[pl.ds(first + k, 8, stride=16), :]
            to = pl.multiple_of(half * CELLS + c8 * 8, 8)
            dens[pl.ds(to, 8), :] = rows8 * DENSITY_SCALE
            return carry

        for c8 in range(CELLS // 8):
            own_sums(c8, 0)

        def near_sums(c8, carry):
            for g in range(1, 5):
                first = (2 * (g * CELLS + c8 * 8) + half) * 8
                rows8 = accl[pl.ds(first, 8, stride=16), :]
                for k in range(1, 8):
                    rows8 = rows8 + accl[pl.ds(first + k, 8, stride=16), :]
                to = pl.multiple_of(g * PLANE + half * CELLS + c8 * 8, 8)
                dens[pl.ds(to, 8), :] = rows8 * DENSITY_SCALE
            return carry

        lax.fori_loop(0, CELLS // 8, near_sums, 0)

    out = pltpu.make_async_copy(dens, dens_hbm, in_sem.at[1])
    out.start()
    listed.wait()
    for slot in range(SLOTS):
        for copy in save(slot, 0):
            copy.wait()
    out.wait()


def force_kernel(
    items_hbm, counts_hbm, near_counts_hbm, side_hbm, remote_hbm, planes_hbm, coef_hbm, gbuf,
    acc_hbm,
    items, counts, near_counts, side, remote, planes, coef, acc,
    vmat, accr, accl, gs, sem, in_sem,
):
    sources = (items_hbm, counts_hbm, near_counts_hbm, side_hbm, remote_hbm, planes_hbm, coef_hbm)
    targets = (items, counts, near_counts, side, remote, planes, coef)
    inputs = [pltpu.make_async_copy(x, y, in_sem.at[k]) for k, (x, y) in enumerate(zip(sources, targets))]
    for copy in inputs:
        copy.start()

    def load(slot, batch):
        return batch_copies(gbuf, gs, sem, slot, FRONT // U + batch, False)

    for copy in inputs:
        copy.wait()
    batches = (items[2 * LIST] - FRONT + U - 1) // U
    for slot in range(SLOTS - 1):
        for copy in load(slot, slot):
            copy.start()

    accr[...] = jnp.zeros_like(accr)
    accl[...] = jnp.zeros_like(accl)

    def build(group, c, count, block):
        for half in range(2):
            tile = cell_tile(planes, group * 5 * PLANE, c, half)
            cc = coef[pl.ds(group * PLANE + half * CELLS + c, 1), :]
            m = masked(tile[3:4, :], count, half)
            mc = m * cc
            x = tile[0:3, :] - 0.5
            stack = jnp.concatenate([m, mc, m * x, mc * x], axis=0)
            vmat[block + half] = two_pieces(stack)

    def own_cells(step, carry):
        for j in range(UNROLL):
            c = step * UNROLL + j
            build(0, c, counts[0, c], 2 * c)
        return carry

    lax.fori_loop(0, CELLS // UNROLL, own_cells, 0)

    def near_cells(step, carry):
        for j in range(UNROLL):
            k = step * UNROLL + j
            build(side[k] + 1, remote[k], near_counts[side[k], 0, remote[k]], OWN + 2 * k)
        return carry

    lax.fori_loop(0, PAIRS // UNROLL, near_cells, 0)

    def step(i, carry):
        slot = lax.rem(i, SLOTS)

        @pl.when(i + SLOTS - 1 < batches)
        def _():
            for copy in load(lax.rem(i + SLOTS - 1, SLOTS), i + SLOTS - 1):
                copy.start()

        for copy in load(slot, i):
            copy.wait()
        for u in range(U):
            s = items[FRONT + i * U + u]
            d = items[LIST + FRONT + i * U + u]
            hi, lo = split(gs[slot, u])
            to_row, to_lane = partner_sums(vmat[s % 1024], vmat[s // 1024], hi, lo)
            r0 = pl.multiple_of((d % 1024) * 8, 8)
            l0 = pl.multiple_of((d // 1024) * 8, 8)
            accr[pl.ds(r0, 8), :] += to_row
            accl[pl.ds(l0, 8), :] += to_lane
        return carry

    lax.fori_loop(0, batches, step, 0)

    for half in range(2):

        def sums(c8, carry):
            for g in range(5):
                first = (2 * (g * CELLS + c8 * 8) + half) * 8

                def total(k):
                    t = accl[pl.ds(first + k, 8, stride=16), :]
                    if g == 0:
                        t = t + accr[pl.ds(first + k, 8, stride=16), :]
                    return t

                cc = coef[pl.ds(pl.multiple_of(g * PLANE + half * CELLS + c8 * 8, 8), 8), :]
                plain = cc * total(0) + total(1)
                for k in range(3):
                    at_x = pl.multiple_of(((g * 2 + half) * 5 + k) * CELLS + c8 * 8, 8)
                    x = planes[pl.ds(at_x, 8), :] - 0.5
                    moment = cc * total(2 + k) + total(5 + k)
                    at_o = pl.multiple_of(((g * 2 + half) * 3 + k) * CELLS + c8 * 8, 8)
                    acc[pl.ds(at_o, 8), :] = (x * plain - moment) * FORCE_SCALE
            return carry

        lax.fori_loop(0, CELLS // 8, sums, 0)

    out = pltpu.make_async_copy(acc, acc_hbm, in_sem.at[0])
    out.start()
    out.wait()


def planes_of(n):
    return jax.ShapeDtypeStruct((n * PLANE, HB), f32)


def call_density(counts, near_counts, local, side, remote, planes):
    return pl.pallas_call(
        density_kernel,
        out_shape=[
            planes_of(6),
            jax.ShapeDtypeStruct((LIST, HB, HB), f32),
            jax.ShapeDtypeStruct((2 * LIST + 8,), i32),
        ],
        in_specs=[HBM] * 6,
        out_specs=[HBM] * 3,
        scratch_shapes=[
            pltpu.SMEM((1, CELLS), i32),
            pltpu.SMEM((4, 1, CELLS), i32),
            pltpu.SMEM((PAIRS,), i32),
            pltpu.SMEM((PAIRS,), i32),
            pltpu.SMEM((PAIRS,), i32),
            pltpu.SMEM((2 * LIST + 8,), i32),
            pltpu.VMEM((PLANES, HB), f32),
            pltpu.VMEM((6 * PLANE, HB), f32),
            pltpu.VMEM((OWN, HB, FEAT), bf16),
            pltpu.VMEM((READ, FEAT, 2 * HB), bf16),
            pltpu.VMEM((OWN, HB, HB), f32),
            pltpu.VMEM((READ, HB), f32),
            pltpu.VMEM((OWN + 1, HB, HB), f32),
            pltpu.VMEM(((ALL + 1) * 8, HB), f32),
            pltpu.VMEM((U, HB, 2 * HB), f32),
            pltpu.VMEM((SLOTS, U, HB, HB), f32),
            pltpu.SemaphoreType.DMA((SLOTS, PARTS)),
            pltpu.SemaphoreType.DMA((6,)),
        ],
        compiler_params=pltpu.CompilerParams(vmem_limit_bytes=60 << 20),
        name="density",
    )(counts, near_counts, local, side, remote, planes)


def call_force(items, counts, near_counts, side, remote, planes, coef, gbuf):
    return pl.pallas_call(
        force_kernel,
        out_shape=planes_of(15),
        in_specs=[HBM] * 8,
        out_specs=HBM,
        scratch_shapes=[
            pltpu.SMEM((2 * LIST + 8,), i32),
            pltpu.SMEM((1, CELLS), i32),
            pltpu.SMEM((4, 1, CELLS), i32),
            pltpu.SMEM((PAIRS,), i32),
            pltpu.SMEM((PAIRS,), i32),
            pltpu.VMEM((PLANES, HB), f32),
            pltpu.VMEM((5 * PLANE, HB), f32),
            pltpu.VMEM((15 * PLANE, HB), f32),
            pltpu.VMEM((READ, 16, HB), bf16),
            pltpu.VMEM(((OWN + 1) * 8, HB), f32),
            pltpu.VMEM(((ALL + 1) * 8, HB), f32),
            pltpu.VMEM((SLOTS, U, HB, HB), f32),
            pltpu.SemaphoreType.DMA((SLOTS, PARTS)),
            pltpu.SemaphoreType.DMA((7,)),
        ],
        compiler_params=pltpu.CompilerParams(vmem_limit_bytes=60 << 20),
        name="force",
    )(items, counts, near_counts, side, remote, planes, coef, gbuf)


def neighbours():
    i, j = lax.axis_index("gx"), lax.axis_index("yz")
    nx, ny = lax.axis_size("gx"), lax.axis_size("yz")
    return (
        (lax.rem(i + nx - 1, nx), j),
        (lax.rem(i + 1, nx), j),
        (i, lax.rem(j + ny - 1, ny)),
        (i, lax.rem(j + 1, ny)),
    )


def greet(devices):
    barrier = pltpu.get_barrier_semaphore()
    for device in devices:
        pl.semaphore_signal(barrier, inc=1, device_id=device, device_id_type=MESH)
    pl.semaphore_wait(barrier, 4)


def exchange(devices, source, target, send, recv):
    copies = []
    for s in (2, 3, 0, 1):
        copy = pltpu.make_async_remote_copy(
            src_ref=source(s),
            dst_ref=target(s ^ 1),
            send_sem=send.at[s],
            recv_sem=recv.at[s ^ 1],
            device_id=devices[s],
            device_id_type=MESH,
        )
        copy.start()
        copies.append(copy)
    return copies


def rows(ref, s, n):
    return ref.at[pl.ds(s * n, n), :]


def halo_kernel(
    positions, masses, smoothing, count,
    planes, near_count,
    pos, mass, smooth, own, in_sem, send, recv,
):
    devices = neighbours()
    sources, targets = (positions, masses, smoothing), (pos, mass, smooth)
    inputs = [pltpu.make_async_copy(x, y, in_sem.at[k]) for k, (x, y) in enumerate(zip(sources, targets))]
    for copy in inputs:
        copy.start()
    greet(devices)
    copies = exchange(devices, lambda s: count, lambda s: near_count.at[s], send.at[1], recv.at[1])
    for copy in inputs:
        copy.wait()
    for half in range(2):
        lanes = slice(half * HB, (half + 1) * HB)
        base = half * 5 * CELLS
        for k in range(3):
            own[base + k * CELLS : base + (k + 1) * CELLS, :] = pos[k, :, lanes]
        own[base + 3 * CELLS : base + 4 * CELLS, :] = mass[:, lanes]
        own[base + 4 * CELLS : base + 5 * CELLS, :] = smooth[:, lanes]
    copies += exchange(
        devices, lambda s: own, lambda s: rows(planes, s + 1, 5 * PLANE), send.at[0], recv.at[0]
    )
    keep = pltpu.make_async_copy(own, rows(planes, 0, 5 * PLANE), in_sem.at[3])
    keep.start()
    for copy in copies:
        copy.wait()
    keep.wait()


def settle_kernel(dens, rho_out, coef, mine, occ, cf, back, in_sem, send, recv):
    devices = neighbours()
    inputs = [
        pltpu.make_async_copy(rows(dens, 0, PLANE), mine, in_sem.at[0]),
        pltpu.make_async_copy(rows(dens, 5, PLANE), occ, in_sem.at[1]),
    ]
    for copy in inputs:
        copy.start()
    greet(devices)
    copies = exchange(
        devices, lambda s: rows(dens, s + 1, PLANE), lambda s: rows(back, s, PLANE), send.at[0], recv.at[0]
    )
    for copy in inputs + copies:
        copy.wait()
    rho = mine[...]
    for s in range(4):
        rho = rho + back[s * PLANE : (s + 1) * PLANE, :]
    mask = occ[...]
    cf[...] = jnp.exp(jnp.log(jnp.where(mask > 0, rho, 1.0)) * (-1.0 / 3.0)) * mask
    copies = exchange(devices, lambda s: cf, lambda s: rows(coef, s + 1, PLANE), send.at[1], recv.at[1])
    keep = pltpu.make_async_copy(cf, rows(coef, 0, PLANE), in_sem.at[0])
    keep.start()
    rho = rho * mask
    for half in range(2):
        rho_out[:, half * HB : (half + 1) * HB] = rho[half * CELLS : (half + 1) * CELLS]
    for copy in copies:
        copy.wait()
    keep.wait()


def finish_kernel(acc, dens, out, mine, occ, back, in_sem, send, recv):
    devices = neighbours()
    size = 3 * PLANE
    inputs = [
        pltpu.make_async_copy(rows(acc, 0, size), mine, in_sem.at[0]),
        pltpu.make_async_copy(rows(dens, 5, PLANE), occ, in_sem.at[1]),
    ]
    for copy in inputs:
        copy.start()
    greet(devices)
    copies = exchange(
        devices, lambda s: rows(acc, s + 1, size), lambda s: rows(back, s, size), send.at[0], recv.at[0]
    )
    for copy in inputs + copies:
        copy.wait()
    for half in range(2):
        mask = occ[half * CELLS : (half + 1) * CELLS, :]
        for k in range(3):
            at = (half * 3 + k) * CELLS
            total = mine[at : at + CELLS, :]
            for s in range(4):
                total = total + back[s * size + at : s * size + at + CELLS, :]
            out[k, :, half * HB : (half + 1) * HB] = total * mask


def remote_call(kernel, name, ident, operands, out_shape, out_specs, scratch, copies, phases):
    return pl.pallas_call(
        kernel,
        out_shape=out_shape,
        in_specs=[HBM] * len(operands),
        out_specs=out_specs,
        scratch_shapes=[pltpu.VMEM(shape, f32) for shape in scratch]
        + [pltpu.SemaphoreType.DMA((copies,))]
        + [pltpu.SemaphoreType.DMA((phases, 4))] * 2,
        compiler_params=pltpu.CompilerParams(collective_id=ident, has_side_effects=True, vmem_limit_bytes=60 << 20),
        name=name,
    )(*operands)


def body(positions, masses, smoothing, counts, pair_local, pair_side, pair_remote):
    count = counts.reshape(1, CELLS)
    local, side, remote = (x.reshape(PAIRS) for x in (pair_local, pair_side, pair_remote))
    slots = 2 * HB
    planes, near_count = remote_call(
        halo_kernel, "halo", 0, (positions[0, 0].transpose(1, 0, 2), masses[0, 0], smoothing[0, 0], count),
        [planes_of(25), jax.ShapeDtypeStruct((4, 1, CELLS), i32)], [HBM] * 2,
        [(3, CELLS, slots), (CELLS, slots), (CELLS, slots), (5 * PLANE, HB)], 4, 2,
    )
    dens, gbuf, items = call_density(count, near_count, local, side, remote, planes)
    rho, coef = remote_call(
        settle_kernel, "settle", 1, (dens,),
        [jax.ShapeDtypeStruct((CELLS, slots), f32), planes_of(5)], [VMEM, HBM],
        [(PLANE, HB), (PLANE, HB), (PLANE, HB), (4 * PLANE, HB)], 2, 2,
    )
    acc = call_force(items, count, near_count, side, remote, planes, coef, gbuf)
    accel = remote_call(
        finish_kernel, "finish", 2, (acc, dens),
        jax.ShapeDtypeStruct((3, CELLS, slots), f32), VMEM,
        [(3 * PLANE, HB), (PLANE, HB), (12 * PLANE, HB)], 2, 1,
    )
    return rho[None, None], accel.transpose(1, 0, 2)[None, None]


def solution(mesh):
    in_specs = (
        P("gx", "yz", None, None, None),
        P("gx", "yz", None, None),
        P("gx", "yz", None, None),
        P("gx", "yz", None),
        P("gx", "yz", None),
        P("gx", "yz", None),
        P("gx", "yz", None),
    )
    out_specs = (P("gx", "yz", None, None), P("gx", "yz", None, None, None))
    return jax.shard_map(body, mesh=mesh, in_specs=in_specs, out_specs=out_specs, check_vma=False)
```

```python
import math

import jax
import jax.numpy as jnp
from jax import lax
from jax.experimental import pallas as pl
from jax.experimental.pallas import tpu as pltpu
from jax.sharding import PartitionSpec as P

f32, bf16, i32 = jnp.float32, jnp.bfloat16, jnp.int32
HB = 128
CELLS = 64
PAIRS = 128
OWN = 2 * CELLS
ALL = 10 * CELLS
READ = 2 * (CELLS + PAIRS)
FEAT = 48
U = 16
PARTS = 4
SLOTS = 4
UNROLL = 4
PLANE = 2 * CELLS
PLANES = 25 * PLANE
UF = 2 * U
FRONT = U
ITEMS = 4 * PAIRS + 3 * CELLS
LIST = FRONT + ITEMS + (SLOTS + 3) * U
DENSITY_SCALE = 21.0 * 8.0 / (16.0 * math.pi)
FORCE_SCALE = 105.0 * 32.0 / (16.0 * math.pi)
SMEM = pl.BlockSpec(memory_space=pltpu.SMEM)
VMEM = pl.BlockSpec(memory_space=pltpu.VMEM)
HBM = pl.BlockSpec(memory_space=pl.ANY)
MESH = pl.DeviceIdType.MESH


def nn(a, b):
    return lax.dot_general(a, b, (((1,), (0,)), ((), ())), preferred_element_type=f32)


def nt(a, b):
    return lax.dot_general(a, b, (((1,), (1,)), ((), ())), preferred_element_type=f32)


def pieces(t):
    one = t.astype(bf16).astype(f32)
    rest = t - one
    two = rest.astype(bf16).astype(f32)
    return one, two, rest - two


def cell_tile(planes, base, cell, half):
    return planes[pl.ds(base + half * 5 * CELLS + cell, 5, stride=CELLS), :]


def masked(mass, count, half):
    slot = lax.broadcasted_iota(i32, mass.shape, 1) + half * HB
    return jnp.where(slot < count, mass, 0.0)


def masked_tile(planes, base, cell, half, count):
    tile = cell_tile(planes, base, cell, half)
    mass = masked(tile[3:4, :], count, half)
    return jnp.concatenate([tile[0:3, :], mass, tile[4:5, :], jnp.zeros((3, HB), f32)], axis=0)


def row_masks():
    row = lax.broadcasted_iota(i32, (8, HB), 0)
    return row, [(row == k).astype(f32) for k in range(8)]


def lane_features(tile, row, at):
    x = jnp.where(row < 3, tile - 0.5, 0.0)
    norm = jnp.sum(x * x, axis=0, keepdims=True)
    h = tile[4:5, :]
    dist = x + at[3] + at[4] * norm
    supp = at[5] + at[6] * h
    d1, d2, d3 = pieces(dist)
    s1, s2, s3 = pieces(supp)
    d12 = jnp.concatenate([d1, d2], axis=0).astype(bf16)
    d31 = jnp.concatenate([d3, d1], axis=0).astype(bf16)
    s12 = jnp.concatenate([s1, s2], axis=0).astype(bf16)
    s31 = jnp.concatenate([s3, s1], axis=0).astype(bf16)
    left = jnp.concatenate([d12, d12, d31], axis=0)
    right = jnp.concatenate([s12, s12, s31], axis=0)
    return jnp.concatenate([left, right], axis=1)


def row_features(tile, row, at):
    x = jnp.where(row < 3, tile - 0.5, 0.0)
    norm = jnp.sum(x * x, axis=0, keepdims=True)
    h = tile[4:5, :]
    form = -2.0 * x + at[3] * norm + at[4] + at[5] * h + at[6]
    p1, p2, p3 = pieces(form)
    rest = jnp.zeros((HB - FEAT - 8, HB), f32)
    m1, m2, m3 = pieces(at[0] * tile[3:4, :])
    masses = m1 + pltpu.roll(m2, 1, 0) + pltpu.roll(m3, 2, 0)
    rest = jnp.zeros((64 - FEAT - 8, HB), f32)
    turned = jnp.concatenate([p1, p1, p2, p2, p1, p3, masses, rest], axis=0).T.astype(bf16)
    k = lax.broadcasted_iota(i32, (64, HB), 0)
    pick = ((k >= FEAT) & (k < FEAT + 3)).astype(f32).astype(bf16)
    return turned[:, :FEAT], nn(turned, pick)


def two_pieces(tile):
    one = tile.astype(bf16).astype(f32)
    return jnp.concatenate([one, tile - one], axis=0).astype(bf16)


def fold(o):
    o = o[:, :HB] + o[:, HB:]
    return o[:8] + o[8:]


def partner_sums(va, vb, hi, lo):
    to_lane = fold(nn(va, jnp.concatenate([hi, lo], axis=1)))
    to_row = fold(nt(vb, jnp.concatenate([hi, lo], axis=0)))
    return to_row, to_lane


def split(g):
    hi = g.astype(bf16)
    return hi, (g - hi.astype(f32)).astype(bf16)


def batch_copies(buffer, gs, sem, slot, first, size, out):
    part = size // PARTS
    copies = []
    for k in range(PARTS):
        here = gs.at[slot, pl.ds(k * part, part)]
        there = buffer.at[pl.ds(first + k * part, part)]
        pair = (here, there) if out else (there, here)
        copies.append(pltpu.make_async_copy(*pair, sem.at[slot, k]))
    return copies


def density_kernel(
    counts_hbm, near_counts_hbm, local_hbm, side_hbm, remote_hbm, planes_hbm,
    dens_hbm, gbuf, items_hbm,
    counts, near_counts, local, side, remote, items, planes, dens,
    rowf, lanef, massc, massr, accr, accl, dist, gs, sem, in_sem,
):
    sources = (counts_hbm, near_counts_hbm, local_hbm, side_hbm, remote_hbm, planes_hbm)
    targets = (counts, near_counts, local, side, remote, planes)
    inputs = [pltpu.make_async_copy(x, y, in_sem.at[k]) for k, (x, y) in enumerate(zip(sources, targets))]
    for copy in inputs:
        copy.start()
    for copy in inputs[:5]:
        copy.wait()
    row, at = row_masks()

    accr[...] = jnp.zeros_like(accr)
    accl[...] = jnp.zeros_like(accl)
    dist[...] = jnp.ones_like(dist)

    def build(tile, block):
        lanef[block] = lane_features(tile, row, at)
        massr[pl.ds(block, 1), :] = tile[3:4, :]

    def dummy(i, carry):
        items[i] = 0
        items[LIST + i] = OWN + ALL * 1024
        return carry

    lax.fori_loop(0, FRONT, dummy, 0)

    def put(pos, a, b, da, db):
        items[pos] = a + b * 1024
        items[LIST + pos] = da + db * 1024

    def pair_items(step, pos):
        for j in range(UNROLL):
            k = step * UNROLL + j
            for half in range(2):
                count = near_counts[side[k], 0, remote[k]]
                tile = masked_tile(planes, (side[k] + 1) * 5 * PLANE, remote[k], half, count)
                build(tile, OWN + 2 * k + half)
            a = local[k]
            two_a = (counts[0, a] > HB).astype(i32)
            two_b = (near_counts[side[k], 0, remote[k]] > HB).astype(i32)
            a0, b0 = 2 * a, OWN + 2 * k
            d0 = 2 * (side[k] * CELLS + remote[k] + CELLS)
            put(pos, a0, b0, a0, d0)
            pos = pos + 1
            put(pos, a0, b0 + 1, a0, d0 + 1)
            pos = pos + two_b
            put(pos, a0 + 1, b0, a0 + 1, d0)
            pos = pos + two_a
            put(pos, a0 + 1, b0 + 1, a0 + 1, d0 + 1)
            pos = pos + two_a * two_b
        return pos

    def self_items(step, pos):
        for j in range(UNROLL):
            a = step * UNROLL + j
            for half in range(2):
                tile = masked_tile(planes, 0, a, half, counts[0, a])
                build(tile, 2 * a + half)
                rowf[2 * a + half], massc[2 * a + half] = row_features(tile, row, at)
                occ = masked(jnp.ones((1, HB), f32), counts[0, a], half)
                dens[pl.ds(5 * PLANE + half * CELLS + a, 1), :] = occ
            two = (counts[0, a] > HB).astype(i32)
            a0 = 2 * a
            put(pos, a0, a0, OWN, a0)
            pos = pos + 1
            put(pos, a0, a0 + 1, a0, a0 + 1)
            pos = pos + two
            put(pos, a0 + 1, a0 + 1, OWN, a0 + 1)
            pos = pos + two
        return pos

    inputs[5].wait()
    pos = lax.fori_loop(0, CELLS // UNROLL, self_items, FRONT)
    pos = lax.fori_loop(0, PAIRS // UNROLL, pair_items, pos)
    lax.fori_loop(pos, pos + (SLOTS + 2) * U, dummy, 0)
    items[2 * LIST] = pos
    listed = pltpu.make_async_copy(items, items_hbm, in_sem.at[0])
    listed.start()

    def save(slot, batch):
        return batch_copies(gbuf, gs, sem, slot, batch * U, U, True)

    for slot in range(SLOTS):
        for copy in save(slot, LIST // U - SLOTS + slot):
            copy.start()

    def step(i, carry):
        slot = lax.rem(i, SLOTS)
        for copy in save(slot, i):
            copy.wait()
        for u in range(U):
            s = items[i * U + u]
            d = items[LIST + i * U + u]
            a, ra = s % 1024, d % 1024
            mq = massr[pl.ds(s // 1024, 1), :]
            down = jnp.zeros((8, HB), f32)
            for c in range(0, HB, 32):
                r2 = jnp.maximum(dist[u, c : c + 32, :HB], 1e-12)
                h2 = dist[u, c : c + 32, HB:]
                r = r2 * lax.rsqrt(r2)
                q = 1.0 / h2
                q2 = q * q
                y = jnp.maximum(q - r * q2, 0.0)
                y2 = y * y
                gs[slot, u, c : c + 32, :] = (y2 * y) * q2
                w = (y2 * y2) * (h2 + 4.0 * r)
                accr[ra, c : c + 32, :] += w * mq
                wm = w * massc[a, c : c + 32, :]
                down = down + ((wm[:8] + wm[8:16]) + (wm[16:24] + wm[24:]))
            l0 = pl.multiple_of((d // 1024) * 8, 8)
            accl[pl.ds(l0, 8), :] += down
        for copy in save(slot, i):
            copy.start()
        for u in range(U):
            s = items[(i + 1) * U + u]
            dist[u] = nn(rowf[s % 1024], lanef[s // 1024])
        return carry

    batches = (pos - FRONT + U - 1) // U
    lax.fori_loop(0, batches + 1, step, 0)

    row16 = lax.broadcasted_iota(i32, (16, HB), 0)
    for half in range(2):

        def own_sums(c8, carry):
            first = (2 * c8 * 8 + half) * 8
            total = jnp.zeros((16, 2 * HB), f32)
            for j in range(8):
                hi, lo = split(accr[2 * (c8 * 8 + j) + half])
                pick = (row16 == j).astype(bf16)
                total = total + nt(pick, jnp.concatenate([hi, lo], axis=0))
            rows8 = total[:8, :HB] + total[:8, HB:]
            for k in range(8):
                rows8 = rows8 + accl[pl.ds(first + k, 8, stride=16), :]
            to = pl.multiple_of(half * CELLS + c8 * 8, 8)
            dens[pl.ds(to, 8), :] = rows8 * DENSITY_SCALE
            return carry

        for c8 in range(CELLS // 8):
            own_sums(c8, 0)

        def near_sums(c8, carry):
            for g in range(1, 5):
                first = (2 * (g * CELLS + c8 * 8) + half) * 8
                rows8 = accl[pl.ds(first, 8, stride=16), :]
                for k in range(1, 8):
                    rows8 = rows8 + accl[pl.ds(first + k, 8, stride=16), :]
                to = pl.multiple_of(g * PLANE + half * CELLS + c8 * 8, 8)
                dens[pl.ds(to, 8), :] = rows8 * DENSITY_SCALE
            return carry

        lax.fori_loop(0, CELLS // 8, near_sums, 0)

    out = pltpu.make_async_copy(dens, dens_hbm, in_sem.at[1])
    out.start()
    listed.wait()
    for slot in range(SLOTS):
        for copy in save(slot, 0):
            copy.wait()
    out.wait()


def force_kernel(
    items_hbm, counts_hbm, near_counts_hbm, side_hbm, remote_hbm, planes_hbm, coef_hbm, gbuf,
    acc_hbm, rho_hbm,
    items, counts, near_counts, side, remote, planes, coef, acc, rho,
    vmat, accr, accl, gs, sem, in_sem,
):
    sources = (items_hbm, counts_hbm, near_counts_hbm, side_hbm, remote_hbm, planes_hbm, coef_hbm)
    targets = (items, counts, near_counts, side, remote, planes, coef)
    inputs = [pltpu.make_async_copy(x, y, in_sem.at[k]) for k, (x, y) in enumerate(zip(sources, targets))]
    for copy in inputs:
        copy.start()

    def load(slot, batch):
        return batch_copies(gbuf, gs, sem, slot, FRONT + batch * UF, UF, False)

    for copy in inputs:
        copy.wait()
    batches = (items[2 * LIST] - FRONT + UF - 1) // UF
    for slot in range(SLOTS - 1):
        for copy in load(slot, slot):
            copy.start()

    for half in range(2):
        at_r = 5 * PLANE + half * CELLS
        rho[:, half * HB : (half + 1) * HB] = coef[at_r : at_r + CELLS, :]
    settled = pltpu.make_async_copy(rho, rho_hbm, in_sem.at[1])
    settled.start()

    accr[...] = jnp.zeros_like(accr)
    accl[...] = jnp.zeros_like(accl)

    def build(group, c, count, block):
        for half in range(2):
            tile = cell_tile(planes, group * 5 * PLANE, c, half)
            cc = coef[pl.ds(group * PLANE + half * CELLS + c, 1), :]
            m = masked(tile[3:4, :], count, half)
            mc = m * cc
            x = tile[0:3, :] - 0.5
            stack = jnp.concatenate([m, mc, m * x, mc * x], axis=0)
            vmat[block + half] = two_pieces(stack)

    def own_cells(step, carry):
        for j in range(UNROLL):
            c = step * UNROLL + j
            build(0, c, counts[0, c], 2 * c)
        return carry

    lax.fori_loop(0, CELLS // UNROLL, own_cells, 0)

    def near_cells(step, carry):
        for j in range(UNROLL):
            k = step * UNROLL + j
            build(side[k] + 1, remote[k], near_counts[side[k], 0, remote[k]], OWN + 2 * k)
        return carry

    lax.fori_loop(0, PAIRS // UNROLL, near_cells, 0)

    def step(i, carry):
        slot = lax.rem(i, SLOTS)

        @pl.when(i + SLOTS - 1 < batches)
        def _():
            for copy in load(lax.rem(i + SLOTS - 1, SLOTS), i + SLOTS - 1):
                copy.start()

        for copy in load(slot, i):
            copy.wait()
        for u in range(UF):
            s = items[FRONT + i * UF + u]
            d = items[LIST + FRONT + i * UF + u]
            hi, lo = split(gs[slot, u])
            to_row, to_lane = partner_sums(vmat[s % 1024], vmat[s // 1024], hi, lo)
            r0 = pl.multiple_of((d % 1024) * 8, 8)
            l0 = pl.multiple_of((d // 1024) * 8, 8)
            accr[pl.ds(r0, 8), :] += to_row
            accl[pl.ds(l0, 8), :] += to_lane
        return carry

    lax.fori_loop(0, batches, step, 0)

    for half in range(2):

        def sums(c8, carry):
            for g in range(5):
                first = (2 * (g * CELLS + c8 * 8) + half) * 8

                def total(k):
                    t = accl[pl.ds(first + k, 8, stride=16), :]
                    if g == 0:
                        t = t + accr[pl.ds(first + k, 8, stride=16), :]
                    return t

                cc = coef[pl.ds(pl.multiple_of(g * PLANE + half * CELLS + c8 * 8, 8), 8), :]
                plain = cc * total(0) + total(1)
                for k in range(3):
                    at_x = pl.multiple_of(((g * 2 + half) * 5 + k) * CELLS + c8 * 8, 8)
                    x = planes[pl.ds(at_x, 8), :] - 0.5
                    moment = cc * total(2 + k) + total(5 + k)
                    at_o = pl.multiple_of((g * 3 + k) * CELLS + c8 * 8, 8)
                    acc[pl.ds(at_o, 8), half * HB : (half + 1) * HB] = jnp.where(
                        cc > 0, (x * plain - moment) * FORCE_SCALE, 0.0
                    )
            return carry

        lax.fori_loop(0, CELLS // 8, sums, 0)

    out = pltpu.make_async_copy(acc, acc_hbm, in_sem.at[0])
    out.start()
    out.wait()
    settled.wait()


def planes_of(n):
    return jax.ShapeDtypeStruct((n * PLANE, HB), f32)


def call_density(counts, near_counts, local, side, remote, planes):
    return pl.pallas_call(
        density_kernel,
        out_shape=[
            planes_of(6),
            jax.ShapeDtypeStruct((LIST, HB, HB), f32),
            jax.ShapeDtypeStruct((2 * LIST + 8,), i32),
        ],
        in_specs=[HBM] * 6,
        out_specs=[HBM] * 3,
        scratch_shapes=[
            pltpu.SMEM((1, CELLS), i32),
            pltpu.SMEM((4, 1, CELLS), i32),
            pltpu.SMEM((PAIRS,), i32),
            pltpu.SMEM((PAIRS,), i32),
            pltpu.SMEM((PAIRS,), i32),
            pltpu.SMEM((2 * LIST + 8,), i32),
            pltpu.VMEM((PLANES, HB), f32),
            pltpu.VMEM((6 * PLANE, HB), f32),
            pltpu.VMEM((OWN, HB, FEAT), bf16),
            pltpu.VMEM((READ, FEAT, 2 * HB), bf16),
            pltpu.VMEM((OWN, HB, HB), f32),
            pltpu.VMEM((READ, HB), f32),
            pltpu.VMEM((OWN + 1, HB, HB), f32),
            pltpu.VMEM(((ALL + 1) * 8, HB), f32),
            pltpu.VMEM((U, HB, 2 * HB), f32),
            pltpu.VMEM((SLOTS, U, HB, HB), f32),
            pltpu.SemaphoreType.DMA((SLOTS, PARTS)),
            pltpu.SemaphoreType.DMA((6,)),
        ],
        compiler_params=pltpu.CompilerParams(vmem_limit_bytes=60 << 20),
        name="density",
    )(counts, near_counts, local, side, remote, planes)


def call_force(items, counts, near_counts, side, remote, planes, coef, gbuf):
    return pl.pallas_call(
        force_kernel,
        out_shape=[jax.ShapeDtypeStruct((15 * CELLS, 2 * HB), f32), jax.ShapeDtypeStruct((CELLS, 2 * HB), f32)],
        in_specs=[HBM] * 8,
        out_specs=[HBM] * 2,
        scratch_shapes=[
            pltpu.SMEM((2 * LIST + 8,), i32),
            pltpu.SMEM((1, CELLS), i32),
            pltpu.SMEM((4, 1, CELLS), i32),
            pltpu.SMEM((PAIRS,), i32),
            pltpu.SMEM((PAIRS,), i32),
            pltpu.VMEM((PLANES, HB), f32),
            pltpu.VMEM((6 * PLANE, HB), f32),
            pltpu.VMEM((15 * CELLS, 2 * HB), f32),
            pltpu.VMEM((CELLS, 2 * HB), f32),
            pltpu.VMEM((READ, 16, HB), bf16),
            pltpu.VMEM(((OWN + 1) * 8, HB), f32),
            pltpu.VMEM(((ALL + 1) * 8, HB), f32),
            pltpu.VMEM((SLOTS, UF, HB, HB), f32),
            pltpu.SemaphoreType.DMA((SLOTS, PARTS)),
            pltpu.SemaphoreType.DMA((7,)),
        ],
        compiler_params=pltpu.CompilerParams(vmem_limit_bytes=60 << 20),
        name="force",
    )(items, counts, near_counts, side, remote, planes, coef, gbuf)


def neighbours():
    i, j = lax.axis_index("gx"), lax.axis_index("yz")
    nx, ny = lax.axis_size("gx"), lax.axis_size("yz")
    return (
        (lax.rem(i + nx - 1, nx), j),
        (lax.rem(i + 1, nx), j),
        (i, lax.rem(j + ny - 1, ny)),
        (i, lax.rem(j + 1, ny)),
    )


def greet(devices):
    barrier = pltpu.get_barrier_semaphore()
    for device in devices:
        pl.semaphore_signal(barrier, inc=1, device_id=device, device_id_type=MESH)
    pl.semaphore_wait(barrier, 4)


def exchange(devices, source, target, send, recv):
    copies = []
    for s in (2, 3, 0, 1):
        copy = pltpu.make_async_remote_copy(
            src_ref=source(s),
            dst_ref=target(s ^ 1),
            send_sem=send.at[s],
            recv_sem=recv.at[s ^ 1],
            device_id=devices[s],
            device_id_type=MESH,
        )
        copy.start()
        copies.append(copy)
    return copies


def rows(ref, s, n):
    return ref.at[pl.ds(s * n, n), :]


def halo_kernel(
    positions, masses, smoothing, count,
    planes, near_count,
    pos, mass, smooth, own, in_sem, send, recv,
):
    devices = neighbours()
    sources, targets = (positions, masses, smoothing), (pos, mass, smooth)
    inputs = [pltpu.make_async_copy(x, y, in_sem.at[k]) for k, (x, y) in enumerate(zip(sources, targets))]
    for copy in inputs:
        copy.start()
    greet(devices)
    copies = exchange(devices, lambda s: count, lambda s: near_count.at[s], send.at[1], recv.at[1])
    for copy in inputs:
        copy.wait()
    for half in range(2):
        lanes = slice(half * HB, (half + 1) * HB)
        base = half * 5 * CELLS
        for k in range(3):
            own[base + k * CELLS : base + (k + 1) * CELLS, :] = pos[k, :, lanes]
        own[base + 3 * CELLS : base + 4 * CELLS, :] = mass[:, lanes]
        own[base + 4 * CELLS : base + 5 * CELLS, :] = smooth[:, lanes]
    copies += exchange(
        devices, lambda s: own, lambda s: rows(planes, s + 1, 5 * PLANE), send.at[0], recv.at[0]
    )
    keep = pltpu.make_async_copy(own, rows(planes, 0, 5 * PLANE), in_sem.at[3])
    keep.start()
    for copy in copies:
        copy.wait()
    keep.wait()


def settle_kernel(dens, coef, mine, occ, cf, rho_out, back, in_sem, send, recv):
    devices = neighbours()
    inputs = [
        pltpu.make_async_copy(rows(dens, 0, PLANE), mine, in_sem.at[0]),
        pltpu.make_async_copy(rows(dens, 5, PLANE), occ, in_sem.at[1]),
    ]
    for copy in inputs:
        copy.start()
    greet(devices)
    copies = exchange(
        devices, lambda s: rows(dens, s + 1, PLANE), lambda s: rows(back, s, PLANE), send.at[0], recv.at[0]
    )
    for copy in inputs + copies:
        copy.wait()
    rho = mine[...]
    for s in range(4):
        rho = rho + back[s * PLANE : (s + 1) * PLANE, :]
    mask = occ[...]
    cf[...] = jnp.exp(jnp.log(jnp.where(mask > 0, rho, 1.0)) * (-1.0 / 3.0)) * mask
    copies = exchange(devices, lambda s: cf, lambda s: rows(coef, s + 1, PLANE), send.at[1], recv.at[1])
    rho_out[...] = rho * mask
    keep = [
        pltpu.make_async_copy(cf, rows(coef, 0, PLANE), in_sem.at[0]),
        pltpu.make_async_copy(rho_out, rows(coef, 5, PLANE), in_sem.at[1]),
    ]
    for copy in keep:
        copy.start()
    for copy in copies + keep:
        copy.wait()


def finish_kernel(acc, back, in_sem, send, recv):
    devices = neighbours()
    greet(devices)
    size = 3 * CELLS
    copies = exchange(
        devices, lambda s: rows(acc, s + 1, size), lambda s: rows(back, s, size), send.at[0], recv.at[0]
    )
    for copy in copies:
        copy.wait()


def remote_call(kernel, name, ident, operands, out_shape, out_specs, scratch, copies, phases):
    return pl.pallas_call(
        kernel,
        out_shape=out_shape,
        in_specs=[HBM] * len(operands),
        out_specs=out_specs,
        scratch_shapes=[pltpu.VMEM(shape, f32) for shape in scratch]
        + [pltpu.SemaphoreType.DMA((copies,))]
        + [pltpu.SemaphoreType.DMA((phases, 4))] * 2,
        compiler_params=pltpu.CompilerParams(collective_id=ident, has_side_effects=True, vmem_limit_bytes=60 << 20),
        name=name,
    )(*operands)


def body(positions, masses, smoothing, counts, pair_local, pair_side, pair_remote):
    count = counts.reshape(1, CELLS)
    local, side, remote = (x.reshape(PAIRS) for x in (pair_local, pair_side, pair_remote))
    slots = 2 * HB
    planes, near_count = remote_call(
        halo_kernel, "halo", 0, (positions[0, 0].transpose(1, 0, 2), masses[0, 0], smoothing[0, 0], count),
        [planes_of(25), jax.ShapeDtypeStruct((4, 1, CELLS), i32)], [HBM] * 2,
        [(3, CELLS, slots), (CELLS, slots), (CELLS, slots), (5 * PLANE, HB)], 4, 2,
    )
    dens, gbuf, items = call_density(count, near_count, local, side, remote, planes)
    coef = remote_call(
        settle_kernel, "settle", 1, (dens,), planes_of(6), HBM,
        [(PLANE, HB)] * 4 + [(4 * PLANE, HB)], 2, 2,
    )
    acc, rho = call_force(items, count, near_count, side, remote, planes, coef, gbuf)
    back = remote_call(
        finish_kernel, "finish", 2, (acc,), jax.ShapeDtypeStruct((12 * CELLS, slots), f32), HBM, [], 1, 1
    )
    total = acc[: 3 * CELLS]
    for s in range(4):
        total = total + back[3 * s * CELLS : 3 * (s + 1) * CELLS]
    return rho[None, None], total.reshape(3, CELLS, slots).transpose(1, 0, 2)[None, None]


def solution(mesh):
    in_specs = (
        P("gx", "yz", None, None, None),
        P("gx", "yz", None, None),
        P("gx", "yz", None, None),
        P("gx", "yz", None),
        P("gx", "yz", None),
        P("gx", "yz", None),
        P("gx", "yz", None),
    )
    out_specs = (P("gx", "yz", None, None), P("gx", "yz", None, None, None))
    return jax.shard_map(body, mesh=mesh, in_specs=in_specs, out_specs=out_specs, check_vma=False)
```

```python
import math

import jax
import jax.numpy as jnp
from jax import lax
from jax.experimental import pallas as pl
from jax.experimental.pallas import tpu as pltpu
from jax.sharding import PartitionSpec as P

f32, bf16, i32 = jnp.float32, jnp.bfloat16, jnp.int32
HB = 128
CELLS = 64
PAIRS = 128
OWN = 2 * CELLS
ALL = 10 * CELLS
READ = 2 * (CELLS + PAIRS)
FEAT = 48
U = 16
PARTS = 4
SLOTS = 4
UNROLL = 4
PLANE = 2 * CELLS
PLANES = 25 * PLANE
UF = 2 * U
FRONT = U
ITEMS = 4 * PAIRS + 3 * CELLS
LIST = FRONT + ITEMS + (SLOTS + 3) * U
DENSITY_SCALE = 21.0 * 8.0 / (16.0 * math.pi)
FORCE_SCALE = 105.0 * 32.0 / (16.0 * math.pi)
SMEM = pl.BlockSpec(memory_space=pltpu.SMEM)
VMEM = pl.BlockSpec(memory_space=pltpu.VMEM)
HBM = pl.BlockSpec(memory_space=pl.ANY)
MESH = pl.DeviceIdType.MESH


def nn(a, b):
    return lax.dot_general(a, b, (((1,), (0,)), ((), ())), preferred_element_type=f32)


def nt(a, b):
    return lax.dot_general(a, b, (((1,), (1,)), ((), ())), preferred_element_type=f32)


def pieces(t):
    one = t.astype(bf16).astype(f32)
    rest = t - one
    two = rest.astype(bf16).astype(f32)
    return one, two, rest - two


def cell_tile(planes, base, cell, half):
    return planes[pl.ds(base + half * 5 * CELLS + cell, 5, stride=CELLS), :]


def masked(mass, count, half):
    slot = lax.broadcasted_iota(i32, mass.shape, 1) + half * HB
    return jnp.where(slot < count, mass, 0.0)


def masked_tile(planes, base, cell, half, count):
    tile = cell_tile(planes, base, cell, half)
    mass = masked(tile[3:4, :], count, half)
    return jnp.concatenate([tile[0:3, :], mass, tile[4:5, :], jnp.zeros((3, HB), f32)], axis=0)


def row_masks():
    row = lax.broadcasted_iota(i32, (8, HB), 0)
    return row, [(row == k).astype(f32) for k in range(8)]


def lane_features(tile, row, at):
    x = jnp.where(row < 3, tile - 0.5, 0.0)
    norm = jnp.sum(x * x, axis=0, keepdims=True)
    h = tile[4:5, :]
    dist = x + at[3] + at[4] * norm
    supp = at[5] + at[6] * h
    d1, d2, d3 = pieces(dist)
    s1, s2, s3 = pieces(supp)
    d12 = jnp.concatenate([d1, d2], axis=0).astype(bf16)
    d31 = jnp.concatenate([d3, d1], axis=0).astype(bf16)
    s12 = jnp.concatenate([s1, s2], axis=0).astype(bf16)
    s31 = jnp.concatenate([s3, s1], axis=0).astype(bf16)
    left = jnp.concatenate([d12, d12, d31], axis=0)
    right = jnp.concatenate([s12, s12, s31], axis=0)
    return jnp.concatenate([left, right], axis=1)


def row_features(tile, row, at):
    x = jnp.where(row < 3, tile - 0.5, 0.0)
    norm = jnp.sum(x * x, axis=0, keepdims=True)
    h = tile[4:5, :]
    form = -2.0 * x + at[3] * norm + at[4] + at[5] * h + at[6]
    p1, p2, p3 = pieces(form)
    rest = jnp.zeros((HB - FEAT - 8, HB), f32)
    m1, m2, m3 = pieces(at[0] * tile[3:4, :])
    masses = m1 + pltpu.roll(m2, 1, 0) + pltpu.roll(m3, 2, 0)
    rest = jnp.zeros((64 - FEAT - 8, HB), f32)
    turned = jnp.concatenate([p1, p1, p2, p2, p1, p3, masses, rest], axis=0).T.astype(bf16)
    k = lax.broadcasted_iota(i32, (64, HB), 0)
    pick = ((k >= FEAT) & (k < FEAT + 3)).astype(f32).astype(bf16)
    return turned[:, :FEAT], nn(turned, pick)


def two_pieces(tile):
    one = tile.astype(bf16).astype(f32)
    return jnp.concatenate([one, tile - one], axis=0).astype(bf16)


def fold(o):
    o = o[:, :HB] + o[:, HB:]
    return o[:8] + o[8:]


def partner_sums(va, vb, hi, lo):
    to_lane = fold(nn(va, jnp.concatenate([hi, lo], axis=1)))
    to_row = fold(nt(vb, jnp.concatenate([hi, lo], axis=0)))
    return to_row, to_lane


def split(g):
    hi = g.astype(bf16)
    return hi, (g - hi.astype(f32)).astype(bf16)


def batch_copies(buffer, gs, sem, slot, first, size, out):
    part = size // PARTS
    copies = []
    for k in range(PARTS):
        here = gs.at[slot, pl.ds(k * part, part)]
        there = buffer.at[pl.ds(first + k * part, part)]
        pair = (here, there) if out else (there, here)
        copies.append(pltpu.make_async_copy(*pair, sem.at[slot, k]))
    return copies


def density_kernel(
    counts_hbm, near_counts_hbm, local_hbm, side_hbm, remote_hbm, planes_hbm,
    dens_hbm, gbuf, items_hbm,
    counts, near_counts, local, side, remote, items, planes, dens,
    rowf, lanef, massc, massr, accr, accl, dist, gs, sem, in_sem, plane_sem,
):
    sources = (counts_hbm, near_counts_hbm, local_hbm, side_hbm, remote_hbm)
    targets = (counts, near_counts, local, side, remote)
    moved = plane_copies(planes_hbm, planes, plane_sem)
    inputs = [pltpu.make_async_copy(x, y, in_sem.at[k]) for k, (x, y) in enumerate(zip(sources, targets))]
    for copy in inputs + moved:
        copy.start()
    for copy in inputs:
        copy.wait()
    row, at = row_masks()

    accr[...] = jnp.zeros_like(accr)
    accl[...] = jnp.zeros_like(accl)
    dist[...] = jnp.ones_like(dist)

    def build(tile, block):
        lanef[block] = lane_features(tile, row, at)
        massr[pl.ds(block, 1), :] = tile[3:4, :]

    def dummy(i, carry):
        items[i] = 0
        items[LIST + i] = OWN + ALL * 1024
        return carry

    lax.fori_loop(0, FRONT, dummy, 0)

    def put(pos, a, b, da, db):
        items[pos] = a + b * 1024
        items[LIST + pos] = da + db * 1024

    def pair_items(step, pos):
        for j in range(UNROLL):
            k = step * UNROLL + j
            for half in range(2):
                count = near_counts[side[k], 0, remote[k]]
                tile = masked_tile(planes, (side[k] + 1) * 5 * PLANE, remote[k], half, count)
                build(tile, OWN + 2 * k + half)
            a = local[k]
            two_a = (counts[0, a] > HB).astype(i32)
            two_b = (near_counts[side[k], 0, remote[k]] > HB).astype(i32)
            a0, b0 = 2 * a, OWN + 2 * k
            d0 = 2 * (side[k] * CELLS + remote[k] + CELLS)
            put(pos, a0, b0, a0, d0)
            pos = pos + 1
            put(pos, a0, b0 + 1, a0, d0 + 1)
            pos = pos + two_b
            put(pos, a0 + 1, b0, a0 + 1, d0)
            pos = pos + two_a
            put(pos, a0 + 1, b0 + 1, a0 + 1, d0 + 1)
            pos = pos + two_a * two_b
        return pos

    def self_items(step, pos):
        for j in range(UNROLL):
            a = step * UNROLL + j
            for half in range(2):
                tile = masked_tile(planes, 0, a, half, counts[0, a])
                build(tile, 2 * a + half)
                rowf[2 * a + half], massc[2 * a + half] = row_features(tile, row, at)
                occ = masked(jnp.ones((1, HB), f32), counts[0, a], half)
                dens[pl.ds(5 * PLANE + half * CELLS + a, 1), :] = occ
            two = (counts[0, a] > HB).astype(i32)
            a0 = 2 * a
            put(pos, a0, a0, OWN, a0)
            pos = pos + 1
            put(pos, a0, a0 + 1, a0, a0 + 1)
            pos = pos + two
            put(pos, a0 + 1, a0 + 1, OWN, a0 + 1)
            pos = pos + two
        return pos

    for copy in moved:
        copy.wait()
    pos = lax.fori_loop(0, CELLS // UNROLL, self_items, FRONT)
    pos = lax.fori_loop(0, PAIRS // UNROLL, pair_items, pos)
    lax.fori_loop(pos, pos + (SLOTS + 2) * U, dummy, 0)
    items[2 * LIST] = pos
    listed = pltpu.make_async_copy(items, items_hbm, in_sem.at[0])
    listed.start()

    def save(slot, batch):
        return batch_copies(gbuf, gs, sem, slot, batch * U, U, True)

    for slot in range(SLOTS):
        for copy in save(slot, LIST // U - SLOTS + slot):
            copy.start()

    def step(i, carry):
        slot = lax.rem(i, SLOTS)
        for copy in save(slot, i):
            copy.wait()
        for u in range(U):
            s = items[i * U + u]
            d = items[LIST + i * U + u]
            a, ra = s % 1024, d % 1024
            mq = massr[pl.ds(s // 1024, 1), :]
            down = jnp.zeros((8, HB), f32)
            for c in range(0, HB, 32):
                r2 = jnp.maximum(dist[u, c : c + 32, :HB], 1e-12)
                h2 = dist[u, c : c + 32, HB:]
                r = r2 * lax.rsqrt(r2)
                q = 1.0 / h2
                q2 = q * q
                y = jnp.maximum(q - r * q2, 0.0)
                y2 = y * y
                gs[slot, u, c : c + 32, :] = (y2 * y) * q2
                w = (y2 * y2) * (h2 + 4.0 * r)
                accr[ra, c : c + 32, :] += w * mq
                wm = w * massc[a, c : c + 32, :]
                down = down + ((wm[:8] + wm[8:16]) + (wm[16:24] + wm[24:]))
            l0 = pl.multiple_of((d // 1024) * 8, 8)
            accl[pl.ds(l0, 8), :] += down
        for copy in save(slot, i):
            copy.start()
        for u in range(U):
            s = items[(i + 1) * U + u]
            dist[u] = nn(rowf[s % 1024], lanef[s // 1024])
        return carry

    batches = (pos - FRONT + U - 1) // U
    lax.fori_loop(0, batches + 1, step, 0)

    row16 = lax.broadcasted_iota(i32, (16, HB), 0)
    for half in range(2):

        def own_sums(c8, carry):
            first = (2 * c8 * 8 + half) * 8
            total = jnp.zeros((16, 2 * HB), f32)
            for j in range(8):
                hi, lo = split(accr[2 * (c8 * 8 + j) + half])
                pick = (row16 == j).astype(bf16)
                total = total + nt(pick, jnp.concatenate([hi, lo], axis=0))
            rows8 = total[:8, :HB] + total[:8, HB:]
            for k in range(8):
                rows8 = rows8 + accl[pl.ds(first + k, 8, stride=16), :]
            to = pl.multiple_of(half * CELLS + c8 * 8, 8)
            dens[pl.ds(to, 8), :] = rows8 * DENSITY_SCALE
            return carry

        for c8 in range(CELLS // 8):
            own_sums(c8, 0)

        def near_sums(c8, carry):
            for g in range(1, 5):
                first = (2 * (g * CELLS + c8 * 8) + half) * 8
                rows8 = accl[pl.ds(first, 8, stride=16), :]
                for k in range(1, 8):
                    rows8 = rows8 + accl[pl.ds(first + k, 8, stride=16), :]
                to = pl.multiple_of(g * PLANE + half * CELLS + c8 * 8, 8)
                dens[pl.ds(to, 8), :] = rows8 * DENSITY_SCALE
            return carry

        lax.fori_loop(0, CELLS // 8, near_sums, 0)

    out = pltpu.make_async_copy(dens, dens_hbm, in_sem.at[1])
    out.start()
    listed.wait()
    for slot in range(SLOTS):
        for copy in save(slot, 0):
            copy.wait()
    out.wait()


def force_kernel(
    items_hbm, counts_hbm, near_counts_hbm, side_hbm, remote_hbm, planes_hbm, coef_hbm, gbuf,
    acc_hbm, rho_hbm,
    items, counts, near_counts, side, remote, planes, coef, acc, rho,
    vmat, accr, accl, gs, sem, in_sem, plane_sem,
):
    sources = (items_hbm, counts_hbm, near_counts_hbm, side_hbm, remote_hbm, coef_hbm)
    targets = (items, counts, near_counts, side, remote, coef)
    inputs = [pltpu.make_async_copy(x, y, in_sem.at[k]) for k, (x, y) in enumerate(zip(sources, targets))]
    inputs += plane_copies(planes_hbm, planes, plane_sem)
    for copy in inputs:
        copy.start()

    def load(slot, batch):
        return batch_copies(gbuf, gs, sem, slot, FRONT + batch * UF, UF, False)

    for copy in inputs:
        copy.wait()
    batches = (items[2 * LIST] - FRONT + UF - 1) // UF
    for slot in range(SLOTS - 1):
        for copy in load(slot, slot):
            copy.start()

    for half in range(2):
        at_r = 5 * PLANE + half * CELLS
        rho[:, half * HB : (half + 1) * HB] = coef[at_r : at_r + CELLS, :]
    settled = pltpu.make_async_copy(rho, rho_hbm, in_sem.at[1])
    settled.start()

    accr[...] = jnp.zeros_like(accr)
    accl[...] = jnp.zeros_like(accl)

    def build(group, c, count, block):
        for half in range(2):
            tile = cell_tile(planes, group * 5 * PLANE, c, half)
            cc = coef[pl.ds(group * PLANE + half * CELLS + c, 1), :]
            m = masked(tile[3:4, :], count, half)
            mc = m * cc
            x = tile[0:3, :] - 0.5
            stack = jnp.concatenate([m, mc, m * x, mc * x], axis=0)
            vmat[block + half] = two_pieces(stack)

    def own_cells(step, carry):
        for j in range(UNROLL):
            c = step * UNROLL + j
            build(0, c, counts[0, c], 2 * c)
        return carry

    lax.fori_loop(0, CELLS // UNROLL, own_cells, 0)

    def near_cells(step, carry):
        for j in range(UNROLL):
            k = step * UNROLL + j
            build(side[k] + 1, remote[k], near_counts[side[k], 0, remote[k]], OWN + 2 * k)
        return carry

    lax.fori_loop(0, PAIRS // UNROLL, near_cells, 0)

    def step(i, carry):
        slot = lax.rem(i, SLOTS)

        @pl.when(i + SLOTS - 1 < batches)
        def _():
            for copy in load(lax.rem(i + SLOTS - 1, SLOTS), i + SLOTS - 1):
                copy.start()

        for copy in load(slot, i):
            copy.wait()
        for u in range(UF):
            s = items[FRONT + i * UF + u]
            d = items[LIST + FRONT + i * UF + u]
            hi, lo = split(gs[slot, u])
            to_row, to_lane = partner_sums(vmat[s % 1024], vmat[s // 1024], hi, lo)
            r0 = pl.multiple_of((d % 1024) * 8, 8)
            l0 = pl.multiple_of((d // 1024) * 8, 8)
            accr[pl.ds(r0, 8), :] += to_row
            accl[pl.ds(l0, 8), :] += to_lane
        return carry

    lax.fori_loop(0, batches, step, 0)

    for half in range(2):

        def sums(c8, carry):
            for g in range(5):
                first = (2 * (g * CELLS + c8 * 8) + half) * 8

                def total(k):
                    t = accl[pl.ds(first + k, 8, stride=16), :]
                    if g == 0:
                        t = t + accr[pl.ds(first + k, 8, stride=16), :]
                    return t

                cc = coef[pl.ds(pl.multiple_of(g * PLANE + half * CELLS + c8 * 8, 8), 8), :]
                plain = cc * total(0) + total(1)
                for k in range(3):
                    at_x = pl.multiple_of(((g * 2 + half) * 5 + k) * CELLS + c8 * 8, 8)
                    x = planes[pl.ds(at_x, 8), :] - 0.5
                    moment = cc * total(2 + k) + total(5 + k)
                    at_o = pl.multiple_of((g * 3 + k) * CELLS + c8 * 8, 8)
                    acc[pl.ds(at_o, 8), half * HB : (half + 1) * HB] = jnp.where(
                        cc > 0, (x * plain - moment) * FORCE_SCALE, 0.0
                    )
            return carry

        lax.fori_loop(0, CELLS // 8, sums, 0)

    out = pltpu.make_async_copy(acc, acc_hbm, in_sem.at[0])
    out.start()
    out.wait()
    settled.wait()


def planes_of(n):
    return jax.ShapeDtypeStruct((n * PLANE, HB), f32)


def call_density(counts, near_counts, local, side, remote, planes):
    return pl.pallas_call(
        density_kernel,
        out_shape=[
            planes_of(6),
            jax.ShapeDtypeStruct((LIST, HB, HB), f32),
            jax.ShapeDtypeStruct((2 * LIST + 8,), i32),
        ],
        in_specs=[HBM] * 6,
        out_specs=[HBM] * 3,
        scratch_shapes=[
            pltpu.SMEM((1, CELLS), i32),
            pltpu.SMEM((4, 1, CELLS), i32),
            pltpu.SMEM((PAIRS,), i32),
            pltpu.SMEM((PAIRS,), i32),
            pltpu.SMEM((PAIRS,), i32),
            pltpu.SMEM((2 * LIST + 8,), i32),
            pltpu.VMEM((PLANES, HB), f32),
            pltpu.VMEM((6 * PLANE, HB), f32),
            pltpu.VMEM((OWN, HB, FEAT), bf16),
            pltpu.VMEM((READ, FEAT, 2 * HB), bf16),
            pltpu.VMEM((OWN, HB, HB), f32),
            pltpu.VMEM((READ, HB), f32),
            pltpu.VMEM((OWN + 1, HB, HB), f32),
            pltpu.VMEM(((ALL + 1) * 8, HB), f32),
            pltpu.VMEM((U, HB, 2 * HB), f32),
            pltpu.VMEM((SLOTS, U, HB, HB), f32),
            pltpu.SemaphoreType.DMA((SLOTS, PARTS)),
            pltpu.SemaphoreType.DMA((6,)),
            pltpu.SemaphoreType.DMA((10,)),
        ],
        compiler_params=pltpu.CompilerParams(vmem_limit_bytes=60 << 20),
        name="density",
    )(counts, near_counts, local, side, remote, planes)


def call_force(items, counts, near_counts, side, remote, planes, coef, gbuf):
    return pl.pallas_call(
        force_kernel,
        out_shape=[jax.ShapeDtypeStruct((15 * CELLS, 2 * HB), f32), jax.ShapeDtypeStruct((CELLS, 2 * HB), f32)],
        in_specs=[HBM] * 8,
        out_specs=[HBM] * 2,
        scratch_shapes=[
            pltpu.SMEM((2 * LIST + 8,), i32),
            pltpu.SMEM((1, CELLS), i32),
            pltpu.SMEM((4, 1, CELLS), i32),
            pltpu.SMEM((PAIRS,), i32),
            pltpu.SMEM((PAIRS,), i32),
            pltpu.VMEM((PLANES, HB), f32),
            pltpu.VMEM((6 * PLANE, HB), f32),
            pltpu.VMEM((15 * CELLS, 2 * HB), f32),
            pltpu.VMEM((CELLS, 2 * HB), f32),
            pltpu.VMEM((READ, 16, HB), bf16),
            pltpu.VMEM(((OWN + 1) * 8, HB), f32),
            pltpu.VMEM(((ALL + 1) * 8, HB), f32),
            pltpu.VMEM((SLOTS, UF, HB, HB), f32),
            pltpu.SemaphoreType.DMA((SLOTS, PARTS)),
            pltpu.SemaphoreType.DMA((6,)),
            pltpu.SemaphoreType.DMA((10,)),
        ],
        compiler_params=pltpu.CompilerParams(vmem_limit_bytes=60 << 20),
        name="force",
    )(items, counts, near_counts, side, remote, planes, coef, gbuf)


def neighbours():
    i, j = lax.axis_index("gx"), lax.axis_index("yz")
    nx, ny = lax.axis_size("gx"), lax.axis_size("yz")
    return (
        (lax.rem(i + nx - 1, nx), j),
        (lax.rem(i + 1, nx), j),
        (i, lax.rem(j + ny - 1, ny)),
        (i, lax.rem(j + 1, ny)),
    )


def greet(devices):
    barrier = pltpu.get_barrier_semaphore()
    for device in devices:
        pl.semaphore_signal(barrier, inc=1, device_id=device, device_id_type=MESH)
    pl.semaphore_wait(barrier, 4)


def exchange(devices, source, target, send, recv):
    copies = []
    for s in (2, 3, 0, 1):
        copy = pltpu.make_async_remote_copy(
            src_ref=source(s),
            dst_ref=target(s ^ 1),
            send_sem=send.at[s],
            recv_sem=recv.at[s ^ 1],
            device_id=devices[s],
            device_id_type=MESH,
        )
        copy.start()
        copies.append(copy)
    return copies


def rows(ref, s, n):
    return ref.at[pl.ds(s * n, n), :]


def halo_kernel(positions, masses, smoothing, count, planes, near_count, own_sem, send, recv):
    devices = neighbours()
    fields = ((positions, 0, 3), (masses, 3, 1), (smoothing, 4, 1))

    def place(group, first, n):
        return planes.at[pl.ds((group * 5 + first) * CELLS, n * CELLS), :]

    keep = [
        pltpu.make_async_copy(x, place(0, first, n), own_sem.at[k]) for k, (x, first, n) in enumerate(fields)
    ]
    for copy in keep:
        copy.start()
    greet(devices)
    copies = []
    for k, (x, first, n) in enumerate(fields):
        copies += exchange(
            devices, lambda s: x, lambda s: place(s + 1, first, n), send.at[k], recv.at[k]
        )
    copies += exchange(devices, lambda s: count, lambda s: near_count.at[s], send.at[3], recv.at[3])
    for copy in copies + keep:
        copy.wait()


def plane_copies(source, target, sem):
    size = 5 * CELLS
    return [
        pltpu.make_async_copy(
            source.at[pl.ds(g * size, size), pl.ds(half * HB, HB)],
            target.at[pl.ds((2 * g + half) * size, size), :],
            sem.at[2 * g + half],
        )
        for g in range(5)
        for half in range(2)
    ]


def settle_kernel(dens, coef, mine, occ, cf, rho_out, back, in_sem, send, recv):
    devices = neighbours()
    inputs = [
        pltpu.make_async_copy(rows(dens, 0, PLANE), mine, in_sem.at[0]),
        pltpu.make_async_copy(rows(dens, 5, PLANE), occ, in_sem.at[1]),
    ]
    for copy in inputs:
        copy.start()
    greet(devices)
    copies = exchange(
        devices, lambda s: rows(dens, s + 1, PLANE), lambda s: rows(back, s, PLANE), send.at[0], recv.at[0]
    )
    for copy in inputs + copies:
        copy.wait()
    rho = mine[...]
    for s in range(4):
        rho = rho + back[s * PLANE : (s + 1) * PLANE, :]
    mask = occ[...]
    cf[...] = jnp.exp(jnp.log(jnp.where(mask > 0, rho, 1.0)) * (-1.0 / 3.0)) * mask
    copies = exchange(devices, lambda s: cf, lambda s: rows(coef, s + 1, PLANE), send.at[1], recv.at[1])
    rho_out[...] = rho * mask
    keep = [
        pltpu.make_async_copy(cf, rows(coef, 0, PLANE), in_sem.at[0]),
        pltpu.make_async_copy(rho_out, rows(coef, 5, PLANE), in_sem.at[1]),
    ]
    for copy in keep:
        copy.start()
    for copy in copies + keep:
        copy.wait()


def finish_kernel(acc, back, in_sem, send, recv):
    devices = neighbours()
    greet(devices)
    size = 3 * CELLS
    copies = exchange(
        devices, lambda s: rows(acc, s + 1, size), lambda s: rows(back, s, size), send.at[0], recv.at[0]
    )
    for copy in copies:
        copy.wait()


def remote_call(kernel, name, ident, operands, out_shape, out_specs, scratch, copies, phases):
    return pl.pallas_call(
        kernel,
        out_shape=out_shape,
        in_specs=[HBM] * len(operands),
        out_specs=out_specs,
        scratch_shapes=[pltpu.VMEM(shape, f32) for shape in scratch]
        + [pltpu.SemaphoreType.DMA((copies,))]
        + [pltpu.SemaphoreType.DMA((phases, 4))] * 2,
        compiler_params=pltpu.CompilerParams(collective_id=ident, has_side_effects=True, vmem_limit_bytes=60 << 20),
        name=name,
    )(*operands)


def body(positions, masses, smoothing, counts, pair_local, pair_side, pair_remote):
    count = counts.reshape(1, CELLS)
    local, side, remote = (x.reshape(PAIRS) for x in (pair_local, pair_side, pair_remote))
    slots = 2 * HB
    fields = (positions[0, 0].transpose(1, 0, 2).reshape(3 * CELLS, slots), masses[0, 0], smoothing[0, 0])
    planes, near_count = remote_call(
        halo_kernel, "halo", 0, fields + (count,),
        [jax.ShapeDtypeStruct((25 * CELLS, slots), f32), jax.ShapeDtypeStruct((4, 1, CELLS), i32)], [HBM] * 2,
        [], 3, 4,
    )
    dens, gbuf, items = call_density(count, near_count, local, side, remote, planes)
    coef = remote_call(
        settle_kernel, "settle", 1, (dens,), planes_of(6), HBM,
        [(PLANE, HB)] * 4 + [(4 * PLANE, HB)], 2, 2,
    )
    acc, rho = call_force(items, count, near_count, side, remote, planes, coef, gbuf)
    back = remote_call(
        finish_kernel, "finish", 2, (acc,), jax.ShapeDtypeStruct((12 * CELLS, slots), f32), HBM, [], 1, 1
    )
    total = acc[: 3 * CELLS]
    for s in range(4):
        total = total + back[3 * s * CELLS : 3 * (s + 1) * CELLS]
    return rho[None, None], total.reshape(3, CELLS, slots).transpose(1, 0, 2)[None, None]


def solution(mesh):
    in_specs = (
        P("gx", "yz", None, None, None),
        P("gx", "yz", None, None),
        P("gx", "yz", None, None),
        P("gx", "yz", None),
        P("gx", "yz", None),
        P("gx", "yz", None),
        P("gx", "yz", None),
    )
    out_specs = (P("gx", "yz", None, None), P("gx", "yz", None, None, None))
    return jax.shard_map(body, mesh=mesh, in_specs=in_specs, out_specs=out_specs, check_vma=False)
```

```python
import math

import jax
import jax.numpy as jnp
from jax import lax
from jax.experimental import pallas as pl
from jax.experimental.pallas import tpu as pltpu
from jax.sharding import PartitionSpec as P

f32, bf16, i32 = jnp.float32, jnp.bfloat16, jnp.int32
HB = 128
CELLS = 64
PAIRS = 128
OWN = 2 * CELLS
ALL = 10 * CELLS
READ = 2 * (CELLS + PAIRS)
FEAT = 48
U = 16
PARTS = 4
SLOTS = 3
UNROLL = 4
PLANE = 2 * CELLS
PLANES = 25 * PLANE
UF = 3 * U
FRONT = U
ITEMS = 4 * PAIRS + 3 * CELLS
LIST = FRONT + ITEMS + (SLOTS + 3) * U
DENSITY_SCALE = 21.0 * 8.0 / (16.0 * math.pi)
FORCE_SCALE = 105.0 * 32.0 / (16.0 * math.pi)
SMEM = pl.BlockSpec(memory_space=pltpu.SMEM)
VMEM = pl.BlockSpec(memory_space=pltpu.VMEM)
HBM = pl.BlockSpec(memory_space=pl.ANY)
MESH = pl.DeviceIdType.MESH


def nn(a, b):
    return lax.dot_general(a, b, (((1,), (0,)), ((), ())), preferred_element_type=f32)


def nt(a, b):
    return lax.dot_general(a, b, (((1,), (1,)), ((), ())), preferred_element_type=f32)


def pieces(t):
    one = t.astype(bf16).astype(f32)
    rest = t - one
    two = rest.astype(bf16).astype(f32)
    return one, two, rest - two


def cell_tile(planes, base, cell, half):
    return planes[pl.ds(base + half * 5 * CELLS + cell, 5, stride=CELLS), :]


def masked(mass, count, half):
    slot = lax.broadcasted_iota(i32, mass.shape, 1) + half * HB
    return jnp.where(slot < count, mass, 0.0)


def masked_tile(planes, base, cell, half, count):
    tile = cell_tile(planes, base, cell, half)
    mass = masked(tile[3:4, :], count, half)
    return jnp.concatenate([tile[0:3, :], mass, tile[4:5, :], jnp.zeros((3, HB), f32)], axis=0)


def row_masks():
    row = lax.broadcasted_iota(i32, (8, HB), 0)
    return row, [(row == k).astype(f32) for k in range(8)]


def lane_features(tile, row, at):
    x = jnp.where(row < 3, tile - 0.5, 0.0)
    norm = jnp.sum(x * x, axis=0, keepdims=True)
    h = tile[4:5, :]
    dist = x + at[3] + at[4] * norm
    supp = at[5] + at[6] * h
    d1, d2, d3 = pieces(dist)
    s1, s2, s3 = pieces(supp)
    d12 = jnp.concatenate([d1, d2], axis=0).astype(bf16)
    d31 = jnp.concatenate([d3, d1], axis=0).astype(bf16)
    s12 = jnp.concatenate([s1, s2], axis=0).astype(bf16)
    s31 = jnp.concatenate([s3, s1], axis=0).astype(bf16)
    left = jnp.concatenate([d12, d12, d31], axis=0)
    right = jnp.concatenate([s12, s12, s31], axis=0)
    return jnp.concatenate([left, right], axis=1)


def row_features(tile, row, at):
    x = jnp.where(row < 3, tile - 0.5, 0.0)
    norm = jnp.sum(x * x, axis=0, keepdims=True)
    h = tile[4:5, :]
    form = -2.0 * x + at[3] * norm + at[4] + at[5] * h + at[6]
    p1, p2, p3 = pieces(form)
    rest = jnp.zeros((HB - FEAT - 8, HB), f32)
    m1, m2, m3 = pieces(at[0] * tile[3:4, :])
    masses = m1 + pltpu.roll(m2, 1, 0) + pltpu.roll(m3, 2, 0)
    rest = jnp.zeros((64 - FEAT - 8, HB), f32)
    turned = jnp.concatenate([p1, p1, p2, p2, p1, p3, masses, rest], axis=0).T.astype(bf16)
    k = lax.broadcasted_iota(i32, (64, HB), 0)
    pick = ((k >= FEAT) & (k < FEAT + 3)).astype(f32).astype(bf16)
    return turned[:, :FEAT], nn(turned, pick)


def two_pieces(tile):
    one = tile.astype(bf16).astype(f32)
    return jnp.concatenate([one, tile - one], axis=0).astype(bf16)


def fold(o):
    o = o[:, :HB] + o[:, HB:]
    return o[:8] + o[8:]


def partner_sums(va, vb, hi, lo):
    to_lane = fold(nn(va, jnp.concatenate([hi, lo], axis=1)))
    to_row = fold(nn(vb, jnp.concatenate([hi.T, lo.T], axis=1)))
    return to_row, to_lane


def split(g):
    hi = g.astype(bf16)
    return hi, (g - hi.astype(f32)).astype(bf16)


def batch_copies(buffer, gs, sem, slot, first, size, out):
    part = size // PARTS
    copies = []
    for k in range(PARTS):
        here = gs.at[slot, pl.ds(k * part, part)]
        there = buffer.at[pl.ds(first + k * part, part)]
        pair = (here, there) if out else (there, here)
        copies.append(pltpu.make_async_copy(*pair, sem.at[slot, k]))
    return copies


def density_kernel(
    counts_hbm, near_counts_hbm, local_hbm, side_hbm, remote_hbm, planes_hbm,
    dens_hbm, gbuf, items_hbm,
    counts, near_counts, local, side, remote, items, planes, dens,
    rowf, lanef, massc, massr, accr, accl, dist, gs, sem, in_sem,
):
    sources = (counts_hbm, near_counts_hbm, local_hbm, side_hbm, remote_hbm, planes_hbm)
    targets = (counts, near_counts, local, side, remote, planes)
    inputs = [pltpu.make_async_copy(x, y, in_sem.at[k]) for k, (x, y) in enumerate(zip(sources, targets))]
    for copy in inputs:
        copy.start()
    for copy in inputs[:5]:
        copy.wait()
    row, at = row_masks()

    accr[...] = jnp.zeros_like(accr)
    accl[...] = jnp.zeros_like(accl)
    dist[...] = jnp.ones_like(dist)

    def build(tile, block):
        lanef[block] = lane_features(tile, row, at)
        massr[pl.ds(block, 1), :] = tile[3:4, :]

    def dummy(i, carry):
        items[i] = 0
        items[LIST + i] = OWN + ALL * 1024
        return carry

    lax.fori_loop(0, FRONT, dummy, 0)

    def put(pos, a, b, da, db):
        items[pos] = a + b * 1024
        items[LIST + pos] = da + db * 1024

    def pair_items(step, pos):
        for j in range(UNROLL):
            k = step * UNROLL + j
            for half in range(2):
                count = near_counts[side[k], 0, remote[k]]
                tile = masked_tile(planes, (side[k] + 1) * 5 * PLANE, remote[k], half, count)
                build(tile, OWN + 2 * k + half)
            a = local[k]
            two_a = (counts[0, a] > HB).astype(i32)
            two_b = (near_counts[side[k], 0, remote[k]] > HB).astype(i32)
            a0, b0 = 2 * a, OWN + 2 * k
            d0 = 2 * (side[k] * CELLS + remote[k] + CELLS)
            put(pos, a0, b0, a0, d0)
            pos = pos + 1
            put(pos, a0, b0 + 1, a0, d0 + 1)
            pos = pos + two_b
            put(pos, a0 + 1, b0, a0 + 1, d0)
            pos = pos + two_a
            put(pos, a0 + 1, b0 + 1, a0 + 1, d0 + 1)
            pos = pos + two_a * two_b
        return pos

    def self_items(step, pos):
        for j in range(UNROLL):
            a = step * UNROLL + j
            for half in range(2):
                tile = masked_tile(planes, 0, a, half, counts[0, a])
                build(tile, 2 * a + half)
                rowf[2 * a + half], massc[2 * a + half] = row_features(tile, row, at)
                occ = masked(jnp.ones((1, HB), f32), counts[0, a], half)
                dens[pl.ds(5 * PLANE + half * CELLS + a, 1), :] = occ
            two = (counts[0, a] > HB).astype(i32)
            a0 = 2 * a
            put(pos, a0, a0, OWN, a0)
            pos = pos + 1
            put(pos, a0, a0 + 1, a0, a0 + 1)
            pos = pos + two
            put(pos, a0 + 1, a0 + 1, OWN, a0 + 1)
            pos = pos + two
        return pos

    inputs[5].wait()
    pos = lax.fori_loop(0, CELLS // UNROLL, self_items, FRONT)
    pos = lax.fori_loop(0, PAIRS // UNROLL, pair_items, pos)
    lax.fori_loop(pos, pos + (SLOTS + 2) * U, dummy, 0)
    items[2 * LIST] = pos
    listed = pltpu.make_async_copy(items, items_hbm, in_sem.at[0])
    listed.start()

    def save(slot, batch):
        return batch_copies(gbuf, gs, sem, slot, batch * U, U, True)

    for slot in range(SLOTS):
        for copy in save(slot, LIST // U - SLOTS + slot):
            copy.start()

    def step(i, carry):
        slot = lax.rem(i, SLOTS)
        for copy in save(slot, i):
            copy.wait()
        for u in range(U):
            s = items[i * U + u]
            d = items[LIST + i * U + u]
            a, ra = s & 1023, d & 1023
            mq = massr[pl.ds(s >> 10, 1), :]
            down = jnp.zeros((8, HB), f32)
            for c in range(0, HB, 32):
                r2 = jnp.maximum(dist[u, c : c + 32, :HB], 1e-12)
                h2 = dist[u, c : c + 32, HB:]
                r = r2 * lax.rsqrt(r2)
                q = 1.0 / h2
                q2 = q * q
                y = jnp.maximum(q - r * q2, 0.0)
                y2 = y * y
                gs[slot, u, c : c + 32, :] = (y2 * y) * q2
                w = (y2 * y2) * (h2 + 4.0 * r)
                accr[ra, c : c + 32, :] += w * mq
                wm = w * massc[a, c : c + 32, :]
                down = down + ((wm[:8] + wm[8:16]) + (wm[16:24] + wm[24:]))
            l0 = pl.multiple_of((d >> 10) * 8, 8)
            accl[pl.ds(l0, 8), :] += down
        for copy in save(slot, i):
            copy.start()
        for u in range(U):
            s = items[(i + 1) * U + u]
            dist[u] = nn(rowf[s & 1023], lanef[s >> 10])
        return carry

    batches = (pos - FRONT + U - 1) // U
    lax.fori_loop(0, batches + 1, step, 0)

    row16 = lax.broadcasted_iota(i32, (16, HB), 0)
    for half in range(2):

        def own_sums(c8, carry):
            first = (2 * c8 * 8 + half) * 8
            total = jnp.zeros((16, 2 * HB), f32)
            for j in range(8):
                hi, lo = split(accr[2 * (c8 * 8 + j) + half])
                pick = (row16 == j).astype(bf16)
                total = total + nt(pick, jnp.concatenate([hi, lo], axis=0))
            rows8 = total[:8, :HB] + total[:8, HB:]
            for k in range(8):
                rows8 = rows8 + accl[pl.ds(first + k, 8, stride=16), :]
            to = pl.multiple_of(half * CELLS + c8 * 8, 8)
            dens[pl.ds(to, 8), :] = rows8 * DENSITY_SCALE
            return carry

        for c8 in range(CELLS // 8):
            own_sums(c8, 0)

        def near_sums(c8, carry):
            for g in range(1, 5):
                first = (2 * (g * CELLS + c8 * 8) + half) * 8
                rows8 = accl[pl.ds(first, 8, stride=16), :]
                for k in range(1, 8):
                    rows8 = rows8 + accl[pl.ds(first + k, 8, stride=16), :]
                to = pl.multiple_of(g * PLANE + half * CELLS + c8 * 8, 8)
                dens[pl.ds(to, 8), :] = rows8 * DENSITY_SCALE
            return carry

        lax.fori_loop(0, CELLS // 8, near_sums, 0)

    out = pltpu.make_async_copy(dens, dens_hbm, in_sem.at[1])
    out.start()
    listed.wait()
    for slot in range(SLOTS):
        for copy in save(slot, 0):
            copy.wait()
    out.wait()


def force_kernel(
    items_hbm, counts_hbm, near_counts_hbm, side_hbm, remote_hbm, planes_hbm, coef_hbm, gbuf,
    acc_hbm, rho_hbm,
    items, counts, near_counts, side, remote, planes, coef, acc, rho,
    vmat, accr, accl, gs, sem, in_sem,
):
    sources = (items_hbm, counts_hbm, near_counts_hbm, side_hbm, remote_hbm, planes_hbm, coef_hbm)
    targets = (items, counts, near_counts, side, remote, planes, coef)
    inputs = [pltpu.make_async_copy(x, y, in_sem.at[k]) for k, (x, y) in enumerate(zip(sources, targets))]
    for copy in inputs:
        copy.start()

    def load(slot, batch):
        return batch_copies(gbuf, gs, sem, slot, FRONT + batch * UF, UF, False)

    for copy in inputs:
        copy.wait()
    batches = (items[2 * LIST] - FRONT + UF - 1) // UF
    for slot in range(SLOTS - 1):
        for copy in load(slot, slot):
            copy.start()

    for half in range(2):
        at_r = 5 * PLANE + half * CELLS
        rho[:, half * HB : (half + 1) * HB] = coef[at_r : at_r + CELLS, :]
    settled = pltpu.make_async_copy(rho, rho_hbm, in_sem.at[1])
    settled.start()

    accr[...] = jnp.zeros_like(accr)
    accl[...] = jnp.zeros_like(accl)

    def build(group, c, count, block):
        for half in range(2):
            tile = cell_tile(planes, group * 5 * PLANE, c, half)
            cc = coef[pl.ds(group * PLANE + half * CELLS + c, 1), :]
            m = masked(tile[3:4, :], count, half)
            mc = m * cc
            x = tile[0:3, :] - 0.5
            stack = jnp.concatenate([m, mc, m * x, mc * x], axis=0)
            vmat[block + half] = two_pieces(stack)

    def own_cells(step, carry):
        for j in range(UNROLL):
            c = step * UNROLL + j
            build(0, c, counts[0, c], 2 * c)
        return carry

    lax.fori_loop(0, CELLS // UNROLL, own_cells, 0)

    def near_cells(step, carry):
        for j in range(UNROLL):
            k = step * UNROLL + j
            build(side[k] + 1, remote[k], near_counts[side[k], 0, remote[k]], OWN + 2 * k)
        return carry

    lax.fori_loop(0, PAIRS // UNROLL, near_cells, 0)

    def step(i, carry):
        slot = lax.rem(i, SLOTS)

        @pl.when(i + SLOTS - 1 < batches)
        def _():
            for copy in load(lax.rem(i + SLOTS - 1, SLOTS), i + SLOTS - 1):
                copy.start()

        for copy in load(slot, i):
            copy.wait()
        for u in range(UF):
            s = items[FRONT + i * UF + u]
            d = items[LIST + FRONT + i * UF + u]
            hi, lo = split(gs[slot, u])
            to_row, to_lane = partner_sums(vmat[s & 1023], vmat[s >> 10], hi, lo)
            r0 = pl.multiple_of((d & 1023) * 8, 8)
            l0 = pl.multiple_of((d >> 10) * 8, 8)
            accr[pl.ds(r0, 8), :] += to_row
            accl[pl.ds(l0, 8), :] += to_lane
        return carry

    lax.fori_loop(0, batches, step, 0)

    for half in range(2):

        def sums(c8, carry):
            for g in range(5):
                first = (2 * (g * CELLS + c8 * 8) + half) * 8

                def total(k):
                    t = accl[pl.ds(first + k, 8, stride=16), :]
                    if g == 0:
                        t = t + accr[pl.ds(first + k, 8, stride=16), :]
                    return t

                cc = coef[pl.ds(pl.multiple_of(g * PLANE + half * CELLS + c8 * 8, 8), 8), :]
                plain = cc * total(0) + total(1)
                for k in range(3):
                    at_x = pl.multiple_of(((g * 2 + half) * 5 + k) * CELLS + c8 * 8, 8)
                    x = planes[pl.ds(at_x, 8), :] - 0.5
                    moment = cc * total(2 + k) + total(5 + k)
                    at_o = pl.multiple_of((g * 3 + k) * CELLS + c8 * 8, 8)
                    acc[pl.ds(at_o, 8), half * HB : (half + 1) * HB] = jnp.where(
                        cc > 0, (x * plain - moment) * FORCE_SCALE, 0.0
                    )
            return carry

        lax.fori_loop(0, CELLS // 8, sums, 0)

    out = pltpu.make_async_copy(acc, acc_hbm, in_sem.at[0])
    out.start()
    out.wait()
    settled.wait()


def planes_of(n):
    return jax.ShapeDtypeStruct((n * PLANE, HB), f32)


def call_density(counts, near_counts, local, side, remote, planes):
    return pl.pallas_call(
        density_kernel,
        out_shape=[
            planes_of(6),
            jax.ShapeDtypeStruct((LIST, HB, HB), f32),
            jax.ShapeDtypeStruct((2 * LIST + 8,), i32),
        ],
        in_specs=[HBM] * 6,
        out_specs=[HBM] * 3,
        scratch_shapes=[
            pltpu.SMEM((1, CELLS), i32),
            pltpu.SMEM((4, 1, CELLS), i32),
            pltpu.SMEM((PAIRS,), i32),
            pltpu.SMEM((PAIRS,), i32),
            pltpu.SMEM((PAIRS,), i32),
            pltpu.SMEM((2 * LIST + 8,), i32),
            pltpu.VMEM((PLANES, HB), f32),
            pltpu.VMEM((6 * PLANE, HB), f32),
            pltpu.VMEM((OWN, HB, FEAT), bf16),
            pltpu.VMEM((READ, FEAT, 2 * HB), bf16),
            pltpu.VMEM((OWN, HB, HB), f32),
            pltpu.VMEM((READ, HB), f32),
            pltpu.VMEM((OWN + 1, HB, HB), f32),
            pltpu.VMEM(((ALL + 1) * 8, HB), f32),
            pltpu.VMEM((U, HB, 2 * HB), f32),
            pltpu.VMEM((SLOTS, U, HB, HB), f32),
            pltpu.SemaphoreType.DMA((SLOTS, PARTS)),
            pltpu.SemaphoreType.DMA((6,)),
        ],
        compiler_params=pltpu.CompilerParams(vmem_limit_bytes=60 << 20),
        name="density",
    )(counts, near_counts, local, side, remote, planes)


def call_force(items, counts, near_counts, side, remote, planes, coef, gbuf):
    return pl.pallas_call(
        force_kernel,
        out_shape=[jax.ShapeDtypeStruct((15 * CELLS, 2 * HB), f32), jax.ShapeDtypeStruct((CELLS, 2 * HB), f32)],
        in_specs=[HBM] * 8,
        out_specs=[HBM] * 2,
        scratch_shapes=[
            pltpu.SMEM((2 * LIST + 8,), i32),
            pltpu.SMEM((1, CELLS), i32),
            pltpu.SMEM((4, 1, CELLS), i32),
            pltpu.SMEM((PAIRS,), i32),
            pltpu.SMEM((PAIRS,), i32),
            pltpu.VMEM((PLANES, HB), f32),
            pltpu.VMEM((6 * PLANE, HB), f32),
            pltpu.VMEM((15 * CELLS, 2 * HB), f32),
            pltpu.VMEM((CELLS, 2 * HB), f32),
            pltpu.VMEM((READ, 16, HB), bf16),
            pltpu.VMEM(((OWN + 1) * 8, HB), f32),
            pltpu.VMEM(((ALL + 1) * 8, HB), f32),
            pltpu.VMEM((SLOTS, UF, HB, HB), f32),
            pltpu.SemaphoreType.DMA((SLOTS, PARTS)),
            pltpu.SemaphoreType.DMA((7,)),
        ],
        compiler_params=pltpu.CompilerParams(vmem_limit_bytes=60 << 20),
        name="force",
    )(items, counts, near_counts, side, remote, planes, coef, gbuf)


def neighbours():
    i, j = lax.axis_index("gx"), lax.axis_index("yz")
    nx, ny = lax.axis_size("gx"), lax.axis_size("yz")
    return (
        (lax.rem(i + nx - 1, nx), j),
        (lax.rem(i + 1, nx), j),
        (i, lax.rem(j + ny - 1, ny)),
        (i, lax.rem(j + 1, ny)),
    )


def greet(devices):
    barrier = pltpu.get_barrier_semaphore()
    for device in devices:
        pl.semaphore_signal(barrier, inc=1, device_id=device, device_id_type=MESH)
    pl.semaphore_wait(barrier, 4)


def exchange(devices, source, target, send, recv):
    copies = []
    for s in (2, 3, 0, 1):
        copy = pltpu.make_async_remote_copy(
            src_ref=source(s),
            dst_ref=target(s ^ 1),
            send_sem=send.at[s],
            recv_sem=recv.at[s ^ 1],
            device_id=devices[s],
            device_id_type=MESH,
        )
        copy.start()
        copies.append(copy)
    return copies


def rows(ref, s, n):
    return ref.at[pl.ds(s * n, n), :]


def halo_kernel(
    positions, masses, smoothing, count,
    planes, near_count,
    pos, mass, smooth, own, in_sem, send, recv,
):
    devices = neighbours()
    sources, targets = (positions, masses, smoothing), (pos, mass, smooth)
    inputs = [pltpu.make_async_copy(x, y, in_sem.at[k]) for k, (x, y) in enumerate(zip(sources, targets))]
    for copy in inputs:
        copy.start()
    greet(devices)
    copies = exchange(devices, lambda s: count, lambda s: near_count.at[s], send.at[1], recv.at[1])
    for copy in inputs:
        copy.wait()
    for half in range(2):
        lanes = slice(half * HB, (half + 1) * HB)
        base = half * 5 * CELLS
        for k in range(3):
            own[base + k * CELLS : base + (k + 1) * CELLS, :] = pos[k, :, lanes]
        own[base + 3 * CELLS : base + 4 * CELLS, :] = mass[:, lanes]
        own[base + 4 * CELLS : base + 5 * CELLS, :] = smooth[:, lanes]
    copies += exchange(
        devices, lambda s: own, lambda s: rows(planes, s + 1, 5 * PLANE), send.at[0], recv.at[0]
    )
    keep = pltpu.make_async_copy(own, rows(planes, 0, 5 * PLANE), in_sem.at[3])
    keep.start()
    for copy in copies:
        copy.wait()
    keep.wait()


def settle_kernel(dens, coef, mine, occ, cf, rho_out, back, in_sem, send, recv):
    devices = neighbours()
    inputs = [
        pltpu.make_async_copy(rows(dens, 0, PLANE), mine, in_sem.at[0]),
        pltpu.make_async_copy(rows(dens, 5, PLANE), occ, in_sem.at[1]),
    ]
    for copy in inputs:
        copy.start()
    greet(devices)
    copies = exchange(
        devices, lambda s: rows(dens, s + 1, PLANE), lambda s: rows(back, s, PLANE), send.at[0], recv.at[0]
    )
    for copy in inputs + copies:
        copy.wait()
    rho = mine[...]
    for s in range(4):
        rho = rho + back[s * PLANE : (s + 1) * PLANE, :]
    mask = occ[...]
    cf[...] = jnp.exp(jnp.log(jnp.where(mask > 0, rho, 1.0)) * (-1.0 / 3.0)) * mask
    copies = exchange(devices, lambda s: cf, lambda s: rows(coef, s + 1, PLANE), send.at[1], recv.at[1])
    rho_out[...] = rho * mask
    keep = [
        pltpu.make_async_copy(cf, rows(coef, 0, PLANE), in_sem.at[0]),
        pltpu.make_async_copy(rho_out, rows(coef, 5, PLANE), in_sem.at[1]),
    ]
    for copy in keep:
        copy.start()
    for copy in copies + keep:
        copy.wait()


def finish_kernel(acc, back, in_sem, send, recv):
    devices = neighbours()
    greet(devices)
    size = 3 * CELLS
    copies = exchange(
        devices, lambda s: rows(acc, s + 1, size), lambda s: rows(back, s, size), send.at[0], recv.at[0]
    )
    for copy in copies:
        copy.wait()


def remote_call(kernel, name, ident, operands, out_shape, out_specs, scratch, copies, phases):
    return pl.pallas_call(
        kernel,
        out_shape=out_shape,
        in_specs=[HBM] * len(operands),
        out_specs=out_specs,
        scratch_shapes=[pltpu.VMEM(shape, f32) for shape in scratch]
        + [pltpu.SemaphoreType.DMA((copies,))]
        + [pltpu.SemaphoreType.DMA((phases, 4))] * 2,
        compiler_params=pltpu.CompilerParams(collective_id=ident, has_side_effects=True, vmem_limit_bytes=60 << 20),
        name=name,
    )(*operands)


def body(positions, masses, smoothing, counts, pair_local, pair_side, pair_remote):
    count = counts.reshape(1, CELLS)
    local, side, remote = (x.reshape(PAIRS) for x in (pair_local, pair_side, pair_remote))
    slots = 2 * HB
    planes, near_count = remote_call(
        halo_kernel, "halo", 0, (positions[0, 0].transpose(1, 0, 2), masses[0, 0], smoothing[0, 0], count),
        [planes_of(25), jax.ShapeDtypeStruct((4, 1, CELLS), i32)], [HBM] * 2,
        [(3, CELLS, slots), (CELLS, slots), (CELLS, slots), (5 * PLANE, HB)], 4, 2,
    )
    dens, gbuf, items = call_density(count, near_count, local, side, remote, planes)
    coef = remote_call(
        settle_kernel, "settle", 1, (dens,), planes_of(6), HBM,
        [(PLANE, HB)] * 4 + [(4 * PLANE, HB)], 2, 2,
    )
    acc, rho = call_force(items, count, near_count, side, remote, planes, coef, gbuf)
    back = remote_call(
        finish_kernel, "finish", 2, (acc,), jax.ShapeDtypeStruct((12 * CELLS, slots), f32), HBM, [], 1, 1
    )
    total = acc[: 3 * CELLS]
    for s in range(4):
        total = total + back[3 * s * CELLS : 3 * (s + 1) * CELLS]
    return rho[None, None], total.reshape(3, CELLS, slots).transpose(1, 0, 2)[None, None]


def solution(mesh):
    in_specs = (
        P("gx", "yz", None, None, None),
        P("gx", "yz", None, None),
        P("gx", "yz", None, None),
        P("gx", "yz", None),
        P("gx", "yz", None),
        P("gx", "yz", None),
        P("gx", "yz", None),
    )
    out_specs = (P("gx", "yz", None, None), P("gx", "yz", None, None, None))
    return jax.shard_map(body, mesh=mesh, in_specs=in_specs, out_specs=out_specs, check_vma=False)
```

```python
import math

import jax
import jax.numpy as jnp
from jax import lax
from jax.experimental import pallas as pl
from jax.experimental.pallas import tpu as pltpu
from jax.sharding import PartitionSpec as P

f32, bf16, i32 = jnp.float32, jnp.bfloat16, jnp.int32
HB = 128
CELLS = 64
PAIRS = 128
OWN = 2 * CELLS
ALL = 10 * CELLS
READ = 2 * (CELLS + PAIRS)
FEAT = 48
U = 16
PARTS = 2
SLOTS = 3
UNROLL = 8
PLANE = 2 * CELLS
PLANES = 25 * PLANE
UF = 3 * U
FRONT = U
ITEMS = 4 * PAIRS + 3 * CELLS
LIST = FRONT + ITEMS + (SLOTS + 3) * U
DENSITY_SCALE = 21.0 * 8.0 / (16.0 * math.pi)
FORCE_SCALE = 105.0 * 32.0 / (16.0 * math.pi)
SMEM = pl.BlockSpec(memory_space=pltpu.SMEM)
VMEM = pl.BlockSpec(memory_space=pltpu.VMEM)
HBM = pl.BlockSpec(memory_space=pl.ANY)
MESH = pl.DeviceIdType.MESH


def nn(a, b):
    return lax.dot_general(a, b, (((1,), (0,)), ((), ())), preferred_element_type=f32)


def nt(a, b):
    return lax.dot_general(a, b, (((1,), (1,)), ((), ())), preferred_element_type=f32)


def pieces(t):
    one = t.astype(bf16).astype(f32)
    rest = t - one
    two = rest.astype(bf16).astype(f32)
    return one, two, rest - two


def cell_tile(planes, base, cell, half):
    return planes[pl.ds(base + half * 5 * CELLS + cell, 5, stride=CELLS), :]


def masked(mass, count, half):
    slot = lax.broadcasted_iota(i32, mass.shape, 1) + half * HB
    return jnp.where(slot < count, mass, 0.0)


def masked_tile(planes, base, cell, half, count):
    tile = cell_tile(planes, base, cell, half)
    mass = masked(tile[3:4, :], count, half)
    return jnp.concatenate([tile[0:3, :], mass, tile[4:5, :], jnp.zeros((3, HB), f32)], axis=0)


def row_masks():
    row = lax.broadcasted_iota(i32, (8, HB), 0)
    return row, [(row == k).astype(f32) for k in range(8)]


def lane_features(tile, row, at):
    x = jnp.where(row < 3, tile - 0.5, 0.0)
    norm = jnp.sum(x * x, axis=0, keepdims=True)
    h = tile[4:5, :]
    dist = x + at[3] + at[4] * norm
    supp = at[5] + at[6] * h
    d1, d2, d3 = pieces(dist)
    s1, s2, s3 = pieces(supp)
    d12 = jnp.concatenate([d1, d2], axis=0).astype(bf16)
    d31 = jnp.concatenate([d3, d1], axis=0).astype(bf16)
    s12 = jnp.concatenate([s1, s2], axis=0).astype(bf16)
    s31 = jnp.concatenate([s3, s1], axis=0).astype(bf16)
    left = jnp.concatenate([d12, d12, d31], axis=0)
    right = jnp.concatenate([s12, s12, s31], axis=0)
    return jnp.concatenate([left, right], axis=1)


def row_features(tile, row, at):
    x = jnp.where(row < 3, tile - 0.5, 0.0)
    norm = jnp.sum(x * x, axis=0, keepdims=True)
    h = tile[4:5, :]
    form = -2.0 * x + at[3] * norm + at[4] + at[5] * h + at[6]
    p1, p2, p3 = pieces(form)
    rest = jnp.zeros((HB - FEAT - 8, HB), f32)
    m1, m2, m3 = pieces(at[0] * tile[3:4, :])
    masses = m1 + pltpu.roll(m2, 1, 0) + pltpu.roll(m3, 2, 0)
    rest = jnp.zeros((64 - FEAT - 8, HB), f32)
    turned = jnp.concatenate([p1, p1, p2, p2, p1, p3, masses, rest], axis=0).T.astype(bf16)
    k = lax.broadcasted_iota(i32, (64, HB), 0)
    pick = ((k >= FEAT) & (k < FEAT + 3)).astype(f32).astype(bf16)
    return turned[:, :FEAT], nn(turned, pick)


def two_pieces(tile):
    one = tile.astype(bf16).astype(f32)
    return jnp.concatenate([one, tile - one], axis=0).astype(bf16)


def fold(o):
    o = o[:, :HB] + o[:, HB:]
    return o[:8] + o[8:]


def partner_sums(va, vb, hi, lo):
    to_lane = fold(nn(va, jnp.concatenate([hi, lo], axis=1)))
    to_row = fold(nn(vb, jnp.concatenate([hi.T, lo.T], axis=1)))
    return to_row, to_lane


def split(g):
    hi = g.astype(bf16)
    return hi, (g - hi.astype(f32)).astype(bf16)


def batch_copies(buffer, gs, sem, slot, first, size, out):
    part = size // PARTS
    copies = []
    for k in range(PARTS):
        here = gs.at[slot, pl.ds(k * part, part)]
        there = buffer.at[pl.ds(first + k * part, part)]
        pair = (here, there) if out else (there, here)
        copies.append(pltpu.make_async_copy(*pair, sem.at[slot, k]))
    return copies


def density_kernel(
    counts_hbm, near_counts_hbm, local_hbm, side_hbm, remote_hbm, planes_hbm,
    dens_hbm, gbuf, items_hbm,
    counts, near_counts, local, side, remote, items, planes, dens,
    rowf, lanef, massc, massr, accr, accl, dist, gs, sem, in_sem,
):
    sources = (counts_hbm, near_counts_hbm, local_hbm, side_hbm, remote_hbm, planes_hbm)
    targets = (counts, near_counts, local, side, remote, planes)
    inputs = [pltpu.make_async_copy(x, y, in_sem.at[k]) for k, (x, y) in enumerate(zip(sources, targets))]
    for copy in inputs:
        copy.start()
    for copy in inputs[:5]:
        copy.wait()
    row, at = row_masks()

    accr[...] = jnp.zeros_like(accr)
    accl[...] = jnp.zeros_like(accl)
    dist[...] = jnp.ones_like(dist)

    def build(tile, block):
        lanef[block] = lane_features(tile, row, at)
        massr[pl.ds(block, 1), :] = tile[3:4, :]

    def dummy(i, carry):
        items[i] = 0
        items[LIST + i] = OWN + ALL * 1024
        return carry

    lax.fori_loop(0, FRONT, dummy, 0)

    def put(pos, a, b, da, db):
        items[pos] = a + b * 1024
        items[LIST + pos] = da + db * 1024

    def pair_items(step, pos):
        for j in range(UNROLL):
            k = step * UNROLL + j
            for half in range(2):
                count = near_counts[side[k], 0, remote[k]]
                tile = masked_tile(planes, (side[k] + 1) * 5 * PLANE, remote[k], half, count)
                build(tile, OWN + 2 * k + half)
            a = local[k]
            two_a = (counts[0, a] > HB).astype(i32)
            two_b = (near_counts[side[k], 0, remote[k]] > HB).astype(i32)
            a0, b0 = 2 * a, OWN + 2 * k
            d0 = 2 * (side[k] * CELLS + remote[k] + CELLS)
            put(pos, a0, b0, a0, d0)
            pos = pos + 1
            put(pos, a0, b0 + 1, a0, d0 + 1)
            pos = pos + two_b
            put(pos, a0 + 1, b0, a0 + 1, d0)
            pos = pos + two_a
            put(pos, a0 + 1, b0 + 1, a0 + 1, d0 + 1)
            pos = pos + two_a * two_b
        return pos

    def self_items(step, pos):
        for j in range(UNROLL):
            a = step * UNROLL + j
            for half in range(2):
                tile = masked_tile(planes, 0, a, half, counts[0, a])
                build(tile, 2 * a + half)
                rowf[2 * a + half], massc[2 * a + half] = row_features(tile, row, at)
                occ = masked(jnp.ones((1, HB), f32), counts[0, a], half)
                dens[pl.ds(5 * PLANE + half * CELLS + a, 1), :] = occ
            two = (counts[0, a] > HB).astype(i32)
            a0 = 2 * a
            put(pos, a0, a0, OWN, a0)
            pos = pos + 1
            put(pos, a0, a0 + 1, a0, a0 + 1)
            pos = pos + two
            put(pos, a0 + 1, a0 + 1, OWN, a0 + 1)
            pos = pos + two
        return pos

    inputs[5].wait()
    pos = lax.fori_loop(0, CELLS // UNROLL, self_items, FRONT)
    pos = lax.fori_loop(0, PAIRS // UNROLL, pair_items, pos)
    lax.fori_loop(pos, pos + (SLOTS + 2) * U, dummy, 0)
    items[2 * LIST] = pos
    listed = pltpu.make_async_copy(items, items_hbm, in_sem.at[0])
    listed.start()

    def save(slot, batch):
        return batch_copies(gbuf, gs, sem, slot, batch * U, U, True)

    for slot in range(SLOTS):
        for copy in save(slot, LIST // U - SLOTS + slot):
            copy.start()

    def step(i, carry):
        slot = lax.rem(i, SLOTS)
        for copy in save(slot, i):
            copy.wait()
        for u in range(U):
            s = items[i * U + u]
            d = items[LIST + i * U + u]
            a, ra = s & 1023, d & 1023
            mq = massr[pl.ds(s >> 10, 1), :]
            down = jnp.zeros((8, HB), f32)
            for c in range(0, HB, 32):
                r2 = jnp.maximum(dist[u, c : c + 32, :HB], 1e-12)
                h2 = dist[u, c : c + 32, HB:]
                r = r2 * lax.rsqrt(r2)
                q = 1.0 / h2
                q2 = q * q
                y = jnp.maximum(q - r * q2, 0.0)
                y2 = y * y
                gs[slot, u, c : c + 32, :] = (y2 * y) * q2
                w = (y2 * y2) * (h2 + 4.0 * r)
                accr[ra, c : c + 32, :] += w * mq
                wm = w * massc[a, c : c + 32, :]
                down = down + ((wm[:8] + wm[8:16]) + (wm[16:24] + wm[24:]))
            l0 = pl.multiple_of((d >> 10) * 8, 8)
            accl[pl.ds(l0, 8), :] += down
        for copy in save(slot, i):
            copy.start()
        for u in range(U):
            s = items[(i + 1) * U + u]
            dist[u] = nn(rowf[s & 1023], lanef[s >> 10])
        return carry

    batches = (pos - FRONT + U - 1) // U
    lax.fori_loop(0, batches + 1, step, 0)

    row16 = lax.broadcasted_iota(i32, (16, HB), 0)
    for half in range(2):

        def own_sums(c8, carry):
            first = (2 * c8 * 8 + half) * 8
            total = jnp.zeros((16, 2 * HB), f32)
            for j in range(8):
                hi, lo = split(accr[2 * (c8 * 8 + j) + half])
                pick = (row16 == j).astype(bf16)
                total = total + nt(pick, jnp.concatenate([hi, lo], axis=0))
            rows8 = total[:8, :HB] + total[:8, HB:]
            for k in range(8):
                rows8 = rows8 + accl[pl.ds(first + k, 8, stride=16), :]
            to = pl.multiple_of(half * CELLS + c8 * 8, 8)
            dens[pl.ds(to, 8), :] = rows8 * DENSITY_SCALE
            return carry

        for c8 in range(CELLS // 8):
            own_sums(c8, 0)

        def near_sums(c8, carry):
            for g in range(1, 5):
                first = (2 * (g * CELLS + c8 * 8) + half) * 8
                rows8 = accl[pl.ds(first, 8, stride=16), :]
                for k in range(1, 8):
                    rows8 = rows8 + accl[pl.ds(first + k, 8, stride=16), :]
                to = pl.multiple_of(g * PLANE + half * CELLS + c8 * 8, 8)
                dens[pl.ds(to, 8), :] = rows8 * DENSITY_SCALE
            return carry

        for c8 in range(CELLS // 8):
            near_sums(c8, 0)

    out = pltpu.make_async_copy(dens, dens_hbm, in_sem.at[1])
    out.start()
    listed.wait()
    for slot in range(SLOTS):
        for copy in save(slot, 0):
            copy.wait()
    out.wait()


def force_kernel(
    items_hbm, counts_hbm, near_counts_hbm, side_hbm, remote_hbm, planes_hbm, coef_hbm, gbuf,
    acc_hbm, rho_hbm,
    items, counts, near_counts, side, remote, planes, coef, acc, rho,
    vmat, accr, accl, gs, sem, in_sem,
):
    sources = (items_hbm, counts_hbm, near_counts_hbm, side_hbm, remote_hbm, planes_hbm, coef_hbm)
    targets = (items, counts, near_counts, side, remote, planes, coef)
    inputs = [pltpu.make_async_copy(x, y, in_sem.at[k]) for k, (x, y) in enumerate(zip(sources, targets))]
    for copy in inputs:
        copy.start()

    def load(slot, batch):
        return batch_copies(gbuf, gs, sem, slot, FRONT + batch * UF, UF, False)

    for copy in inputs:
        copy.wait()
    batches = (items[2 * LIST] - FRONT + UF - 1) // UF
    for slot in range(SLOTS - 1):
        for copy in load(slot, slot):
            copy.start()

    for half in range(2):
        at_r = 5 * PLANE + half * CELLS
        rho[:, half * HB : (half + 1) * HB] = coef[at_r : at_r + CELLS, :]
    settled = pltpu.make_async_copy(rho, rho_hbm, in_sem.at[1])
    settled.start()

    accr[...] = jnp.zeros_like(accr)
    accl[...] = jnp.zeros_like(accl)

    def build(group, c, count, block):
        for half in range(2):
            tile = cell_tile(planes, group * 5 * PLANE, c, half)
            cc = coef[pl.ds(group * PLANE + half * CELLS + c, 1), :]
            m = masked(tile[3:4, :], count, half)
            mc = m * cc
            x = tile[0:3, :] - 0.5
            stack = jnp.concatenate([m, mc, m * x, mc * x], axis=0)
            vmat[block + half] = two_pieces(stack)

    def own_cells(step, carry):
        for j in range(UNROLL):
            c = step * UNROLL + j
            build(0, c, counts[0, c], 2 * c)
        return carry

    lax.fori_loop(0, CELLS // UNROLL, own_cells, 0)

    def near_cells(step, carry):
        for j in range(UNROLL):
            k = step * UNROLL + j
            build(side[k] + 1, remote[k], near_counts[side[k], 0, remote[k]], OWN + 2 * k)
        return carry

    lax.fori_loop(0, PAIRS // UNROLL, near_cells, 0)

    def step(i, carry):
        slot = lax.rem(i, SLOTS)

        @pl.when(i + SLOTS - 1 < batches)
        def _():
            for copy in load(lax.rem(i + SLOTS - 1, SLOTS), i + SLOTS - 1):
                copy.start()

        for copy in load(slot, i):
            copy.wait()
        for u in range(UF):
            s = items[FRONT + i * UF + u]
            d = items[LIST + FRONT + i * UF + u]
            hi, lo = split(gs[slot, u])
            to_row, to_lane = partner_sums(vmat[s & 1023], vmat[s >> 10], hi, lo)
            r0 = pl.multiple_of((d & 1023) * 8, 8)
            l0 = pl.multiple_of((d >> 10) * 8, 8)
            accr[pl.ds(r0, 8), :] += to_row
            accl[pl.ds(l0, 8), :] += to_lane
        return carry

    lax.fori_loop(0, batches, step, 0)

    for half in range(2):

        def sums(c8, carry):
            for g in range(5):
                first = (2 * (g * CELLS + c8 * 8) + half) * 8

                def total(k):
                    t = accl[pl.ds(first + k, 8, stride=16), :]
                    if g == 0:
                        t = t + accr[pl.ds(first + k, 8, stride=16), :]
                    return t

                cc = coef[pl.ds(pl.multiple_of(g * PLANE + half * CELLS + c8 * 8, 8), 8), :]
                plain = cc * total(0) + total(1)
                for k in range(3):
                    at_x = pl.multiple_of(((g * 2 + half) * 5 + k) * CELLS + c8 * 8, 8)
                    x = planes[pl.ds(at_x, 8), :] - 0.5
                    moment = cc * total(2 + k) + total(5 + k)
                    at_o = pl.multiple_of((g * 3 + k) * CELLS + c8 * 8, 8)
                    acc[pl.ds(at_o, 8), half * HB : (half + 1) * HB] = jnp.where(
                        cc > 0, (x * plain - moment) * FORCE_SCALE, 0.0
                    )
            return carry

        lax.fori_loop(0, CELLS // 8, sums, 0)

    out = pltpu.make_async_copy(acc, acc_hbm, in_sem.at[0])
    out.start()
    out.wait()
    settled.wait()


def planes_of(n):
    return jax.ShapeDtypeStruct((n * PLANE, HB), f32)


def call_density(counts, near_counts, local, side, remote, planes):
    return pl.pallas_call(
        density_kernel,
        out_shape=[
            planes_of(6),
            jax.ShapeDtypeStruct((LIST, HB, HB), f32),
            jax.ShapeDtypeStruct((2 * LIST + 8,), i32),
        ],
        in_specs=[HBM] * 6,
        out_specs=[HBM] * 3,
        scratch_shapes=[
            pltpu.SMEM((1, CELLS), i32),
            pltpu.SMEM((4, 1, CELLS), i32),
            pltpu.SMEM((PAIRS,), i32),
            pltpu.SMEM((PAIRS,), i32),
            pltpu.SMEM((PAIRS,), i32),
            pltpu.SMEM((2 * LIST + 8,), i32),
            pltpu.VMEM((PLANES, HB), f32),
            pltpu.VMEM((6 * PLANE, HB), f32),
            pltpu.VMEM((OWN, HB, FEAT), bf16),
            pltpu.VMEM((READ, FEAT, 2 * HB), bf16),
            pltpu.VMEM((OWN, HB, HB), f32),
            pltpu.VMEM((READ, HB), f32),
            pltpu.VMEM((OWN + 1, HB, HB), f32),
            pltpu.VMEM(((ALL + 1) * 8, HB), f32),
            pltpu.VMEM((U, HB, 2 * HB), f32),
            pltpu.VMEM((SLOTS, U, HB, HB), f32),
            pltpu.SemaphoreType.DMA((SLOTS, PARTS)),
            pltpu.SemaphoreType.DMA((6,)),
        ],
        compiler_params=pltpu.CompilerParams(vmem_limit_bytes=60 << 20),
        name="density",
    )(counts, near_counts, local, side, remote, planes)


def call_force(items, counts, near_counts, side, remote, planes, coef, gbuf):
    return pl.pallas_call(
        force_kernel,
        out_shape=[jax.ShapeDtypeStruct((15 * CELLS, 2 * HB), f32), jax.ShapeDtypeStruct((CELLS, 2 * HB), f32)],
        in_specs=[HBM] * 8,
        out_specs=[HBM] * 2,
        scratch_shapes=[
            pltpu.SMEM((2 * LIST + 8,), i32),
            pltpu.SMEM((1, CELLS), i32),
            pltpu.SMEM((4, 1, CELLS), i32),
            pltpu.SMEM((PAIRS,), i32),
            pltpu.SMEM((PAIRS,), i32),
            pltpu.VMEM((PLANES, HB), f32),
            pltpu.VMEM((6 * PLANE, HB), f32),
            pltpu.VMEM((15 * CELLS, 2 * HB), f32),
            pltpu.VMEM((CELLS, 2 * HB), f32),
            pltpu.VMEM((READ, 16, HB), bf16),
            pltpu.VMEM(((OWN + 1) * 8, HB), f32),
            pltpu.VMEM(((ALL + 1) * 8, HB), f32),
            pltpu.VMEM((SLOTS, UF, HB, HB), f32),
            pltpu.SemaphoreType.DMA((SLOTS, PARTS)),
            pltpu.SemaphoreType.DMA((7,)),
        ],
        compiler_params=pltpu.CompilerParams(vmem_limit_bytes=60 << 20),
        name="force",
    )(items, counts, near_counts, side, remote, planes, coef, gbuf)


def neighbours():
    i, j = lax.axis_index("gx"), lax.axis_index("yz")
    nx, ny = lax.axis_size("gx"), lax.axis_size("yz")
    return (
        (lax.rem(i + nx - 1, nx), j),
        (lax.rem(i + 1, nx), j),
        (i, lax.rem(j + ny - 1, ny)),
        (i, lax.rem(j + 1, ny)),
    )


def greet(devices):
    barrier = pltpu.get_barrier_semaphore()
    for device in devices:
        pl.semaphore_signal(barrier, inc=1, device_id=device, device_id_type=MESH)
    pl.semaphore_wait(barrier, 4)


def exchange(devices, source, target, send, recv):
    copies = []
    for s in (2, 3, 0, 1):
        copy = pltpu.make_async_remote_copy(
            src_ref=source(s),
            dst_ref=target(s ^ 1),
            send_sem=send.at[s],
            recv_sem=recv.at[s ^ 1],
            device_id=devices[s],
            device_id_type=MESH,
        )
        copy.start()
        copies.append(copy)
    return copies


def rows(ref, s, n):
    return ref.at[pl.ds(s * n, n), :]


def halo_kernel(
    positions, masses, smoothing, count,
    planes, near_count,
    pos, mass, smooth, own, in_sem, send, recv,
):
    devices = neighbours()
    sources, targets = (positions, masses, smoothing), (pos, mass, smooth)
    inputs = [pltpu.make_async_copy(x, y, in_sem.at[k]) for k, (x, y) in enumerate(zip(sources, targets))]
    for copy in inputs:
        copy.start()
    greet(devices)
    copies = exchange(devices, lambda s: count, lambda s: near_count.at[s], send.at[1], recv.at[1])
    for copy in inputs:
        copy.wait()
    for half in range(2):
        lanes = slice(half * HB, (half + 1) * HB)
        base = half * 5 * CELLS
        for k in range(3):
            own[base + k * CELLS : base + (k + 1) * CELLS, :] = pos[k, :, lanes]
        own[base + 3 * CELLS : base + 4 * CELLS, :] = mass[:, lanes]
        own[base + 4 * CELLS : base + 5 * CELLS, :] = smooth[:, lanes]
    copies += exchange(
        devices, lambda s: own, lambda s: rows(planes, s + 1, 5 * PLANE), send.at[0], recv.at[0]
    )
    keep = pltpu.make_async_copy(own, rows(planes, 0, 5 * PLANE), in_sem.at[3])
    keep.start()
    for copy in copies:
        copy.wait()
    keep.wait()


def settle_kernel(dens, coef, mine, occ, cf, rho_out, back, in_sem, send, recv):
    devices = neighbours()
    inputs = [
        pltpu.make_async_copy(rows(dens, 0, PLANE), mine, in_sem.at[0]),
        pltpu.make_async_copy(rows(dens, 5, PLANE), occ, in_sem.at[1]),
    ]
    for copy in inputs:
        copy.start()
    greet(devices)
    copies = exchange(
        devices, lambda s: rows(dens, s + 1, PLANE), lambda s: rows(back, s, PLANE), send.at[0], recv.at[0]
    )
    for copy in inputs + copies:
        copy.wait()
    rho = mine[...]
    for s in range(4):
        rho = rho + back[s * PLANE : (s + 1) * PLANE, :]
    mask = occ[...]
    cf[...] = jnp.exp(jnp.log(jnp.where(mask > 0, rho, 1.0)) * (-1.0 / 3.0)) * mask
    copies = exchange(devices, lambda s: cf, lambda s: rows(coef, s + 1, PLANE), send.at[1], recv.at[1])
    rho_out[...] = rho * mask
    keep = [
        pltpu.make_async_copy(cf, rows(coef, 0, PLANE), in_sem.at[0]),
        pltpu.make_async_copy(rho_out, rows(coef, 5, PLANE), in_sem.at[1]),
    ]
    for copy in keep:
        copy.start()
    for copy in copies + keep:
        copy.wait()


def finish_kernel(acc, back, in_sem, send, recv):
    devices = neighbours()
    greet(devices)
    size = 3 * CELLS
    copies = exchange(
        devices, lambda s: rows(acc, s + 1, size), lambda s: rows(back, s, size), send.at[0], recv.at[0]
    )
    for copy in copies:
        copy.wait()


def remote_call(kernel, name, ident, operands, out_shape, out_specs, scratch, copies, phases):
    return pl.pallas_call(
        kernel,
        out_shape=out_shape,
        in_specs=[HBM] * len(operands),
        out_specs=out_specs,
        scratch_shapes=[pltpu.VMEM(shape, f32) for shape in scratch]
        + [pltpu.SemaphoreType.DMA((copies,))]
        + [pltpu.SemaphoreType.DMA((phases, 4))] * 2,
        compiler_params=pltpu.CompilerParams(collective_id=ident, has_side_effects=True, vmem_limit_bytes=60 << 20),
        name=name,
    )(*operands)


def body(positions, masses, smoothing, counts, pair_local, pair_side, pair_remote):
    count = counts.reshape(1, CELLS)
    local, side, remote = (x.reshape(PAIRS) for x in (pair_local, pair_side, pair_remote))
    slots = 2 * HB
    planes, near_count = remote_call(
        halo_kernel, "halo", 0, (positions[0, 0].transpose(1, 0, 2), masses[0, 0], smoothing[0, 0], count),
        [planes_of(25), jax.ShapeDtypeStruct((4, 1, CELLS), i32)], [HBM] * 2,
        [(3, CELLS, slots), (CELLS, slots), (CELLS, slots), (5 * PLANE, HB)], 4, 2,
    )
    dens, gbuf, items = call_density(count, near_count, local, side, remote, planes)
    coef = remote_call(
        settle_kernel, "settle", 1, (dens,), planes_of(6), HBM,
        [(PLANE, HB)] * 4 + [(4 * PLANE, HB)], 2, 2,
    )
    acc, rho = call_force(items, count, near_count, side, remote, planes, coef, gbuf)
    back = remote_call(
        finish_kernel, "finish", 2, (acc,), jax.ShapeDtypeStruct((12 * CELLS, slots), f32), HBM, [], 1, 1
    )
    total = acc[: 3 * CELLS]
    for s in range(4):
        total = total + back[3 * s * CELLS : 3 * (s + 1) * CELLS]
    return rho[None, None], total.reshape(3, CELLS, slots).transpose(1, 0, 2)[None, None]


def solution(mesh):
    in_specs = (
        P("gx", "yz", None, None, None),
        P("gx", "yz", None, None),
        P("gx", "yz", None, None),
        P("gx", "yz", None),
        P("gx", "yz", None),
        P("gx", "yz", None),
        P("gx", "yz", None),
    )
    out_specs = (P("gx", "yz", None, None), P("gx", "yz", None, None, None))
    return jax.shard_map(body, mesh=mesh, in_specs=in_specs, out_specs=out_specs, check_vma=False)
```

```python
import math

import jax
import jax.numpy as jnp
from jax import lax
from jax.experimental import pallas as pl
from jax.experimental.pallas import tpu as pltpu
from jax.sharding import PartitionSpec as P

f32, bf16, i32 = jnp.float32, jnp.bfloat16, jnp.int32
HB = 128
CELLS = 64
PAIRS = 128
OWN = 2 * CELLS
ALL = 10 * CELLS
READ = 2 * (CELLS + PAIRS)
FEAT = 48
U = 16
PARTS = 2
SLOTS = 3
UNROLL = 8
PLANE = 2 * CELLS
PLANES = 25 * PLANE
UF = 4 * U
FRONT = U
ITEMS = 4 * PAIRS + 3 * CELLS
LIST = FRONT + ITEMS + (SLOTS + 3) * U
DENSITY_SCALE = 21.0 * 8.0 / (16.0 * math.pi)
FORCE_SCALE = 105.0 * 32.0 / (16.0 * math.pi)
SMEM = pl.BlockSpec(memory_space=pltpu.SMEM)
VMEM = pl.BlockSpec(memory_space=pltpu.VMEM)
HBM = pl.BlockSpec(memory_space=pl.ANY)
MESH = pl.DeviceIdType.MESH


def nn(a, b):
    return lax.dot_general(a, b, (((1,), (0,)), ((), ())), preferred_element_type=f32)


def nt(a, b):
    return lax.dot_general(a, b, (((1,), (1,)), ((), ())), preferred_element_type=f32)


def pieces(t):
    one = t.astype(bf16).astype(f32)
    rest = t - one
    two = rest.astype(bf16).astype(f32)
    return one, two, rest - two


def cell_tile(planes, base, cell, half):
    return planes[pl.ds(base + half * 5 * CELLS + cell, 5, stride=CELLS), :]


def masked(mass, count, half):
    slot = lax.broadcasted_iota(i32, mass.shape, 1) + half * HB
    return jnp.where(slot < count, mass, 0.0)


def masked_tile(planes, base, cell, half, count):
    tile = cell_tile(planes, base, cell, half)
    mass = masked(tile[3:4, :], count, half)
    return jnp.concatenate([tile[0:3, :], mass, tile[4:5, :], jnp.zeros((3, HB), f32)], axis=0)


def row_masks():
    row = lax.broadcasted_iota(i32, (8, HB), 0)
    return row, [(row == k).astype(f32) for k in range(8)]


def lane_features(tile, row, at):
    x = jnp.where(row < 3, tile - 0.5, 0.0)
    norm = jnp.sum(x * x, axis=0, keepdims=True)
    h = tile[4:5, :]
    dist = x + at[3] + at[4] * norm
    supp = at[5] + at[6] * h
    d1, d2, d3 = pieces(dist)
    s1, s2, s3 = pieces(supp)
    d12 = jnp.concatenate([d1, d2], axis=0).astype(bf16)
    d31 = jnp.concatenate([d3, d1], axis=0).astype(bf16)
    s12 = jnp.concatenate([s1, s2], axis=0).astype(bf16)
    s31 = jnp.concatenate([s3, s1], axis=0).astype(bf16)
    left = jnp.concatenate([d12, d12, d31], axis=0)
    right = jnp.concatenate([s12, s12, s31], axis=0)
    return jnp.concatenate([left, right], axis=1)


def row_features(tile, row, at):
    x = jnp.where(row < 3, tile - 0.5, 0.0)
    norm = jnp.sum(x * x, axis=0, keepdims=True)
    h = tile[4:5, :]
    form = -2.0 * x + at[3] * norm + at[4] + at[5] * h + at[6]
    p1, p2, p3 = pieces(form)
    rest = jnp.zeros((HB - FEAT - 8, HB), f32)
    m1, m2, m3 = pieces(at[0] * tile[3:4, :])
    masses = m1 + pltpu.roll(m2, 1, 0) + pltpu.roll(m3, 2, 0)
    rest = jnp.zeros((64 - FEAT - 8, HB), f32)
    turned = jnp.concatenate([p1, p1, p2, p2, p1, p3, masses, rest], axis=0).T.astype(bf16)
    k = lax.broadcasted_iota(i32, (64, HB), 0)
    pick = ((k >= FEAT) & (k < FEAT + 3)).astype(f32).astype(bf16)
    return turned[:, :FEAT], nn(turned, pick)


def two_pieces(tile):
    one = tile.astype(bf16).astype(f32)
    return jnp.concatenate([one, tile - one], axis=0).astype(bf16)


def fold(o):
    o = o[:, :HB] + o[:, HB:]
    return o[:8] + o[8:]


def partner_sums(va, vb, hi, lo):
    to_lane = fold(nn(va, jnp.concatenate([hi, lo], axis=1)))
    to_row = fold(nn(vb, jnp.concatenate([hi.T, lo.T], axis=1)))
    return to_row, to_lane


def split(g):
    hi = g.astype(bf16)
    return hi, (g - hi.astype(f32)).astype(bf16)


def batch_copies(buffer, gs, sem, slot, first, size, out):
    part = size // PARTS
    copies = []
    for k in range(PARTS):
        here = gs.at[slot, pl.ds(k * part, part)]
        there = buffer.at[pl.ds(first + k * part, part)]
        pair = (here, there) if out else (there, here)
        copies.append(pltpu.make_async_copy(*pair, sem.at[slot, k]))
    return copies


def density_kernel(
    counts_hbm, near_counts_hbm, local_hbm, side_hbm, remote_hbm, planes_hbm,
    dens_hbm, gbuf, items_hbm,
    counts, near_counts, local, side, remote, items, planes, dens,
    rowf, lanef, massc, massr, accr, accl, dist, gs, sem, in_sem,
):
    sources = (counts_hbm, near_counts_hbm, local_hbm, side_hbm, remote_hbm, planes_hbm)
    targets = (counts, near_counts, local, side, remote, planes)
    inputs = [pltpu.make_async_copy(x, y, in_sem.at[k]) for k, (x, y) in enumerate(zip(sources, targets))]
    for copy in inputs:
        copy.start()
    for copy in inputs[:5]:
        copy.wait()
    row, at = row_masks()

    accr[...] = jnp.zeros_like(accr)
    accl[...] = jnp.zeros_like(accl)
    dist[...] = jnp.ones_like(dist)

    def build(tile, block):
        lanef[block] = lane_features(tile, row, at)
        massr[pl.ds(block, 1), :] = tile[3:4, :]

    def dummy(i, carry):
        items[i] = 0
        items[LIST + i] = OWN + ALL * 1024
        return carry

    lax.fori_loop(0, FRONT, dummy, 0)

    def put(pos, a, b, da, db):
        items[pos] = a + b * 1024
        items[LIST + pos] = da + db * 1024

    def pair_items(step, pos):
        for j in range(UNROLL):
            k = step * UNROLL + j
            for half in range(2):
                count = near_counts[side[k], 0, remote[k]]
                tile = masked_tile(planes, (side[k] + 1) * 5 * PLANE, remote[k], half, count)
                build(tile, OWN + 2 * k + half)
            a = local[k]
            two_a = (counts[0, a] > HB).astype(i32)
            two_b = (near_counts[side[k], 0, remote[k]] > HB).astype(i32)
            a0, b0 = 2 * a, OWN + 2 * k
            d0 = 2 * (side[k] * CELLS + remote[k] + CELLS)
            put(pos, a0, b0, a0, d0)
            pos = pos + 1
            put(pos, a0, b0 + 1, a0, d0 + 1)
            pos = pos + two_b
            put(pos, a0 + 1, b0, a0 + 1, d0)
            pos = pos + two_a
            put(pos, a0 + 1, b0 + 1, a0 + 1, d0 + 1)
            pos = pos + two_a * two_b
        return pos

    def self_items(step, pos):
        for j in range(UNROLL):
            a = step * UNROLL + j
            for half in range(2):
                tile = masked_tile(planes, 0, a, half, counts[0, a])
                build(tile, 2 * a + half)
                rowf[2 * a + half], massc[2 * a + half] = row_features(tile, row, at)
                occ = masked(jnp.ones((1, HB), f32), counts[0, a], half)
                dens[pl.ds(5 * PLANE + half * CELLS + a, 1), :] = occ
            two = (counts[0, a] > HB).astype(i32)
            a0 = 2 * a
            put(pos, a0, a0, OWN, a0)
            pos = pos + 1
            put(pos, a0, a0 + 1, a0, a0 + 1)
            pos = pos + two
            put(pos, a0 + 1, a0 + 1, OWN, a0 + 1)
            pos = pos + two
        return pos

    inputs[5].wait()
    pos = lax.fori_loop(0, CELLS // UNROLL, self_items, FRONT)
    pos = lax.fori_loop(0, PAIRS // UNROLL, pair_items, pos)
    lax.fori_loop(pos, pos + (SLOTS + 2) * U, dummy, 0)
    items[2 * LIST] = pos
    listed = pltpu.make_async_copy(items, items_hbm, in_sem.at[0])
    listed.start()

    def save(slot, batch):
        return batch_copies(gbuf, gs, sem, slot, batch * U, U, True)

    for slot in range(SLOTS):
        for copy in save(slot, LIST // U - SLOTS + slot):
            copy.start()

    def step(i, carry):
        slot = lax.rem(i, SLOTS)
        for copy in save(slot, i):
            copy.wait()
        for u in range(U):
            s = items[i * U + u]
            d = items[LIST + i * U + u]
            a, ra = s & 1023, d & 1023
            mq = massr[pl.ds(s >> 10, 1), :]
            down = jnp.zeros((8, HB), f32)
            for c in range(0, HB, 32):
                r2 = jnp.maximum(dist[u, c : c + 32, :HB], 1e-12)
                h2 = dist[u, c : c + 32, HB:]
                r = r2 * lax.rsqrt(r2)
                q = 1.0 / h2
                q2 = q * q
                y = jnp.maximum(q - r * q2, 0.0)
                y2 = y * y
                gs[slot, u, c : c + 32, :] = (y2 * y) * q2
                w = (y2 * y2) * (h2 + 4.0 * r)
                accr[ra, c : c + 32, :] += w * mq
                wm = w * massc[a, c : c + 32, :]
                down = down + ((wm[:8] + wm[8:16]) + (wm[16:24] + wm[24:]))
            l0 = pl.multiple_of((d >> 10) * 8, 8)
            accl[pl.ds(l0, 8), :] += down
        for copy in save(slot, i):
            copy.start()
        for u in range(U):
            s = items[(i + 1) * U + u]
            dist[u] = nn(rowf[s & 1023], lanef[s >> 10])
        return carry

    batches = (pos - FRONT + U - 1) // U
    lax.fori_loop(0, batches + 1, step, 0)

    row16 = lax.broadcasted_iota(i32, (16, HB), 0)
    for half in range(2):

        def own_sums(c8, carry):
            first = (2 * c8 * 8 + half) * 8
            total = jnp.zeros((16, 2 * HB), f32)
            for j in range(8):
                hi, lo = split(accr[2 * (c8 * 8 + j) + half])
                pick = (row16 == j).astype(bf16)
                total = total + nt(pick, jnp.concatenate([hi, lo], axis=0))
            rows8 = total[:8, :HB] + total[:8, HB:]
            for k in range(8):
                rows8 = rows8 + accl[pl.ds(first + k, 8, stride=16), :]
            to = pl.multiple_of(half * CELLS + c8 * 8, 8)
            dens[pl.ds(to, 8), :] = rows8 * DENSITY_SCALE
            return carry

        for c8 in range(CELLS // 8):
            own_sums(c8, 0)

        def near_sums(c8, carry):
            for g in range(1, 5):
                first = (2 * (g * CELLS + c8 * 8) + half) * 8
                rows8 = accl[pl.ds(first, 8, stride=16), :]
                for k in range(1, 8):
                    rows8 = rows8 + accl[pl.ds(first + k, 8, stride=16), :]
                to = pl.multiple_of(g * PLANE + half * CELLS + c8 * 8, 8)
                dens[pl.ds(to, 8), :] = rows8 * DENSITY_SCALE
            return carry

        for c8 in range(CELLS // 8):
            near_sums(c8, 0)

    out = pltpu.make_async_copy(dens, dens_hbm, in_sem.at[1])
    out.start()
    listed.wait()
    for slot in range(SLOTS):
        for copy in save(slot, 0):
            copy.wait()
    out.wait()


def force_kernel(
    items_hbm, counts_hbm, near_counts_hbm, side_hbm, remote_hbm, planes_hbm, coef_hbm, gbuf,
    acc_hbm, rho_hbm,
    items, counts, near_counts, side, remote, planes, coef, acc, rho,
    vmat, accr, accl, gs, sem, in_sem,
):
    sources = (items_hbm, counts_hbm, near_counts_hbm, side_hbm, remote_hbm, planes_hbm, coef_hbm)
    targets = (items, counts, near_counts, side, remote, planes, coef)
    inputs = [pltpu.make_async_copy(x, y, in_sem.at[k]) for k, (x, y) in enumerate(zip(sources, targets))]
    for copy in inputs:
        copy.start()

    def load(slot, batch):
        return batch_copies(gbuf, gs, sem, slot, FRONT + batch * UF, UF, False)

    for copy in inputs:
        copy.wait()
    batches = (items[2 * LIST] - FRONT + UF - 1) // UF
    for slot in range(SLOTS - 1):
        for copy in load(slot, slot):
            copy.start()

    for half in range(2):
        at_r = 5 * PLANE + half * CELLS
        rho[:, half * HB : (half + 1) * HB] = coef[at_r : at_r + CELLS, :]
    settled = pltpu.make_async_copy(rho, rho_hbm, in_sem.at[1])
    settled.start()

    accr[...] = jnp.zeros_like(accr)
    accl[...] = jnp.zeros_like(accl)

    def build(group, c, count, block):
        for half in range(2):
            tile = cell_tile(planes, group * 5 * PLANE, c, half)
            cc = coef[pl.ds(group * PLANE + half * CELLS + c, 1), :]
            m = masked(tile[3:4, :], count, half)
            mc = m * cc
            x = tile[0:3, :] - 0.5
            stack = jnp.concatenate([m, mc, m * x, mc * x], axis=0)
            vmat[block + half] = two_pieces(stack)

    def own_cells(step, carry):
        for j in range(UNROLL):
            c = step * UNROLL + j
            build(0, c, counts[0, c], 2 * c)
        return carry

    lax.fori_loop(0, CELLS // UNROLL, own_cells, 0)

    def near_cells(step, carry):
        for j in range(UNROLL):
            k = step * UNROLL + j
            build(side[k] + 1, remote[k], near_counts[side[k], 0, remote[k]], OWN + 2 * k)
        return carry

    lax.fori_loop(0, PAIRS // UNROLL, near_cells, 0)

    def step(i, carry):
        slot = lax.rem(i, SLOTS)

        @pl.when(i + SLOTS - 1 < batches)
        def _():
            for copy in load(lax.rem(i + SLOTS - 1, SLOTS), i + SLOTS - 1):
                copy.start()

        for copy in load(slot, i):
            copy.wait()
        for u in range(UF):
            s = items[FRONT + i * UF + u]
            d = items[LIST + FRONT + i * UF + u]
            hi, lo = split(gs[slot, u])
            to_row, to_lane = partner_sums(vmat[s & 1023], vmat[s >> 10], hi, lo)
            r0 = pl.multiple_of((d & 1023) * 8, 8)
            l0 = pl.multiple_of((d >> 10) * 8, 8)
            accr[pl.ds(r0, 8), :] += to_row
            accl[pl.ds(l0, 8), :] += to_lane
        return carry

    lax.fori_loop(0, batches, step, 0)

    for half in range(2):

        def sums(c8, carry):
            for g in range(5):
                first = (2 * (g * CELLS + c8 * 8) + half) * 8

                def total(k):
                    t = accl[pl.ds(first + k, 8, stride=16), :]
                    if g == 0:
                        t = t + accr[pl.ds(first + k, 8, stride=16), :]
                    return t

                cc = coef[pl.ds(pl.multiple_of(g * PLANE + half * CELLS + c8 * 8, 8), 8), :]
                plain = cc * total(0) + total(1)
                for k in range(3):
                    at_x = pl.multiple_of(((g * 2 + half) * 5 + k) * CELLS + c8 * 8, 8)
                    x = planes[pl.ds(at_x, 8), :] - 0.5
                    moment = cc * total(2 + k) + total(5 + k)
                    at_o = pl.multiple_of((g * 3 + k) * CELLS + c8 * 8, 8)
                    acc[pl.ds(at_o, 8), half * HB : (half + 1) * HB] = jnp.where(
                        cc > 0, (x * plain - moment) * FORCE_SCALE, 0.0
                    )
            return carry

        lax.fori_loop(0, CELLS // 8, sums, 0)

    out = pltpu.make_async_copy(acc, acc_hbm, in_sem.at[0])
    out.start()
    out.wait()
    settled.wait()


def planes_of(n):
    return jax.ShapeDtypeStruct((n * PLANE, HB), f32)


def call_density(counts, near_counts, local, side, remote, planes):
    return pl.pallas_call(
        density_kernel,
        out_shape=[
            planes_of(6),
            jax.ShapeDtypeStruct((LIST, HB, HB), f32),
            jax.ShapeDtypeStruct((2 * LIST + 8,), i32),
        ],
        in_specs=[HBM] * 6,
        out_specs=[HBM] * 3,
        scratch_shapes=[
            pltpu.SMEM((1, CELLS), i32),
            pltpu.SMEM((4, 1, CELLS), i32),
            pltpu.SMEM((PAIRS,), i32),
            pltpu.SMEM((PAIRS,), i32),
            pltpu.SMEM((PAIRS,), i32),
            pltpu.SMEM((2 * LIST + 8,), i32),
            pltpu.VMEM((PLANES, HB), f32),
            pltpu.VMEM((6 * PLANE, HB), f32),
            pltpu.VMEM((OWN, HB, FEAT), bf16),
            pltpu.VMEM((READ, FEAT, 2 * HB), bf16),
            pltpu.VMEM((OWN, HB, HB), f32),
            pltpu.VMEM((READ, HB), f32),
            pltpu.VMEM((OWN + 1, HB, HB), f32),
            pltpu.VMEM(((ALL + 1) * 8, HB), f32),
            pltpu.VMEM((U, HB, 2 * HB), f32),
            pltpu.VMEM((SLOTS, U, HB, HB), f32),
            pltpu.SemaphoreType.DMA((SLOTS, PARTS)),
            pltpu.SemaphoreType.DMA((6,)),
        ],
        compiler_params=pltpu.CompilerParams(vmem_limit_bytes=60 << 20),
        name="density",
    )(counts, near_counts, local, side, remote, planes)


def call_force(items, counts, near_counts, side, remote, planes, coef, gbuf):
    return pl.pallas_call(
        force_kernel,
        out_shape=[jax.ShapeDtypeStruct((15 * CELLS, 2 * HB), f32), jax.ShapeDtypeStruct((CELLS, 2 * HB), f32)],
        in_specs=[HBM] * 8,
        out_specs=[HBM] * 2,
        scratch_shapes=[
            pltpu.SMEM((2 * LIST + 8,), i32),
            pltpu.SMEM((1, CELLS), i32),
            pltpu.SMEM((4, 1, CELLS), i32),
            pltpu.SMEM((PAIRS,), i32),
            pltpu.SMEM((PAIRS,), i32),
            pltpu.VMEM((PLANES, HB), f32),
            pltpu.VMEM((6 * PLANE, HB), f32),
            pltpu.VMEM((15 * CELLS, 2 * HB), f32),
            pltpu.VMEM((CELLS, 2 * HB), f32),
            pltpu.VMEM((READ, 16, HB), bf16),
            pltpu.VMEM(((OWN + 1) * 8, HB), f32),
            pltpu.VMEM(((ALL + 1) * 8, HB), f32),
            pltpu.VMEM((SLOTS, UF, HB, HB), f32),
            pltpu.SemaphoreType.DMA((SLOTS, PARTS)),
            pltpu.SemaphoreType.DMA((7,)),
        ],
        compiler_params=pltpu.CompilerParams(vmem_limit_bytes=60 << 20),
        name="force",
    )(items, counts, near_counts, side, remote, planes, coef, gbuf)


def neighbours():
    i, j = lax.axis_index("gx"), lax.axis_index("yz")
    nx, ny = lax.axis_size("gx"), lax.axis_size("yz")
    return (
        (lax.rem(i + nx - 1, nx), j),
        (lax.rem(i + 1, nx), j),
        (i, lax.rem(j + ny - 1, ny)),
        (i, lax.rem(j + 1, ny)),
    )


def greet(devices):
    barrier = pltpu.get_barrier_semaphore()
    for device in devices:
        pl.semaphore_signal(barrier, inc=1, device_id=device, device_id_type=MESH)
    pl.semaphore_wait(barrier, 4)


def exchange(devices, source, target, send, recv):
    copies = []
    for s in (2, 3, 0, 1):
        copy = pltpu.make_async_remote_copy(
            src_ref=source(s),
            dst_ref=target(s ^ 1),
            send_sem=send.at[s],
            recv_sem=recv.at[s ^ 1],
            device_id=devices[s],
            device_id_type=MESH,
        )
        copy.start()
        copies.append(copy)
    return copies


def rows(ref, s, n):
    return ref.at[pl.ds(s * n, n), :]


def halo_kernel(
    positions, masses, smoothing, count,
    planes, near_count,
    pos, mass, smooth, own, in_sem, send, recv,
):
    devices = neighbours()
    sources, targets = (positions, masses, smoothing), (pos, mass, smooth)
    inputs = [pltpu.make_async_copy(x, y, in_sem.at[k]) for k, (x, y) in enumerate(zip(sources, targets))]
    for copy in inputs:
        copy.start()
    greet(devices)
    copies = exchange(devices, lambda s: count, lambda s: near_count.at[s], send.at[1], recv.at[1])
    for copy in inputs:
        copy.wait()
    for half in range(2):
        lanes = slice(half * HB, (half + 1) * HB)
        base = half * 5 * CELLS
        for k in range(3):
            own[base + k * CELLS : base + (k + 1) * CELLS, :] = pos[k, :, lanes]
        own[base + 3 * CELLS : base + 4 * CELLS, :] = mass[:, lanes]
        own[base + 4 * CELLS : base + 5 * CELLS, :] = smooth[:, lanes]
    copies += exchange(
        devices, lambda s: own, lambda s: rows(planes, s + 1, 5 * PLANE), send.at[0], recv.at[0]
    )
    keep = pltpu.make_async_copy(own, rows(planes, 0, 5 * PLANE), in_sem.at[3])
    keep.start()
    for copy in copies:
        copy.wait()
    keep.wait()


def settle_kernel(dens, coef, mine, occ, cf, rho_out, back, in_sem, send, recv):
    devices = neighbours()
    inputs = [
        pltpu.make_async_copy(rows(dens, 0, PLANE), mine, in_sem.at[0]),
        pltpu.make_async_copy(rows(dens, 5, PLANE), occ, in_sem.at[1]),
    ]
    for copy in inputs:
        copy.start()
    greet(devices)
    copies = exchange(
        devices, lambda s: rows(dens, s + 1, PLANE), lambda s: rows(back, s, PLANE), send.at[0], recv.at[0]
    )
    for copy in inputs + copies:
        copy.wait()
    rho = mine[...]
    for s in range(4):
        rho = rho + back[s * PLANE : (s + 1) * PLANE, :]
    mask = occ[...]
    cf[...] = jnp.exp(jnp.log(jnp.where(mask > 0, rho, 1.0)) * (-1.0 / 3.0)) * mask
    copies = exchange(devices, lambda s: cf, lambda s: rows(coef, s + 1, PLANE), send.at[1], recv.at[1])
    rho_out[...] = rho * mask
    keep = [
        pltpu.make_async_copy(cf, rows(coef, 0, PLANE), in_sem.at[0]),
        pltpu.make_async_copy(rho_out, rows(coef, 5, PLANE), in_sem.at[1]),
    ]
    for copy in keep:
        copy.start()
    for copy in copies + keep:
        copy.wait()


def finish_kernel(acc, back, in_sem, send, recv):
    devices = neighbours()
    greet(devices)
    size = 3 * CELLS
    copies = exchange(
        devices, lambda s: rows(acc, s + 1, size), lambda s: rows(back, s, size), send.at[0], recv.at[0]
    )
    for copy in copies:
        copy.wait()


def remote_call(kernel, name, ident, operands, out_shape, out_specs, scratch, copies, phases):
    return pl.pallas_call(
        kernel,
        out_shape=out_shape,
        in_specs=[HBM] * len(operands),
        out_specs=out_specs,
        scratch_shapes=[pltpu.VMEM(shape, f32) for shape in scratch]
        + [pltpu.SemaphoreType.DMA((copies,))]
        + [pltpu.SemaphoreType.DMA((phases, 4))] * 2,
        compiler_params=pltpu.CompilerParams(collective_id=ident, has_side_effects=True, vmem_limit_bytes=60 << 20),
        name=name,
    )(*operands)


def body(positions, masses, smoothing, counts, pair_local, pair_side, pair_remote):
    count = counts.reshape(1, CELLS)
    local, side, remote = (x.reshape(PAIRS) for x in (pair_local, pair_side, pair_remote))
    slots = 2 * HB
    planes, near_count = remote_call(
        halo_kernel, "halo", 0, (positions[0, 0].transpose(1, 0, 2), masses[0, 0], smoothing[0, 0], count),
        [planes_of(25), jax.ShapeDtypeStruct((4, 1, CELLS), i32)], [HBM] * 2,
        [(3, CELLS, slots), (CELLS, slots), (CELLS, slots), (5 * PLANE, HB)], 4, 2,
    )
    dens, gbuf, items = call_density(count, near_count, local, side, remote, planes)
    coef = remote_call(
        settle_kernel, "settle", 1, (dens,), planes_of(6), HBM,
        [(PLANE, HB)] * 4 + [(4 * PLANE, HB)], 2, 2,
    )
    acc, rho = call_force(items, count, near_count, side, remote, planes, coef, gbuf)
    back = remote_call(
        finish_kernel, "finish", 2, (acc,), jax.ShapeDtypeStruct((12 * CELLS, slots), f32), HBM, [], 1, 1
    )
    total = acc[: 3 * CELLS]
    for s in range(4):
        total = total + back[3 * s * CELLS : 3 * (s + 1) * CELLS]
    return rho[None, None], total.reshape(3, CELLS, slots).transpose(1, 0, 2)[None, None]


def solution(mesh):
    in_specs = (
        P("gx", "yz", None, None, None),
        P("gx", "yz", None, None),
        P("gx", "yz", None, None),
        P("gx", "yz", None),
        P("gx", "yz", None),
        P("gx", "yz", None),
        P("gx", "yz", None),
    )
    out_specs = (P("gx", "yz", None, None), P("gx", "yz", None, None, None))
    return jax.shard_map(body, mesh=mesh, in_specs=in_specs, out_specs=out_specs, check_vma=False)
```
